128 devices in a mesh: dp: 16 (over z, x_lo, core), tensor: 8 (over y, x_hi).
Axes of the slice: x: 4 (x_hi: 2, x_lo: 2; x = x_hi * 2 + x_lo), y: 4, z: 4, core: 2. Of those that a mesh axis runs over, the one named last changes fastest.
Arguments:
- tokens: bfloat16 [20480, 2048], P(('dp', 'tensor')), may hold values from -6 to 6
- lengths: int32 [16, 3], P('dp'), may hold values from 1 to 1024, 1280 in all within a row
- order: int32 [16, 1280], P('dp'), may hold values from 0 to 1279, each once within a row
- sequence_adapter: int32 [16, 3], P('dp'), may hold values from 0 to 7
- first_norm_gain: float32 [1, 2048], replicated, may hold values from 0.5 to 1.5
- first_norm_bias: float32 [1, 2048], replicated, may hold values from -4 to 4
- second_norm_gain: float32 [1, 2048], replicated, may hold values from 0.5 to 1.5
- second_norm_bias: float32 [1, 2048], replicated, may hold values from -4 to 4
- joined_matrix: bfloat16 [1, 2048, 6144], P(None, 'dp', 'tensor'), may hold values from -0.125 to 0.125
- joined_offset_bias: float32 [1, 6144], P(None, 'tensor'), may hold values from -4 to 4
- output_matrix: bfloat16 [1, 2048, 2048], P(None, 'tensor', 'dp'), may hold values from -0.25 to 0.25
- output_offset_bias: float32 [1, 2048], replicated, may hold values from -4 to 4
- up_matrix: bfloat16 [1, 2048, 8192], P(None, 'dp', 'tensor'), may hold values from -0.125 to 0.125
- up_offset_bias: float32 [1, 8192], P(None, 'tensor'), may hold values from -4 to 4
- down_matrix: bfloat16 [1, 8192, 2048], P(None, 'tensor', 'dp'), may hold values from -0.09375 to 0.09375
- down_offset_bias: float32 [1, 2048], replicated, may hold values from -4 to 4
- joined_adapter_reduce: bfloat16 [1, 2048, 128], replicated, may hold values from -0.125 to 0.125
- joined_adapter_expand: bfloat16 [1, 128, 6144], P(None, None, 'tensor'), may hold values from -1.5 to 1.5
- output_adapter_reduce: bfloat16 [1, 2048, 128], P(None, 'tensor'), may hold values from -0.25 to 0.25
- output_adapter_expand: bfloat16 [1, 128, 2048], replicated, may hold values from -1.5 to 1.5
- up_adapter_reduce: bfloat16 [1, 2048, 128], replicated, may hold values from -0.125 to 0.125
- up_adapter_expand: bfloat16 [1, 128, 8192], P(None, None, 'tensor'), may hold values from -1.5 to 1.5
- down_adapter_reduce: bfloat16 [1, 8192, 128], P(None, 'tensor'), may hold values from -0.09375 to 0.09375
- down_adapter_expand: bfloat16 [1, 128, 2048], replicated, may hold values from -1.5 to 1.5
- cotangent: bfloat16 [20480, 2048], P(('dp', 'tensor')), may hold values from -6 to 6
Outputs:
- block_out: float32 [20480, 2048], P(('dp', 'tensor'))
- input_grad: float32 [20480, 2048], P(('dp', 'tensor'))
- qkv_lora_a_grad: float32 [1, 2048, 128], replicated
- qkv_lora_b_grad: float32 [1, 128, 6144], P(None, None, 'tensor')
- out_lora_a_grad: float32 [1, 2048, 128], P(None, 'tensor')
- out_lora_b_grad: float32 [1, 128, 2048], replicated
- up_lora_a_grad: float32 [1, 2048, 128], replicated
- up_lora_b_grad: float32 [1, 128, 8192], P(None, None, 'tensor')
- down_lora_a_grad: float32 [1, 8192, 128], P(None, 'tensor')
- down_lora_b_grad: float32 [1, 128, 2048], replicated
The draws below stay inside these ranges and needn't reach their ends.
Inputs may be any that keep to these rules, and one draw needn't show every extreme that they name: `order`: each row holds every number of 0 to 1279 once.
All inputs are finite; a program needn't handle non-finite values.
Results may differ from the reference program's by a relative error of at most 0.02.
Values may be sent and summed in bfloat16 or wider, within the bound.
A program may use at most 128 MiB of HBM per device.

```python
import math
import jax
import jax.numpy as jnp
import numpy as np
from jax import lax

MODEL_WIDTH = 2048
HEADS = 16
HEAD_SIZE = 128
FEEDFWD_UNITS = 8192
ADAPTERS = 8
ADAPTER_RANK = 16
LAYER_COUNT = 1
SEQS = 3
GROUP_TOK = 1280
MOST_LEN = 1024
ADAPTER_COLUMNS = 128
TOKENS = 20480
N_DP = 16
N_TENSOR = 8


def with_ends(values, rng, low, high):
    shape = values.shape
    place = [jax.random.randint(jax.random.fold_in(rng, axis), (), 0, shape[axis]) for axis in range(len(shape))]
    values = values.at[tuple(place)].set(low)
    longest = shape.index(max(shape))
    place[longest] = (place[longest] + 1) % shape[longest]
    return values.at[tuple(place)].set(high)


def block_levels(rng, shape, cuts, smallest, largest):
    loudness, own = 1.0, jax.random.fold_in(rng, 6)
    for dim, shards_of in cuts:
        draws = jnp.exp(jax.random.uniform(jax.random.fold_in(own, dim), (shards_of,), jnp.float32, smallest / len(cuts), largest / len(cuts)))
        loudness = loudness * jnp.repeat(draws, shape[dim] // shards_of).reshape([-1 if axis == dim else 1 for axis in range(len(shape))])
    return loudness


def length_profile(amount, total, reach, skew):
    portions = [(1 << 20) // math.isqrt(grade ** skew) + 1 for grade in range(2, amount + 1)]
    surplus, holding = total - reach - (amount - 1), [1] * (amount - 1)
    while surplus > 0:
        candidates = [i for i in range(amount - 1) if holding[i] < reach]
        whole, remaining = sum([portions[i] for i in candidates]), surplus
        for i in candidates:
            extra = min(reach - holding[i], max(1, remaining * portions[i] // whole), surplus)
            holding[i] = holding[i] + extra
            surplus = surplus - extra
    return np.array([reach] + holding)


def uneven(rng, number_of, total, reach, skew):
    if number_of == 2:
        one = jax.random.randint(rng, (), max(1, total - reach), min(reach, total - 1) + 1)
        return jnp.stack([one, total - one])
    sizes = jnp.asarray(length_profile(number_of, total, reach, skew), jnp.int32)
    couples = (number_of - 1) // 2
    source_of, taker = sizes[1:1 + 2 * couples:2], sizes[2:2 + 2 * couples:2]
    margin = jnp.minimum(source_of - 1, reach - taker)
    shifted = jax.random.randint(jax.random.fold_in(rng, 1), (couples,), 0, 1 << 20) % (margin + 1)
    sizes = sizes.at[1:1 + 2 * couples:2].set(source_of - shifted).at[2:2 + 2 * couples:2].set(taker + shifted)
    return sizes[jax.random.permutation(jax.random.fold_in(rng, 2), number_of)]


def noise(stream_key, dims, scale, bound, shards=(), kind=jnp.bfloat16):
    level = block_levels(stream_key, dims, shards, -0.22, 0.18) if shards else 1.0
    entries = jax.random.normal(stream_key, dims, jnp.float32) * scale * level
    return jnp.minimum(jnp.maximum(entries, -bound), bound).astype(kind)


def setup_inputs(seed: int = 0) -> dict:
    streams_of = jax.random.split(jax.random.key(seed), 26)
    return {
        "tokens": noise(streams_of[0], (TOKENS, MODEL_WIDTH), 1.0, 6.0, ((0, 128),)),
        "lengths": jax.vmap(lambda own: uneven(own, SEQS, GROUP_TOK, MOST_LEN, 2))(jax.random.split(streams_of[1], N_DP)).reshape((N_DP, SEQS)).astype(jnp.int32),
        "order": jax.vmap(lambda own: jax.random.permutation(own, GROUP_TOK))(jax.random.split(streams_of[2], N_DP)).reshape((N_DP, GROUP_TOK)).astype(jnp.int32),
        "sequence_adapter": with_ends(jax.random.randint(streams_of[3], (N_DP, SEQS), 0, ADAPTERS), jax.random.fold_in(streams_of[3], 1), 0, ADAPTERS - 1).astype(jnp.int32),
        "first_norm_gain": jnp.clip(1.0 + 0.1 * jax.random.normal(streams_of[4], (LAYER_COUNT, MODEL_WIDTH), jnp.float32), 0.5, 1.5),
        "first_norm_bias": noise(streams_of[5], (LAYER_COUNT, MODEL_WIDTH), 0.3, 4.0, (), jnp.float32),
        "second_norm_gain": jnp.clip(1.0 + 0.1 * jax.random.normal(streams_of[6], (LAYER_COUNT, MODEL_WIDTH), jnp.float32), 0.5, 1.5),
        "second_norm_bias": noise(streams_of[7], (LAYER_COUNT, MODEL_WIDTH), 0.3, 4.0, (), jnp.float32),
        "joined_matrix": noise(streams_of[8], (LAYER_COUNT, MODEL_WIDTH, 3 * MODEL_WIDTH), MODEL_WIDTH ** -0.5, 0.125, ((1, 16), (2, 8))),
        "joined_offset_bias": noise(streams_of[9], (LAYER_COUNT, 3 * MODEL_WIDTH), 0.3, 4.0, ((1, 8),), jnp.float32),
        "output_matrix": noise(streams_of[10], (LAYER_COUNT, MODEL_WIDTH, MODEL_WIDTH), (MODEL_WIDTH // 4) ** -0.5, 0.25, ((1, 8), (2, 16))),
        "output_offset_bias": noise(streams_of[11], (LAYER_COUNT, MODEL_WIDTH), 0.3, 4.0, (), jnp.float32),
        "up_matrix": noise(streams_of[12], (LAYER_COUNT, MODEL_WIDTH, FEEDFWD_UNITS), MODEL_WIDTH ** -0.5, 0.125, ((1, 16), (2, 8))),
        "up_offset_bias": noise(streams_of[13], (LAYER_COUNT, FEEDFWD_UNITS), 0.3, 4.0, ((1, 8),), jnp.float32),
        "down_matrix": noise(streams_of[14], (LAYER_COUNT, FEEDFWD_UNITS, MODEL_WIDTH), (FEEDFWD_UNITS // 2) ** -0.5, 0.09375, ((1, 8), (2, 16))),
        "down_offset_bias": noise(streams_of[15], (LAYER_COUNT, MODEL_WIDTH), 0.3, 4.0, (), jnp.float32),
        "joined_adapter_reduce": noise(streams_of[16], (LAYER_COUNT, MODEL_WIDTH, ADAPTER_COLUMNS), MODEL_WIDTH ** -0.5, 0.125),
        "joined_adapter_expand": noise(streams_of[17], (LAYER_COUNT, ADAPTER_COLUMNS, 3 * MODEL_WIDTH), ADAPTER_RANK ** -0.5, 1.5, ((2, 8),)),
        "output_adapter_reduce": noise(streams_of[18], (LAYER_COUNT, MODEL_WIDTH, ADAPTER_COLUMNS), (MODEL_WIDTH // 4) ** -0.5, 0.25, ((1, 8),)),
        "output_adapter_expand": noise(streams_of[19], (LAYER_COUNT, ADAPTER_COLUMNS, MODEL_WIDTH), ADAPTER_RANK ** -0.5, 1.5),
        "up_adapter_reduce": noise(streams_of[20], (LAYER_COUNT, MODEL_WIDTH, ADAPTER_COLUMNS), MODEL_WIDTH ** -0.5, 0.125),
        "up_adapter_expand": noise(streams_of[21], (LAYER_COUNT, ADAPTER_COLUMNS, FEEDFWD_UNITS), ADAPTER_RANK ** -0.5, 1.5, ((2, 8),)),
        "down_adapter_reduce": noise(streams_of[22], (LAYER_COUNT, FEEDFWD_UNITS, ADAPTER_COLUMNS), (FEEDFWD_UNITS // 2) ** -0.5, 0.09375, ((1, 8),)),
        "down_adapter_expand": noise(streams_of[23], (LAYER_COUNT, ADAPTER_COLUMNS, MODEL_WIDTH), ADAPTER_RANK ** -0.5, 1.5),
        "cotangent": noise(streams_of[24], (TOKENS, MODEL_WIDTH), 1.0, 6.0, ((0, 128),)),
    }


@jax.custom_vjp
def lowered_rank(v):
    return lax.optimization_barrier(v.astype(jnp.bfloat16)).astype(jnp.float32)

@jax.custom_vjp
def lowered_backward(v):
    return v

def low_keep(v):
    return (lowered_rank(v), None)

def low_pass(kept, grad):
    return (grad,)

def back_keep(v):
    return (v, None)

def back_low(kept, grad):
    return (lowered_rank(grad),)
lowered_rank.defvjp(low_keep, low_pass)
lowered_backward.defvjp(back_keep, back_low)
adapter_scale = 0.5
ln_eps = 1e-05
masked_score = -1e+30
highest_precision = lax.Precision.HIGHEST

def layer_norm(value_rows, gain, shift):
    center = value_rows - lax.optimization_barrier(jnp.mean(value_rows, axis=-1, keepdims=True))
    spread_sq = lax.optimization_barrier(jnp.mean(center * center, axis=-1, keepdims=True))
    return center * lax.rsqrt(spread_sq + ln_eps) * gain + shift

def gelu_tanh(value_rows):
    return 0.5 * value_rows * (1.0 + jnp.tanh(0.7978845608028654 * (value_rows + 0.044715 * value_rows * value_rows * value_rows)))

def row_layout(lengths, order, sequence_adapter):
    lengths = lengths.astype(jnp.int32)
    ends = jnp.cumsum(lengths).astype(jnp.int32)
    starts = ends - lengths
    sequence_slot = lax.optimization_barrier(jnp.sum((order[:, None] >= ends[None, :]).astype(jnp.int32), axis=1)).astype(jnp.int32)
    member = sequence_slot[:, None] == jnp.arange(lengths.shape[0], dtype=jnp.int32)[None, :]
    token_position = (order - lax.optimization_barrier(jnp.sum(jnp.where(member, starts[None, :], 0), axis=1))).astype(jnp.int32)
    adapter_slot = lax.optimization_barrier(jnp.sum(jnp.where(member, sequence_adapter[None, :], 0), axis=1)).astype(jnp.int32)
    column_range = jnp.arange(ADAPTERS * ADAPTER_RANK, dtype=jnp.int32) // ADAPTER_RANK
    adapter_mask = (column_range[None, :] == adapter_slot[:, None]).astype(jnp.float32)
    return (sequence_slot, token_position, adapter_mask)

def column_slot(value_rows, weight):
    copies = lowered_backward(jnp.broadcast_to(value_rows[:, None, :], (value_rows.shape[0], N_TENSOR, value_rows.shape[1])))
    split = weight.reshape(weight.shape[0], N_TENSOR, weight.shape[1] // N_TENSOR)
    final_result = jnp.einsum('tgi,igc->tgc', copies, split, precision=highest_precision)
    return final_result.reshape(value_rows.shape[0], weight.shape[1])

def row_sum(value_rows, weight):
    split_values = value_rows.reshape(value_rows.shape[0], N_TENSOR, value_rows.shape[1] // N_TENSOR)
    split_weight = weight.reshape(N_TENSOR, weight.shape[0] // N_TENSOR, weight.shape[1])
    partial_sums = jnp.einsum('tgi,gic->tgc', split_values, split_weight, precision=highest_precision)
    return lax.optimization_barrier(jnp.sum(lowered_rank(partial_sums), axis=1))

def attention(parts, slopes, allowed, offset):
    head_scale = 1.0 / math.sqrt(HEAD_SIZE)
    queries = jnp.transpose(parts[:, :, 0], (1, 0, 2))
    keys = jnp.transpose(parts[:, :, 1], (1, 0, 2))
    value_rows = jnp.transpose(parts[:, :, 2], (1, 0, 2))

    def one_head(item):
        query, key, value, slope = item
        scores = jnp.dot(query, key.T, precision=highest_precision) * head_scale + slope * offset
        scores = lowered_backward(jnp.where(allowed, scores, masked_score))
        weights = jax.nn.softmax(scores, axis=-1)
        return jnp.dot(lowered_rank(weights), value, precision=highest_precision)
    contexts = lax.map(jax.checkpoint(one_head), (queries, keys, value_rows, slopes))
    return jnp.transpose(contexts, (1, 0, 2)).reshape(parts.shape[0], HEADS * HEAD_SIZE)

def forward_block(residual_state, frozen_params, adapter_params, sequence_slot, token_position, adapter_mask):
    first_norm_gain, first_norm_bias, second_norm_gain, second_norm_bias, joined_matrix, joined_offset_bias, output_matrix, output_offset_bias, up_matrix, up_offset_bias, down_matrix, down_offset_bias = frozen_params
    joined_adapter_lower, joined_adapter_upper, output_adapter_lower, output_adapter_upper, up_adapter_lower, up_adapter_upper, down_adapter_lower, down_adapter_upper = adapter_params
    group_rows = residual_state.shape[0]
    allowed = (sequence_slot[:, None] == sequence_slot[None, :]) & (token_position[None, :] <= token_position[:, None])
    offset = (token_position[None, :] - token_position[:, None]).astype(jnp.float32)
    slopes = jnp.exp2(-0.5 * (jnp.arange(HEADS, dtype=jnp.int32) + 1).astype(jnp.float32))
    for layer_params in range(LAYER_COUNT):
        normalized = lowered_rank(layer_norm(residual_state, first_norm_gain[layer_params], first_norm_bias[layer_params]))
        adapter_joined_part = lowered_backward(lowered_rank(adapter_mask * jnp.dot(normalized, joined_adapter_lower[layer_params], precision=highest_precision)))
        joined_projection = column_slot(normalized, joined_matrix[layer_params]) + joined_offset_bias[layer_params] + adapter_scale * column_slot(adapter_joined_part, joined_adapter_upper[layer_params])
        joined_projection = lowered_backward(lowered_rank(joined_projection))
        parts = joined_projection.reshape(group_rows, HEADS, 3, HEAD_SIZE)
        attended_context = lowered_backward(lowered_rank(attention(parts, slopes, allowed, offset)))
        attention_primary = row_sum(attended_context, output_matrix[layer_params])
        attention_adapter = row_sum(attended_context, output_adapter_lower[layer_params])
        adapter_output_part = lowered_backward(lowered_rank(adapter_mask * attention_adapter))
        adapter_branch = lowered_backward(attention_primary + output_offset_bias[layer_params] + adapter_scale * jnp.dot(adapter_output_part, output_adapter_upper[layer_params], precision=highest_precision))
        residual_state = residual_state + adapter_branch
        normalized_feedforward = lowered_rank(layer_norm(residual_state, second_norm_gain[layer_params], second_norm_bias[layer_params]))
        adapter_up_part = lowered_backward(lowered_rank(adapter_mask * jnp.dot(normalized_feedforward, up_adapter_lower[layer_params], precision=highest_precision)))
        hidden_units = column_slot(normalized_feedforward, up_matrix[layer_params]) + up_offset_bias[layer_params] + adapter_scale * column_slot(adapter_up_part, up_adapter_upper[layer_params])
        hidden_units = lowered_backward(hidden_units)
        activation = lowered_rank(gelu_tanh(hidden_units))
        feedforward_primary = row_sum(activation, down_matrix[layer_params])
        feedforward_adapter = row_sum(activation, down_adapter_lower[layer_params])
        adapter_down_part = lowered_backward(lowered_rank(adapter_mask * feedforward_adapter))
        adapter_branch = lowered_backward(feedforward_primary + down_offset_bias[layer_params] + adapter_scale * jnp.dot(adapter_down_part, down_adapter_upper[layer_params], precision=highest_precision))
        residual_state = residual_state + adapter_branch
    return residual_state

def reference(tokens, lengths, order, sequence_adapter, first_norm_gain, first_norm_bias, second_norm_gain, second_norm_bias, joined_matrix, joined_offset_bias, output_matrix, output_offset_bias, up_matrix, up_offset_bias, down_matrix, down_offset_bias, joined_adapter_reduce, joined_adapter_expand, output_adapter_reduce, output_adapter_expand, up_adapter_reduce, up_adapter_expand, down_adapter_reduce, down_adapter_expand, cotangent):
    frozen_params = tuple((tensor_array.astype(jnp.float32) for tensor_array in (first_norm_gain, first_norm_bias, second_norm_gain, second_norm_bias, joined_matrix, joined_offset_bias, output_matrix, output_offset_bias, up_matrix, up_offset_bias, down_matrix, down_offset_bias)))
    adapter_table = tuple((tensor_array.astype(jnp.float32) for tensor_array in (joined_adapter_reduce, joined_adapter_expand, output_adapter_reduce, output_adapter_expand, up_adapter_reduce, up_adapter_expand, down_adapter_reduce, down_adapter_expand)))
    states = tokens.astype(jnp.float32).reshape(N_DP, GROUP_TOK, MODEL_WIDTH)
    cotangents = cotangent.astype(jnp.float32).reshape(N_DP, GROUP_TOK, MODEL_WIDTH)

    def one_group(running_sums, item):
        residual_state, group_tangent, group_length_list, group_sorting, group_labels = item
        sequence_slot, token_position, adapter_mask = row_layout(group_length_list, group_sorting, group_labels)

        def forward_call(value_rows, adapter_params):
            return forward_block(value_rows, frozen_params, adapter_params, sequence_slot, token_position, adapter_mask)
        final_result, pullback = jax.vjp(forward_call, residual_state, adapter_table)
        residual_state_gradient, adapter_gradients = pullback(group_tangent)
        return (tuple((grand_total + additional for grand_total, additional in zip(running_sums, adapter_gradients))), (final_result, residual_state_gradient))
    start = tuple((jnp.zeros_like(tensor_array) for tensor_array in adapter_table))
    running_sums, (results, grads) = lax.scan(one_group, start, (states, cotangents, lengths, order, sequence_adapter))
    return (results.reshape(TOKENS, MODEL_WIDTH), grads.reshape(TOKENS, MODEL_WIDTH), running_sums[0], running_sums[1], running_sums[2], running_sums[3], running_sums[4], running_sums[5], running_sums[6], running_sums[7])
```

```python
import functools
import math

import jax
import jax.numpy as jnp
from jax import lax
from jax.experimental import pallas as pl
from jax.experimental.pallas import tpu as pltpu
from jax.sharding import PartitionSpec as P

HEAD = 128
WIDTH = 2048
LANES = 128
WIDE = WIDTH + LANES
ROWS = 160
HALF = ROWS // 2
PAIR = 2 * ROWS
GROUP = 8 * ROWS
QKV = 768
UNITS = 1024
CTX = 256
BLOCK = 32
AUX_UP, AUX_TOKEN, AUX_START, AUX_ALL = QKV, QKV + UNITS, QKV + UNITS + GROUP, QKV + UNITS + 2 * GROUP
SCALE = 0.5
EPS = 1e-05
MASKED = -1e30
LOG2E = 1.4426950408889634
VMEM_LIMIT = 60 * 2**20
BF = jnp.bfloat16
F32 = jnp.float32
BY_MESH = pl.DeviceIdType.MESH
ANYWHERE = pl.BlockSpec(memory_space=pl.ANY)
IN_VMEM = pl.BlockSpec(memory_space=pltpu.VMEM)


def nn(left, right):
    return jnp.dot(left, right, preferred_element_type=F32)


def nt(left, right):
    return lax.dot_general(left, right, (((1,), (1,)), ((), ())), preferred_element_type=F32)


def tn(left, right):
    return lax.dot_general(left, right, (((0,), (0,)), ((), ())), preferred_element_type=F32)


def rows_at(start, size):
    return pl.ds(pl.multiple_of(start, 16), size)


def lanes_at(start, size):
    return pl.ds(pl.multiple_of(start, 128), size)


def loop(count, body):
    def step(index, carry):
        body(index)
        return carry

    lax.fori_loop(0, count, step, 0)


class Place:
    def __init__(self):
        dp = lax.axis_index("dp")
        tensor = lax.axis_index("tensor")
        self.dp = dp
        self.z = lax.div(dp, 4)
        self.xl = lax.rem(lax.div(dp, 2), 2)
        self.c = lax.rem(dp, 2)
        self.y = lax.div(tensor, 2)
        self.g = lax.rem(tensor, 2)
        self.x = self.g * 2 + self.xl
        self.sib = self.at(c=1 - self.c)
        self.up = self.at(y=lax.rem(self.y + 1, 4))
        self.down = self.at(y=lax.rem(self.y + 3, 4))
        self.z_up = self.at(z=lax.rem(self.z + 1, 4))
        self.z_down = self.at(z=lax.rem(self.z + 3, 4))
        self.partner = self.at(g=self.c, c=self.g)
        self.home = self.c == self.g
        self.away = self.c != self.g

    def at(self, z=None, x=None, xl=None, c=None, y=None, g=None):
        z = self.z if z is None else z
        c = self.c if c is None else c
        y = self.y if y is None else y
        if x is None:
            xl = self.xl if xl is None else xl
            g = self.g if g is None else g
        else:
            xl = lax.rem(x, 2)
            g = lax.div(x, 2)
        return (z * 4 + xl * 2 + c, y * 2 + g)

    def in_row(self, dx, core):
        return self.at(x=lax.rem(self.x + dx, 4), c=core)

    def row_mates(self):
        return [self.in_row(dx, core) for dx in (1, 2, 3) for core in (0, 1)]

    def ring(self, dy, same):
        return lax.rem(self.y + dy + 4, 4) * 2 + (self.c if same else 1 - self.c)


def greet(devices):
    barrier = pltpu.get_barrier_semaphore()
    for device in devices:
        pl.semaphore_signal(barrier, 1, device_id=device, device_id_type=BY_MESH)
    pl.semaphore_wait(barrier, len(devices))


def remote(src, dst, send, recv, device):
    return pltpu.make_async_remote_copy(
        src_ref=src, dst_ref=dst, send_sem=send, recv_sem=recv, device_id=device, device_id_type=BY_MESH
    )


class Gather:
    SENDS = (
        (0, True, None),
        (0, True, None),
        (0, True, None),
        (-1, True, 0),
        (1, True, 1),
        (-1, True, None),
        (1, True, None),
        (2, True, 0),
        (2, True, 1),
    )
    LANDS = (
        (0, False, None),
        (-1, True, None),
        (1, True, None),
        (2, True, 0),
        (2, True, 1),
        (-1, False, None),
        (1, False, None),
        (2, False, 0),
        (2, False, 1),
    )

    def __init__(self, place, buf, send, recv):
        self.place, self.buf, self.send, self.recv = place, buf, send, recv
        p = place
        self.to = (p.sib, p.up, p.down, p.up, p.down, p.sib, p.sib, p.sib, p.sib)

    def piece(self, what):
        dy, same, half = what
        start = self.place.ring(dy, same) * ROWS
        if half is None:
            return self.buf.at[rows_at(start, ROWS)]
        return self.buf.at[rows_at(start + half * HALF, HALF)]

    def copy(self, i):
        piece = self.piece(self.SENDS[i])
        return remote(piece, piece, self.send.at[i], self.recv.at[i], self.to[i])

    def landed(self, i):
        piece = self.piece(self.LANDS[i])
        remote(piece, piece, self.send.at[i], self.recv.at[i], self.to[i]).wait_recv()

    def begin(self):
        for i in (1, 2, 0):
            self.copy(i).start()

    def near(self):
        self.landed(1)
        self.copy(3).start()
        self.copy(5).start()
        self.landed(2)
        self.copy(4).start()
        self.copy(6).start()

    def far(self):
        self.landed(3)
        self.copy(7).start()
        self.landed(4)
        self.copy(8).start()

    def own_pair(self):
        self.landed(0)

    def near_pairs(self):
        self.landed(5)
        self.landed(6)

    def far_pair(self):
        self.landed(7)
        self.landed(8)

    def end(self):
        for i in range(9):
            self.copy(i).wait_send()


class Scatter:
    def __init__(self, place, part, sib_in, relay, near, send, recv):
        self.place, self.part, self.sib_in, self.relay, self.near = place, part, sib_in, relay, near
        self.send, self.recv = send, recv

    def mine(self, dy, half=None):
        start = self.place.ring(dy, True) * ROWS
        if half is None:
            return self.part.at[rows_at(start, ROWS)]
        return self.part.at[rows_at(start + half * HALF, HALF)]

    def others(self, dy):
        return self.part.at[rows_at(self.place.ring(dy, False) * ROWS, ROWS)]

    def copy(self, i):
        p = self.place
        if i < 4:
            src, dst, to = self.others(i), self.sib_in.at[i], p.sib
        elif i == 4:
            src, dst, to = self.mine(2, 0), self.relay.at[0], p.up
        elif i == 5:
            src, dst, to = self.mine(2, 1), self.relay.at[1], p.down
        elif i == 6:
            src, dst, to = self.mine(1, 1), self.near.at[0, pl.ds(HALF, HALF)], p.up
        elif i == 7:
            src, dst, to = self.mine(-1, 0), self.near.at[1, pl.ds(0, HALF)], p.down
        elif i == 8:
            src, dst, to = self.mine(1, 0), self.near.at[0, pl.ds(0, HALF)], p.up
        else:
            src, dst, to = self.mine(-1, 1), self.near.at[1, pl.ds(HALF, HALF)], p.down
        return remote(src, dst, self.send.at[i], self.recv.at[i], to)

    def exchange(self, dy):
        self.copy(dy % 4).start()

    def combine(self, dy):
        self.copy(dy % 4).wait_recv()
        start = self.place.ring(dy, True) * ROWS
        add_rows(self.part, start, self.sib_in.at[dy % 4], 0, ROWS)

    def relay_out(self):
        self.copy(4).start()
        self.copy(5).start()

    def near_free(self):
        self.copy(6).start()
        self.copy(7).start()

    def near_rest(self):
        self.copy(4).wait_recv()
        add_rows(self.part, self.place.ring(1, True) * ROWS, self.relay.at[0], 0, HALF)
        self.copy(8).start()
        self.copy(5).wait_recv()
        add_rows(self.part, self.place.ring(-1, True) * ROWS + HALF, self.relay.at[1], 0, HALF)
        self.copy(9).start()

    def arrived(self):
        for i in (6, 7, 8, 9):
            self.copy(i).wait_recv()

    def total(self, start, size, lanes):
        own = self.part[rows_at(self.place.ring(0, True) * ROWS + start, size), lanes].astype(F32)
        return (
            own
            + self.near[0, rows_at(start, size), lanes].astype(F32)
            + self.near[1, rows_at(start, size), lanes].astype(F32)
        )

    def end(self):
        for i in range(10):
            self.copy(i).wait_send()


def scatter_scratch():
    return [
        pltpu.VMEM((GROUP, WIDE), BF),
        pltpu.VMEM((4, ROWS, WIDE), BF),
        pltpu.VMEM((2, HALF, WIDE), BF),
        pltpu.VMEM((2, ROWS, WIDE), BF),
        pltpu.SemaphoreType.DMA((10,)),
        pltpu.SemaphoreType.DMA((10,)),
    ]


def gather_scratch():
    return [pltpu.VMEM((GROUP, WIDE), BF), pltpu.SemaphoreType.DMA((9,)), pltpu.SemaphoreType.DMA((9,))]


def add_rows(dst, start, src, src_start, count):
    def body(index):
        at = rows_at(start + index * 16, 16)
        dst[at, :] = (dst[at, :].astype(F32) + src[rows_at(src_start + index * 16, 16), :].astype(F32)).astype(BF)

    loop(count // 16, body)


class Weights:
    def __init__(self, place, piece, full, by_rows, send, recv):
        self.place, self.piece, self.full, self.by_rows = place, piece, full, by_rows
        self.send, self.recv = send, recv

    def slot(self, index, count=1):
        span = lanes_at(index * 128, count * 128)
        return self.full.at[span, :] if self.by_rows else self.full.at[:, span]

    def first(self):
        p = self.place
        mark = self.recv.at[p.xl * 2 + p.c]
        for dx in (2, 1, 3):
            remote(self.piece, self.slot(p.dp), self.send.at[dx], mark, p.in_row(dx, p.g)).start()

        @pl.when(p.home)
        def _():
            pltpu.make_async_copy(self.piece, self.slot(p.dp), mark).start()

        @pl.when(p.away)
        def _():
            remote(self.piece, self.slot(p.dp), self.send.at[0], mark, p.sib).start()

    def block(self, dz, first=0, count=4):
        return self.slot(lax.rem(self.place.z + dz + 4, 4) * 4 + first, count)

    def copy(self, i):
        p = self.place
        dz, first, count, to = (
            (0, 0, 4, p.z_up),
            (0, 0, 4, p.z_down),
            (-1, 0, 2, p.z_up),
            (1, 2, 2, p.z_down),
        )[i]
        block = self.block(dz, first, count)
        return remote(block, block, self.send.at[4 + i], self.recv.at[4 + i], to)

    def landed(self, i):
        dz, first, count = ((-1, 0, 4), (1, 0, 4), (2, 0, 2), (2, 2, 2))[i]
        block = self.block(dz, first, count)
        remote(block, block, self.send.at[4 + i], self.recv.at[4 + i], self.place.z_up).wait_recv()

    def second(self):
        for index in range(4):
            slot = self.slot(self.place.z * 4 + index)
            remote(slot, slot, self.send.at[0], self.recv.at[index], self.place.sib).wait_recv()
        self.copy(0).start()
        self.copy(1).start()

    def third(self):
        self.landed(0)
        self.copy(2).start()
        self.landed(1)
        self.copy(3).start()

    def arrived(self):
        self.landed(2)
        self.landed(3)

    def end(self):
        p = self.place
        for dx in (1, 2, 3):
            remote(self.piece, self.slot(p.dp), self.send.at[dx], self.recv.at[0], p.sib).wait_send()

        @pl.when(p.away)
        def _():
            remote(self.piece, self.slot(p.dp), self.send.at[0], self.recv.at[0], p.sib).wait_send()

        for i in range(4):
            self.copy(i).wait_send()


def weight_marks():
    return [pltpu.SemaphoreType.DMA((8,)), pltpu.SemaphoreType.DMA((8,))]


class Swap:
    def __init__(self, place, pairs, send, recv):
        self.place, self.pairs, self.send, self.recv = place, pairs, send, recv

    def begin(self, i):
        src, dst = self.pairs[i]
        p = self.place

        @pl.when(p.home)
        def _():
            pltpu.make_async_copy(src, dst, self.recv.at[i]).start()

        @pl.when(p.away)
        def _():
            remote(src, dst, self.send.at[i], self.recv.at[i], p.partner).start()

    def arrived(self, i):
        src, dst = self.pairs[i]
        remote(src, dst, self.send.at[i], self.recv.at[i], self.place.sib).wait_recv()

    def end(self):
        @pl.when(self.place.away)
        def _():
            for i, (src, dst) in enumerate(self.pairs):
                remote(src, dst, self.send.at[i], self.recv.at[i], self.place.sib).wait_send()


def swap_marks(count):
    return [pltpu.SemaphoreType.DMA((count,)), pltpu.SemaphoreType.DMA((count,))]


def normalise(value):
    mean = jnp.mean(value, axis=-1, keepdims=True)
    center = value - mean
    inverse = lax.rsqrt(jnp.mean(center * center, axis=-1, keepdims=True) + EPS)
    return center * inverse, inverse


def norm_back(value, gain, grad):
    normed, inverse = normalise(value)
    e = grad * gain
    return (e - jnp.mean(e, axis=-1, keepdims=True) - normed * jnp.mean(e * normed, axis=-1, keepdims=True)) * inverse


def pair_rows(place, dy):
    return rows_at(lax.rem(place.y + dy + 4, 4) * PAIR, PAIR)


def wide_product(put, make):
    loop(4, lambda j: put(lanes_at(j * 512, 512), make(lanes_at(j * 512, 512))))
    put(pl.ds(WIDTH, LANES), make(pl.ds(WIDTH, LANES)))


def call(kernel, collective, ins, specs, outs, out_specs, scratch):
    return pl.pallas_call(
        kernel,
        name=kernel.__name__,
        out_shape=outs,
        in_specs=specs,
        out_specs=out_specs,
        scratch_shapes=scratch,
        compiler_params=pltpu.CompilerParams(
            collective_id=collective, has_side_effects=True, vmem_limit_bytes=VMEM_LIMIT
        ),
    )(*ins)


def shape(*dims, kind=BF):
    return jax.ShapeDtypeStruct(dims, kind)


def project_kernel(
    tokens, cotangent, gain, shift, joined_reduce, down_expand, mask,
    joined_expand, aux, joined_piece, output_piece, output_reduce, up_expand, down_reduce,
    qkv, side_q, normed_own, gathered_grad, joined_full, output_full, tokens_own, cot_own, mask_own, aux_own,
    up_expand_own, down_reduce_own,
    stage, stage_grad, aux_here, joined_here, rows, rows_send, rows_recv, grads, grads_send, grads_recv,
    w_send, w_recv, o_send, o_recv, swap_send, swap_recv, out_sem,
):
    p = Place()
    greet([p.sib, p.up, p.down, p.z_up, p.z_down] + p.row_mates())
    joined = Weights(p, joined_piece, joined_here.at[pl.ds(0, WIDTH)], True, w_send, w_recv)
    output = Weights(p, output_piece, output_full.at[:, pl.ds(0, WIDTH)], False, o_send, o_recv)
    own_rows = rows_at(p.ring(0, True) * ROWS, ROWS)
    their_rows = rows_at((p.y * 2 + p.g) * ROWS, ROWS)
    swap = Swap(
        p,
        [
            (stage, rows.at[their_rows]),
            (stage_grad, grads.at[their_rows]),
            (joined_expand, joined_here.at[pl.ds(WIDTH, LANES)]),
            (aux, aux_here),
            (tokens, tokens_own),
            (cotangent, cot_own),
            (mask, mask_own),
            (output_reduce, output_full.at[:, pl.ds(WIDTH, LANES)]),
            (up_expand, up_expand_own),
            (down_reduce, down_reduce_own),
        ],
        swap_send,
        swap_recv,
    )
    joined.first()

    def norm_block(index):
        at = rows_at(index * BLOCK, BLOCK)
        normed, _ = normalise(tokens[at, :].astype(F32))
        stage[at, pl.ds(0, WIDTH)] = (normed * gain[...] + shift[...]).astype(BF)

    loop(ROWS // BLOCK, norm_block)
    mask_rows = mask[...].astype(F32)
    stage[:, pl.ds(WIDTH, LANES)] = (mask_rows * nn(stage[:, pl.ds(0, WIDTH)], joined_reduce[...])).astype(BF)
    swap.begin(0)
    swap.begin(2)
    swap.begin(3)
    output.first()
    stage_grad[:, pl.ds(0, WIDTH)] = cotangent[...]
    stage_grad[:, pl.ds(WIDTH, LANES)] = (mask_rows * (SCALE * nt(cotangent[...], down_expand[...]))).astype(BF)
    joined.second()
    swap.begin(1)
    gather = Gather(p, rows, rows_send, rows_recv)
    gather_grad = Gather(p, grads, grads_send, grads_recv)
    swap.arrived(0)
    gather.begin()
    for i in range(4, 10):
        swap.begin(i)
    output.second()
    swap.arrived(1)
    gather_grad.begin()
    gather.near()
    joined.third()
    output.third()
    swap.arrived(2)
    swap.arrived(3)
    gather.far()
    joined.arrived()
    copies = [
        pltpu.make_async_copy(joined_here, joined_full, out_sem.at[0]),
        pltpu.make_async_copy(aux_here, aux_own, out_sem.at[1]),
        pltpu.make_async_copy(rows.at[own_rows, pl.ds(0, WIDTH)], normed_own, out_sem.at[2]),
    ]
    for copy in copies:
        copy.start()

    def project(dy):
        at = pair_rows(p, dy)

        def body(j):
            lanes = lanes_at(j * 256, 256)
            qkv[at, lanes] = (nn(rows[at, :], joined_here[:, lanes]) + aux_here[0:1, lanes]).astype(BF)

        loop(QKV // 256, body)

    gather.own_pair()
    project(0)
    gather.near_pairs()
    project(1)
    project(-1)
    gather_grad.near()
    gather.far_pair()
    project(2)
    last = pltpu.make_async_copy(rows.at[:, pl.ds(WIDTH, LANES)], side_q, out_sem.at[3])
    last.start()
    gather_grad.far()
    gather_grad.own_pair()
    gather_grad.near_pairs()
    gather_grad.far_pair()
    grads_out = pltpu.make_async_copy(grads, gathered_grad, out_sem.at[4])
    grads_out.start()
    output.arrived()
    for i in range(4, 10):
        swap.arrived(i)
    swap.end()
    gather.end()
    gather_grad.end()
    joined.end()
    output.end()
    for copy in copies + [last, grads_out]:
        copy.wait()


def project_call(ins):
    outs = [
        shape(GROUP, QKV), shape(GROUP, LANES), shape(ROWS, WIDTH), shape(GROUP, WIDE), shape(WIDE, QKV),
        shape(CTX, WIDE), shape(ROWS, WIDTH), shape(ROWS, WIDTH), shape(ROWS, LANES),
        shape(8, AUX_ALL, kind=F32), shape(LANES, UNITS), shape(UNITS, LANES),
    ]
    return call(
        project_kernel,
        1,
        ins,
        [IN_VMEM] * 10 + [ANYWHERE] * 4,
        outs,
        [IN_VMEM] + [ANYWHERE] * 11,
        [
            pltpu.VMEM((ROWS, WIDE), BF), pltpu.VMEM((ROWS, WIDE), BF), pltpu.VMEM((8, AUX_ALL), F32),
            pltpu.VMEM((WIDE, QKV), BF), *gather_scratch(), *gather_scratch(), *weight_marks(), *weight_marks(),
            *swap_marks(10), pltpu.SemaphoreType.DMA((5,)),
        ],
    )


def slope_row(place, head, tokens_row):
    number = (place.ring(0, True) * 2 + head + 1).astype(F32)
    slope = jnp.exp2(jnp.full((1, GROUP), -0.5, F32) * number)
    return slope * LOG2E * tokens_row


def attend_kernel(
    qkv, aux, info, output_full, tokens, mask, output_expand, output_shift, gain, shift, up_reduce, up_piece, up_expand,
    normed, middle, side_o, context, probs_out, up_full,
    probs, part, sib_in, relay, near, s_send, s_recv, w_send, w_recv, out_sem,
):
    p = Place()
    greet([p.sib, p.up, p.down, p.z_up, p.z_down] + p.row_mates())
    up = Weights(p, up_piece, up_full.at[pl.ds(0, WIDTH)], True, w_send, w_recv)
    up.first()
    tail = pltpu.make_async_copy(up_expand, up_full.at[pl.ds(WIDTH, LANES)], out_sem.at[4])
    tail.start()
    token_row = aux[0:1, pl.ds(AUX_TOKEN, GROUP)]
    probs_copies = []

    def attend(dy):
        base = lax.rem(p.y + dy + 4, 4) * PAIR

        def body(index):
            at = rows_at(base + index * ROWS, ROWS)
            query_token = info[at, 0:1]
            query_start = info[at, 1:2]
            allowed = (token_row <= query_token) & (token_row >= query_start)
            for head in range(2):
                first = head * 3 * HEAD
                scores = nt(qkv[at, first : first + HEAD], qkv[:, first + HEAD : first + 2 * HEAD])
                scores = scores * (LOG2E / math.sqrt(HEAD)) + slope_row(p, head, token_row)
                scores = jnp.where(allowed, scores, MASKED)
                top = jnp.max(scores, axis=-1, keepdims=True)
                weights = jnp.exp2(scores - top)
                total = jnp.sum(weights, axis=-1, keepdims=True)
                weights = (weights * (1.0 / total)).astype(BF)
                probs[head, at, :] = weights
                context[at, head * HEAD : (head + 1) * HEAD] = nn(
                    weights, qkv[:, first + 2 * HEAD : first + 3 * HEAD]
                ).astype(BF)

        loop(2, body)
        at = pair_rows(p, dy)
        copy = pltpu.make_async_copy(probs.at[:, at], probs_out.at[:, at], out_sem.at[dy % 4])
        copy.start()
        probs_copies.append(copy)

        def put(lanes, value):
            part[at, lanes] = value.astype(BF)

        wide_product(put, lambda lanes: nn(context[at, :], output_full[:, lanes]))

    scatter = Scatter(p, part, sib_in, relay, near, s_send, s_recv)
    attend(2)
    scatter.exchange(2)
    up.second()
    attend(1)
    scatter.exchange(1)
    scatter.combine(2)
    scatter.relay_out()
    attend(-1)
    scatter.exchange(-1)
    scatter.combine(1)
    scatter.combine(-1)
    scatter.near_free()
    attend(0)
    scatter.exchange(0)
    scatter.near_rest()
    scatter.combine(0)
    up.third()
    scatter.arrived()
    mask_rows = mask[...].astype(F32)
    side = (mask_rows * scatter.total(0, ROWS, pl.ds(WIDTH, LANES))).astype(BF)
    side_o[...] = side

    def add_tile(j):
        lanes = lanes_at(j * 512, 512)
        middle[:, lanes] = (
            tokens[:, lanes].astype(F32)
            + scatter.total(0, ROWS, lanes)
            + output_shift[:, lanes]
            + SCALE * nn(side, output_expand[:, lanes])
        )

    loop(4, add_tile)

    def norm_block(index):
        at = rows_at(index * BLOCK, BLOCK)
        value, _ = normalise(middle[at, :])
        normed[at, pl.ds(0, WIDTH)] = (value * gain[...] + shift[...]).astype(BF)

    loop(ROWS // BLOCK, norm_block)
    normed[:, pl.ds(WIDTH, LANES)] = (mask_rows * nn(normed[:, pl.ds(0, WIDTH)], up_reduce[...])).astype(BF)
    up.arrived()
    scatter.end()
    up.end()
    for copy in probs_copies + [tail]:
        copy.wait()


def attend_call(ins):
    outs = [
        shape(ROWS, WIDE), shape(ROWS, WIDTH, kind=F32), shape(ROWS, LANES), shape(GROUP, CTX),
        shape(2, GROUP, GROUP), shape(WIDE, UNITS),
    ]
    return call(
        attend_kernel,
        2,
        ins,
        [IN_VMEM] * 11 + [ANYWHERE] * 2,
        outs,
        [IN_VMEM] * 4 + [ANYWHERE] * 2,
        [pltpu.VMEM((2, GROUP, GROUP), BF), *scatter_scratch(), *weight_marks(), pltpu.SemaphoreType.DMA((5,))],
    )


def feed_kernel(
    normed, middle, side_o, grads, up_full, aux, mask, cotangent, down_shift, gain, up_reduce, output_expand, down_expand,
    down_piece, down_reduce,
    block_out, grad_out, grad_stage, by_shard, whole,
    down_full, rows, rows_send, rows_recv, act, slope, part, sib_in, relay, near, s_send, s_recv,
    part_out, sib_in_out, relay_out, near_out, t_send, t_recv, w_send, w_recv, own_sem,
):
    p = Place()
    own_rows = rows_at(p.ring(0, True) * ROWS, ROWS)
    stage = pltpu.make_async_copy(normed, rows.at[own_rows], own_sem.at[0])
    stage.start()
    greet([p.sib, p.up, p.down, p.z_up, p.z_down] + p.row_mates())
    down = Weights(p, down_piece, down_full.at[:, pl.ds(0, WIDTH)], False, w_send, w_recv)
    down.first()
    tail = pltpu.make_async_copy(down_reduce, down_full.at[:, pl.ds(WIDTH, LANES)], own_sem.at[1])
    tail.start()
    gather = Gather(p, rows, rows_send, rows_recv)
    stage.wait()
    gather.begin()

    def hide(dy):
        at = pair_rows(p, dy)

        def body(j):
            lanes = lanes_at(j * 256, 256)
            v = nn(rows[at, :], up_full[:, lanes]) + aux[0:1, lanes_at(AUX_UP + j * 256, 256)]
            inner = 0.7978845608028654 * (v + 0.044715 * v * v * v)
            t = jnp.tanh(inner)
            act[at, lanes] = (0.5 * v * (1.0 + t)).astype(BF)
            slope[at, lanes] = (
                0.5 * (1.0 + t)
                + 0.5 * v * (1.0 - t * t) * (0.7978845608028654 * (1.0 + 3.0 * 0.044715 * v * v))
            ).astype(BF)

        loop(UNITS // 256, body)

    def back(dy):
        at = pair_rows(p, dy)

        def body(j):
            lanes = lanes_at(j * 256, 256)
            value = nt(grads[at, :], down_full[lanes, :])
            slope[at, lanes] = (value * slope[at, lanes].astype(F32)).astype(BF)

        loop(UNITS // 256, body)

        def put(lanes, value):
            part[at, lanes] = value.astype(BF)

        wide_product(put, lambda lanes: nt(slope[at, :], up_full[lanes, :]))

    def forth(dy):
        at = pair_rows(p, dy)

        def put(lanes, value):
            part_out[at, lanes] = value.astype(BF)

        wide_product(put, lambda lanes: nn(act[at, :], down_full[:, lanes]))

    down.second()
    gather.own_pair()
    hide(0)
    gather.near()
    gather.near_pairs()
    hide(1)
    hide(-1)
    gather.far()
    down.third()
    gather.far_pair()
    hide(2)
    down.arrived()
    tail.wait()
    scatter = Scatter(p, part, sib_in, relay, near, s_send, s_recv)
    back(2)
    scatter.exchange(2)
    back(1)
    scatter.exchange(1)
    scatter.combine(2)
    scatter.relay_out()
    back(-1)
    scatter.exchange(-1)
    scatter.combine(1)
    scatter.combine(-1)
    scatter.near_free()
    back(0)
    scatter.exchange(0)
    scatter.near_rest()
    scatter.combine(0)
    scatter_out = Scatter(p, part_out, sib_in_out, relay_out, near_out, t_send, t_recv)
    forth(2)
    scatter_out.exchange(2)
    forth(1)
    scatter_out.exchange(1)
    scatter_out.combine(2)
    scatter_out.relay_out()
    forth(-1)
    scatter_out.exchange(-1)
    scatter_out.combine(1)
    scatter_out.combine(-1)
    scatter_out.near_free()
    forth(0)
    scatter_out.exchange(0)

    def by_unit(j):
        at = lanes_at(j * 256, 256)
        by_shard[at, :] = tn(act[:, at], grads[:, pl.ds(WIDTH, LANES)]).astype(BF)
        by_shard[lanes_at(UNITS + j * 256, 256), :] = (
            SCALE * tn(slope[:, at], rows[:, pl.ds(WIDTH, LANES)])
        ).astype(BF)

    loop(UNITS // 256, by_unit)
    scatter.arrived()
    mask_rows = mask[...].astype(F32)
    side_u = (mask_rows * scatter.total(0, ROWS, pl.ds(WIDTH, LANES))).astype(BF)

    def norm_block(index):
        at = rows_at(index * BLOCK, BLOCK)
        side = (mask[at, :].astype(F32) * scatter.total(index * BLOCK, BLOCK, pl.ds(WIDTH, LANES))).astype(BF)
        grad = scatter.total(index * BLOCK, BLOCK, pl.ds(0, WIDTH)) + nt(side, up_reduce[...])
        grad = cotangent[at, :].astype(F32) + norm_back(middle[at, :], gain[...], grad)
        grad_out[at, :] = grad
        grad_stage[at, pl.ds(0, WIDTH)] = grad.astype(BF)

    loop(ROWS // BLOCK, norm_block)
    grad_stage[:, pl.ds(WIDTH, LANES)] = (
        mask_rows * (SCALE * nt(grad_stage[:, pl.ds(0, WIDTH)], output_expand[...]))
    ).astype(BF)

    def by_column(j):
        lanes = lanes_at(j * 256, 256)
        whole[lanes, :] = tn(normed[:, lanes], side_u).astype(BF)
        whole[lanes_at(WIDTH + j * 256, 256), :] = (SCALE * tn(grad_stage[:, lanes], side_o[...])).astype(BF)

    loop(WIDTH // 256, by_column)
    scatter_out.near_rest()
    scatter_out.combine(0)
    scatter_out.arrived()
    side_d = (mask_rows * scatter_out.total(0, ROWS, pl.ds(WIDTH, LANES))).astype(BF)

    def add_tile(j):
        lanes = lanes_at(j * 256, 256)
        block_out[:, lanes] = (
            middle[:, lanes]
            + scatter_out.total(0, ROWS, lanes)
            + down_shift[:, lanes]
            + SCALE * nn(side_d, down_expand[:, lanes])
        )
        whole[lanes_at(2 * WIDTH + j * 256, 256), :] = (SCALE * tn(cotangent[:, lanes], side_d)).astype(BF)

    loop(WIDTH // 256, add_tile)
    gather.end()
    scatter.end()
    scatter_out.end()
    down.end()


def feed_call(ins):
    outs = [
        shape(ROWS, WIDTH, kind=F32), shape(ROWS, WIDTH, kind=F32), shape(ROWS, WIDE), shape(2 * UNITS, LANES),
        shape(3 * WIDTH, LANES),
    ]
    return call(
        feed_kernel,
        3,
        ins,
        [IN_VMEM] * 13 + [ANYWHERE] * 2,
        outs,
        [IN_VMEM] * 5,
        [
            pltpu.VMEM((UNITS, WIDE), BF), *gather_scratch(), pltpu.VMEM((GROUP, UNITS), BF),
            pltpu.VMEM((GROUP, UNITS), BF), *scatter_scratch(), *scatter_scratch(), *weight_marks(),
            pltpu.SemaphoreType.DMA((2,)),
        ],
    )


def back_kernel(
    grad_stage, output_full, qkv, context, joined_full, side_q, tokens, gain, mask, grad, joined_reduce, normed,
    block_own, probs_in,
    block_out, input_grad, by_shard, whole,
    rows, rows_send, rows_recv, probs, key_grad, value_grad, joined_grad, result,
    part, sib_in, relay, near, s_send, s_recv, swap_send, swap_recv, own_sem,
):
    p = Place()
    own_rows = rows_at(p.ring(0, True) * ROWS, ROWS)
    stage = pltpu.make_async_copy(grad_stage, rows.at[own_rows], own_sem.at[0])
    stage.start()
    loads = []
    for dy in (0, 1, -1, 2):
        at = pair_rows(p, dy)
        load = pltpu.make_async_copy(probs_in.at[:, at], probs.at[:, at], own_sem.at[1 + dy % 4])
        load.start()
        loads.append(load)
    greet([p.sib, p.up, p.down] + p.row_mates())
    gather = Gather(p, rows, rows_send, rows_recv)
    stage.wait()
    gather.begin()
    swap = Swap(p, [(block_own, block_out), (result, input_grad)], swap_send, swap_recv)
    swap.begin(0)

    def back(dy, first):
        base = lax.rem(p.y + dy + 4, 4) * PAIR

        def body(index):
            at = rows_at(base + index * ROWS, ROWS)
            context_grad = nt(rows[at, :], output_full[...]).astype(BF)
            for head in range(2):
                start = head * 3 * HEAD
                query = qkv[at, start : start + HEAD]
                key = qkv[:, start + HEAD : start + 2 * HEAD]
                value = qkv[:, start + 2 * HEAD : start + 3 * HEAD]
                own = context_grad[:, head * HEAD : (head + 1) * HEAD]
                weights = probs[head, at, :]
                kept = weights.astype(F32)
                weight_grad = nt(own, value)
                mean = jnp.sum(kept * weight_grad, axis=-1, keepdims=True)
                score_grad = (kept * (weight_grad - mean)).astype(BF)
                joined_grad[at, start : start + HEAD] = (nn(score_grad, key) * (1.0 / math.sqrt(HEAD))).astype(BF)
                value_part = tn(weights, own)
                key_part = tn(score_grad, query)
                value_grad[head] = value_grad[head] + value_part
                key_grad[head] = key_grad[head] + key_part

        loop(2, body)

    value_grad[...] = jnp.zeros_like(value_grad)
    key_grad[...] = jnp.zeros_like(key_grad)
    gather.own_pair()
    loads[0].wait()
    back(0, True)
    gather.near()
    gather.near_pairs()
    loads[1].wait()
    back(1, False)
    loads[2].wait()
    back(-1, False)
    gather.far()
    gather.far_pair()
    loads[3].wait()
    back(2, False)
    for head in range(2):
        start = head * 3 * HEAD
        joined_grad[:, start + HEAD : start + 2 * HEAD] = (key_grad[head] * (1.0 / math.sqrt(HEAD))).astype(BF)
        joined_grad[:, start + 2 * HEAD : start + 3 * HEAD] = value_grad[head].astype(BF)

    def product(dy):
        at = pair_rows(p, dy)

        def put(lanes, value):
            part[at, lanes] = value.astype(BF)

        wide_product(put, lambda lanes: nt(joined_grad[at, :], joined_full[lanes, :]))

    scatter = Scatter(p, part, sib_in, relay, near, s_send, s_recv)
    product(2)
    scatter.exchange(2)
    product(1)
    scatter.exchange(1)
    scatter.combine(2)
    scatter.relay_out()
    product(-1)
    scatter.exchange(-1)
    scatter.combine(1)
    scatter.combine(-1)
    scatter.near_free()
    product(0)
    scatter.exchange(0)
    scatter.near_rest()
    scatter.combine(0)
    by_shard[pl.ds(0, CTX), :] = tn(context[...], rows[:, pl.ds(WIDTH, LANES)]).astype(BF)

    def by_lane(j):
        lanes = lanes_at(j * 256, 256)
        by_shard[lanes_at(CTX + j * 256, 256), :] = (SCALE * tn(joined_grad[:, lanes], side_q[...])).astype(BF)

    loop(QKV // 256, by_lane)
    scatter.arrived()
    side = (mask[...].astype(F32) * scatter.total(0, ROWS, pl.ds(WIDTH, LANES))).astype(BF)

    def by_column(j):
        lanes = lanes_at(j * 256, 256)
        whole[lanes, :] = tn(normed[:, lanes], side).astype(BF)

    loop(WIDTH // 256, by_column)

    def norm_block(index):
        at = rows_at(index * BLOCK, BLOCK)
        side_rows = (mask[at, :].astype(F32) * scatter.total(index * BLOCK, BLOCK, pl.ds(WIDTH, LANES))).astype(BF)
        back_grad = scatter.total(index * BLOCK, BLOCK, pl.ds(0, WIDTH)) + nt(side_rows, joined_reduce[...])
        result[at, :] = grad[at, :] + norm_back(tokens[at, :].astype(F32), gain[...], back_grad)

    loop(ROWS // BLOCK, norm_block)
    swap.begin(1)
    gather.end()
    scatter.end()
    swap.arrived(0)
    swap.arrived(1)
    swap.end()


def back_call(ins):
    outs = [
        shape(ROWS, WIDTH, kind=F32), shape(ROWS, WIDTH, kind=F32), shape(CTX + QKV, LANES), shape(WIDTH, LANES),
    ]
    return call(
        back_kernel,
        4,
        ins,
        [IN_VMEM] * 12 + [ANYWHERE] * 2,
        outs,
        [ANYWHERE] * 2 + [IN_VMEM] * 2,
        [
            *gather_scratch(), pltpu.VMEM((2, GROUP, GROUP), BF), pltpu.VMEM((2, GROUP, HEAD), F32),
            pltpu.VMEM((2, GROUP, HEAD), F32), pltpu.VMEM((GROUP, QKV), BF), pltpu.VMEM((ROWS, WIDTH), F32),
            *scatter_scratch(), *swap_marks(2), pltpu.SemaphoreType.DMA((5,)),
        ],
    )


SHARD_ROWS = 2 * UNITS + CTX + QKV
SHARD_SLICE = SHARD_ROWS // 16
WHOLE_ROWS = 4 * WIDTH
WHOLE_HALF = WHOLE_ROWS // 2
WHOLE_SLICE = WHOLE_HALF // 16
WHOLE_BIT = WHOLE_SLICE // 4


def reduce_kernel(
    by_shard, whole,
    shard_out, whole_out,
    shard_in, shard_sum, whole_sib, whole_here, whole_in, slice_sum, bit_in, bit_sum, shard_all, whole_all,
    a_send, a_recv, b_send, b_recv, c_send, c_recv, d_send, d_recv, e_send, e_recv,
    f_send, f_recv, g_send, g_recv, out_sem,
):
    p = Place()
    m = p.z * 4 + p.x

    def member(k):
        other = lax.rem(m + k, 16)
        return other, p.at(z=lax.div(other, 4), x=lax.rem(other, 4))

    mates = []
    for k in range(1, 16):
        other = lax.rem(m + k, 16)
        for core in (0, 1):
            mates.append(p.at(z=lax.div(other, 4), x=lax.rem(other, 4), c=core))
    rings = [p.at(y=lax.rem(p.y + dy, 4)) for dy in (1, 2, 3)]
    greet([p.sib] + mates + rings)
    there = rows_at((1 - p.c) * WHOLE_HALF, WHOLE_HALF)
    sib_copy = remote(whole.at[there], whole_sib, f_send.at[0], f_recv.at[0], p.sib)
    sib_copy.start()
    shard_copies = []
    for k in range(1, 16):
        other, device = member(k)
        copy = remote(
            by_shard.at[rows_at(other * SHARD_SLICE, SHARD_SLICE)], shard_in.at[k], a_send.at[k], a_recv.at[k], device
        )
        copy.start()
        shard_copies.append(copy)
    sib_copy.wait_recv()

    def sum_half(index):
        at = rows_at(index * 256, 256)
        whole_here[at, :] = (
            whole[rows_at(p.c * WHOLE_HALF + index * 256, 256), :].astype(F32) + whole_sib[at, :].astype(F32)
        ).astype(BF)

    loop(WHOLE_HALF // 256, sum_half)
    whole_copies = []
    for k in range(1, 16):
        other, device = member(k)
        copy = remote(
            whole_here.at[rows_at(other * WHOLE_SLICE, WHOLE_SLICE)], whole_in.at[k], b_send.at[k], b_recv.at[k], device
        )
        copy.start()
        whole_copies.append(copy)
    total = by_shard[rows_at(m * SHARD_SLICE, SHARD_SLICE), :].astype(F32)
    for k in range(1, 16):
        shard_copies[k - 1].wait_recv()
        total = total + shard_in[k].astype(F32)
    shard_sum[...] = total.astype(BF)
    spread = []
    mine = shard_all.at[rows_at(m * SHARD_SLICE, SHARD_SLICE)]
    for dz in range(4):
        for dx in range(2):
            for dc in range(2):
                n = (dz * 2 + dx) * 2 + dc
                device = p.at(
                    z=lax.rem(p.z + dz, 4), xl=lax.rem(p.xl + dx, 2), g=p.c, c=lax.rem(p.c + dc, 2)
                )
                copy = remote(shard_sum, mine, c_send.at[n], c_recv.at[m], device)
                if n == 0:
                    pl.when(p.away)(copy.start)
                    pl.when(p.home)(pltpu.make_async_copy(shard_sum, mine, c_recv.at[m]).start)
                else:
                    copy.start()
                spread.append(copy)
    total = whole_here[rows_at(m * WHOLE_SLICE, WHOLE_SLICE), :].astype(F32)
    for k in range(1, 16):
        whole_copies[k - 1].wait_recv()
        total = total + whole_in[k].astype(F32)
    slice_sum[...] = total.astype(BF)
    bits = []
    for dy in (1, 2, 3):
        other = lax.rem(p.y + dy, 4)
        copy = remote(
            slice_sum.at[rows_at(other * WHOLE_BIT, WHOLE_BIT)], bit_in.at[dy], d_send.at[dy], d_recv.at[dy], rings[dy - 1]
        )
        copy.start()
        bits.append(copy)
    total = slice_sum[rows_at(p.y * WHOLE_BIT, WHOLE_BIT), :].astype(F32)
    for dy in (1, 2, 3):
        bits[dy - 1].wait_recv()
        total = total + bit_in[dy].astype(F32)
    bit_sum[...] = total.astype(BF)
    base = p.c * WHOLE_HALF + m * WHOLE_SLICE
    own_bit = whole_all.at[rows_at(base + p.y * WHOLE_BIT, WHOLE_BIT)]
    place_bit = pltpu.make_async_copy(bit_sum, own_bit, out_sem.at[0])
    place_bit.start()
    bits_back = []
    for dy in (1, 2, 3):
        copy = remote(bit_sum, own_bit, e_send.at[dy], e_recv.at[dy], rings[dy - 1])
        copy.start()
        bits_back.append(copy)
    place_bit.wait()
    for dy in (1, 2, 3):
        source = lax.rem(p.y + 4 - dy, 4)
        landing = whole_all.at[rows_at(base + source * WHOLE_BIT, WHOLE_BIT)]
        remote(bit_sum, landing, e_send.at[dy], e_recv.at[dy], rings[dy - 1]).wait_recv()
    own_slice = whole_all.at[rows_at(base, WHOLE_SLICE)]
    slices_back = []
    for k in range(1, 16):
        _, device = member(k)
        copy = remote(own_slice, own_slice, g_send.at[k], g_recv.at[k], device)
        copy.start()
        slices_back.append(copy)
    for k in range(1, 16):
        source = lax.rem(m + 16 - k, 16)
        landing = whole_all.at[rows_at(p.c * WHOLE_HALF + source * WHOLE_SLICE, WHOLE_SLICE)]
        remote(landing, landing, g_send.at[k], g_recv.at[k], p.sib).wait_recv()
    half = whole_all.at[rows_at(p.c * WHOLE_HALF, WHOLE_HALF)]
    half_copy = remote(half, half, f_send.at[1], f_recv.at[1], p.sib)
    half_copy.start()
    for index in range(16):
        landing = shard_all.at[pl.ds(index * SHARD_SLICE, SHARD_SLICE)]
        remote(shard_sum, landing, c_send.at[0], c_recv.at[index], p.sib).wait_recv()
    shard_out[...] = shard_all[...].astype(F32)
    other_half = whole_all.at[there]
    remote(other_half, other_half, f_send.at[1], f_recv.at[1], p.sib).wait_recv()
    whole_out[...] = whole_all[...].astype(F32)
    for copy in [sib_copy, half_copy] + shard_copies + whole_copies + bits + bits_back + slices_back + spread[1:]:
        copy.wait_send()
    pl.when(p.away)(spread[0].wait_send)


def reduce_call(ins):
    dma = pltpu.SemaphoreType.DMA
    return call(
        reduce_kernel,
        5,
        ins,
        [IN_VMEM] * 2,
        [shape(SHARD_ROWS, LANES, kind=F32), shape(WHOLE_ROWS, LANES, kind=F32)],
        [IN_VMEM] * 2,
        [
            pltpu.VMEM((16, SHARD_SLICE, LANES), BF), pltpu.VMEM((SHARD_SLICE, LANES), BF),
            pltpu.VMEM((WHOLE_HALF, LANES), BF), pltpu.VMEM((WHOLE_HALF, LANES), BF),
            pltpu.VMEM((16, WHOLE_SLICE, LANES), BF), pltpu.VMEM((WHOLE_SLICE, LANES), BF),
            pltpu.VMEM((4, WHOLE_BIT, LANES), BF), pltpu.VMEM((WHOLE_BIT, LANES), BF),
            pltpu.VMEM((SHARD_ROWS, LANES), BF), pltpu.VMEM((WHOLE_ROWS, LANES), BF),
            dma((16,)), dma((16,)), dma((16,)), dma((16,)), dma((16,)), dma((16,)), dma((4,)), dma((4,)),
            dma((4,)), dma((4,)), dma((2,)), dma((2,)), dma((16,)), dma((16,)), dma((1,)),
        ],
    )


def row_layout(lengths, order, sequence_adapter):
    ends = jnp.cumsum(lengths)
    starts = ends - lengths
    slot = jnp.sum((order[:, None] >= ends[None, :]).astype(jnp.int32), axis=1)
    member = slot[:, None] == jnp.arange(lengths.shape[0], dtype=jnp.int32)[None, :]
    start = jnp.sum(jnp.where(member, starts[None, :], 0), axis=1)
    adapter = jnp.sum(jnp.where(member, sequence_adapter[None, :], 0), axis=1)
    return start, adapter


def shards(
    tokens, lengths, order, sequence_adapter, first_norm_gain, first_norm_bias, second_norm_gain, second_norm_bias,
    joined_matrix, joined_offset_bias, output_matrix, output_offset_bias, up_matrix, up_offset_bias, down_matrix,
    down_offset_bias, joined_adapter_reduce, joined_adapter_expand, output_adapter_reduce, output_adapter_expand,
    up_adapter_reduce, up_adapter_expand, down_adapter_reduce, down_adapter_expand, cotangent,
):
    start, adapter = row_layout(lengths[0], order[0], sequence_adapter[0])
    own = lax.dynamic_slice_in_dim(adapter, lax.axis_index("tensor") * ROWS, ROWS, 0)
    columns = jnp.arange(LANES, dtype=jnp.int32) // 16
    mask = (columns[None, :] == own[:, None]).astype(BF)
    aux = jnp.concatenate([joined_offset_bias[0], up_offset_bias[0], order[0].astype(F32), start.astype(F32)])
    aux = jnp.broadcast_to(aux[None, :], (8, AUX_ALL))
    half = jnp.asarray(SCALE, BF)
    (
        qkv, side_q, normed_first, gathered_grad, joined_full, output_full, tokens_own, cot_own, mask_own, aux_own,
        up_expand_own, down_reduce_own,
    ) = project_call(
        (
            tokens, cotangent, first_norm_gain, first_norm_bias, joined_adapter_reduce[0], down_adapter_expand[0], mask,
            joined_adapter_expand[0] * half, aux, joined_matrix[0], output_matrix[0], output_adapter_reduce[0],
            up_adapter_expand[0] * half, down_adapter_reduce[0],
        )
    )
    info = jnp.pad(
        jnp.stack([aux_own[0, AUX_TOKEN:AUX_START], aux_own[0, AUX_START:]], axis=1), ((0, 0), (0, LANES - 2))
    )
    normed, middle, side_o, context, probs, up_full = attend_call(
        (
            qkv, aux_own, info, output_full, tokens_own, mask_own, output_adapter_expand[0], output_offset_bias,
            second_norm_gain, second_norm_bias, up_adapter_reduce[0], up_matrix[0], up_expand_own,
        )
    )
    block_own, grad, grad_stage, shard_feed, whole_feed = feed_call(
        (
            normed, middle, side_o, gathered_grad, up_full, aux_own, mask_own, cot_own, down_offset_bias,
            second_norm_gain, up_adapter_reduce[0], output_adapter_expand[0], down_adapter_expand[0], down_matrix[0],
            down_reduce_own,
        )
    )
    block_out, input_grad, shard_back, whole_back = back_call(
        (
            grad_stage, output_full, qkv, context, joined_full, side_q, tokens_own, first_norm_gain, mask_own, grad,
            joined_adapter_reduce[0], normed_first, block_own, probs,
        )
    )
    by_shard = jnp.concatenate([shard_feed, shard_back])
    whole = jnp.concatenate([whole_feed, whole_back])
    by_shard, whole = reduce_call((by_shard, whole))
    down_a, up_b, out_a, joined_b = jnp.split(by_shard, [UNITS, 2 * UNITS, 2 * UNITS + CTX])
    up_a, out_b, down_b, joined_a = jnp.split(whole, 4)
    return (
        block_out, input_grad, joined_a[None], joined_b.T[None], out_a[None], out_b.T[None], up_a[None], up_b.T[None],
        down_a[None], down_b.T[None],
    )


def solution(mesh):
    spread = P(("dp", "tensor"), None)
    by_dp = P("dp", None)
    rows = P(None, "dp", "tensor")
    cols = P(None, "tensor", "dp")
    last = P(None, None, "tensor")
    middle = P(None, "tensor", None)
    vector = P(None, "tensor")
    return jax.shard_map(
        shards,
        mesh=mesh,
        in_specs=(
            spread, by_dp, by_dp, by_dp, P(), P(), P(), P(), rows, vector, cols, P(), rows, vector, cols, P(),
            P(), last, middle, P(), P(), last, middle, P(), spread,
        ),
        out_specs=(spread, spread, P(), last, middle, P(), P(), last, middle, P()),
        check_vma=False,
    )
```

```python
import functools
import math

import jax
import jax.numpy as jnp
from jax import lax
from jax.experimental import pallas as pl
from jax.experimental.pallas import tpu as pltpu
from jax.sharding import PartitionSpec as P

HEAD = 128
WIDTH = 2048
LANES = 128
WIDE = WIDTH + LANES
ROWS = 160
HALF = ROWS // 2
PAIR = 2 * ROWS
GROUP = 8 * ROWS
QKV = 768
UNITS = 1024
CTX = 256
BLOCK = 32
SCALE = 0.5
EPS = 1e-05
MASKED = -1e30
LOG2E = 1.4426950408889634
VMEM_LIMIT = 60 * 2**20
BF = jnp.bfloat16
F32 = jnp.float32
BY_MESH = pl.DeviceIdType.MESH
ANYWHERE = pl.BlockSpec(memory_space=pl.ANY)
IN_VMEM = pl.BlockSpec(memory_space=pltpu.VMEM)
IN_SMEM = pl.BlockSpec(memory_space=pltpu.SMEM)


def nn(left, right):
    return jnp.dot(left, right, preferred_element_type=F32)


def nt(left, right):
    return lax.dot_general(left, right, (((1,), (1,)), ((), ())), preferred_element_type=F32)


def tn(left, right):
    return lax.dot_general(left, right, (((0,), (0,)), ((), ())), preferred_element_type=F32)


def rows_at(start, size):
    return pl.ds(pl.multiple_of(start, 16), size)


def lanes_at(start, size):
    return pl.ds(pl.multiple_of(start, 128), size)


def loop(count, body):
    def step(index, carry):
        body(index)
        return carry

    lax.fori_loop(0, count, step, 0)


class Place:
    def __init__(self):
        dp = lax.axis_index("dp")
        tensor = lax.axis_index("tensor")
        self.dp = dp
        self.z = lax.div(dp, 4)
        self.xl = lax.rem(lax.div(dp, 2), 2)
        self.c = lax.rem(dp, 2)
        self.y = lax.div(tensor, 2)
        self.g = lax.rem(tensor, 2)
        self.x = self.g * 2 + self.xl
        self.sib = self.at(c=1 - self.c)
        self.up = self.at(y=lax.rem(self.y + 1, 4))
        self.down = self.at(y=lax.rem(self.y + 3, 4))
        self.z_up = self.at(z=lax.rem(self.z + 1, 4))
        self.z_down = self.at(z=lax.rem(self.z + 3, 4))
        self.partner = self.at(g=self.c, c=self.g)
        self.home = self.c == self.g
        self.away = self.c != self.g

    def at(self, z=None, x=None, xl=None, c=None, y=None, g=None):
        z = self.z if z is None else z
        c = self.c if c is None else c
        y = self.y if y is None else y
        if x is None:
            xl = self.xl if xl is None else xl
            g = self.g if g is None else g
        else:
            xl = lax.rem(x, 2)
            g = lax.div(x, 2)
        return (z * 4 + xl * 2 + c, y * 2 + g)

    def in_row(self, dx, core):
        return self.at(x=lax.rem(self.x + dx, 4), c=core)

    def row_mates(self):
        return [self.in_row(dx, core) for dx in (1, 2, 3) for core in (0, 1)]

    def column_mates(self):
        return [self.at(z=lax.rem(self.z + dz, 4), c=core) for dz in (1, 2, 3) for core in (0, 1)]

    def ring(self, dy, same):
        return lax.rem(self.y + dy + 4, 4) * 2 + (self.c if same else 1 - self.c)


def greet(devices):
    barrier = pltpu.get_barrier_semaphore()
    for device in devices:
        pl.semaphore_signal(barrier, 1, device_id=device, device_id_type=BY_MESH)
    pl.semaphore_wait(barrier, len(devices))


def remote(src, dst, send, recv, device):
    return pltpu.make_async_remote_copy(
        src_ref=src, dst_ref=dst, send_sem=send, recv_sem=recv, device_id=device, device_id_type=BY_MESH
    )


class Gather:
    SENDS = (
        (0, True, None),
        (0, True, None),
        (0, True, None),
        (-1, True, 0),
        (1, True, 1),
        (-1, True, None),
        (1, True, None),
        (2, True, 0),
        (2, True, 1),
    )
    LANDS = (
        (0, False, None),
        (-1, True, None),
        (1, True, None),
        (2, True, 0),
        (2, True, 1),
        (-1, False, None),
        (1, False, None),
        (2, False, 0),
        (2, False, 1),
    )

    def __init__(self, place, buf, send, recv):
        self.place, self.buf, self.send, self.recv = place, buf, send, recv
        p = place
        self.to = (p.sib, p.up, p.down, p.up, p.down, p.sib, p.sib, p.sib, p.sib)

    def piece(self, what):
        dy, same, half = what
        start = self.place.ring(dy, same) * ROWS
        if half is None:
            return self.buf.at[rows_at(start, ROWS)]
        return self.buf.at[rows_at(start + half * HALF, HALF)]

    def copy(self, i):
        piece = self.piece(self.SENDS[i])
        return remote(piece, piece, self.send.at[i], self.recv.at[i], self.to[i])

    def landed(self, i):
        piece = self.piece(self.LANDS[i])
        remote(piece, piece, self.send.at[i], self.recv.at[i], self.to[i]).wait_recv()

    def begin(self):
        for i in (1, 2, 0):
            self.copy(i).start()

    def near(self):
        self.landed(1)
        self.copy(3).start()
        self.copy(5).start()
        self.landed(2)
        self.copy(4).start()
        self.copy(6).start()

    def far(self):
        self.landed(3)
        self.copy(7).start()
        self.landed(4)
        self.copy(8).start()

    def own_pair(self):
        self.landed(0)

    def near_pairs(self):
        self.landed(5)
        self.landed(6)

    def far_pair(self):
        self.landed(7)
        self.landed(8)

    def end(self):
        for i in range(9):
            self.copy(i).wait_send()


class Scatter:
    def __init__(self, place, part, sib_in, relay, near, send, recv, start=None):
        self.place, self.part, self.sib_in, self.relay, self.near = place, part, sib_in, relay, near
        self.send, self.recv = send, recv
        self.start = start or (lambda dy: place.ring(dy, True) * ROWS)

    def mine(self, dy, half=None):
        start = self.start(dy)
        if half is None:
            return self.part.at[rows_at(start, ROWS)]
        return self.part.at[rows_at(start + half * HALF, HALF)]

    def others(self, dy):
        return self.part.at[rows_at(self.place.ring(dy, False) * ROWS, ROWS)]

    def copy(self, i):
        p = self.place
        if i < 4:
            src, dst, to = self.others(i), self.sib_in.at[i], p.sib
        elif i == 4:
            src, dst, to = self.mine(2, 0), self.relay.at[0], p.up
        elif i == 5:
            src, dst, to = self.mine(2, 1), self.relay.at[1], p.down
        elif i == 6:
            src, dst, to = self.mine(1, 1), self.near.at[0, pl.ds(HALF, HALF)], p.up
        elif i == 7:
            src, dst, to = self.mine(-1, 0), self.near.at[1, pl.ds(0, HALF)], p.down
        elif i == 8:
            src, dst, to = self.mine(1, 0), self.near.at[0, pl.ds(0, HALF)], p.up
        else:
            src, dst, to = self.mine(-1, 1), self.near.at[1, pl.ds(HALF, HALF)], p.down
        return remote(src, dst, self.send.at[i], self.recv.at[i], to)

    def exchange(self, dy):
        self.copy(dy % 4).start()

    def combine(self, dy):
        self.copy(dy % 4).wait_recv()
        add_rows(self.part, self.start(dy), self.sib_in.at[dy % 4], 0, ROWS)

    def relay_out(self):
        self.copy(4).start()
        self.copy(5).start()

    def near_free(self, dy):
        self.copy(6 if dy == 1 else 7).start()

    def near_rest(self):
        self.copy(4).wait_recv()
        add_rows(self.part, self.start(1), self.relay.at[0], 0, HALF)
        self.copy(8).start()
        self.copy(5).wait_recv()
        add_rows(self.part, self.start(-1) + HALF, self.relay.at[1], 0, HALF)
        self.copy(9).start()

    def arrived(self):
        for i in (6, 7, 8, 9):
            self.copy(i).wait_recv()

    def total(self, start, size, lanes):
        own = self.part[rows_at(self.start(0) + start, size), lanes].astype(F32)
        return (
            own
            + self.near[0, rows_at(start, size), lanes].astype(F32)
            + self.near[1, rows_at(start, size), lanes].astype(F32)
        )

    def end(self, first=0):
        for i in range(first, 10):
            self.copy(i).wait_send()


def scatter_scratch():
    return [
        pltpu.VMEM((GROUP, WIDE), BF),
        pltpu.VMEM((4, ROWS, WIDE), BF),
        pltpu.VMEM((2, HALF, WIDE), BF),
        pltpu.VMEM((2, ROWS, WIDE), BF),
        pltpu.SemaphoreType.DMA((10,)),
        pltpu.SemaphoreType.DMA((10,)),
    ]


def gather_scratch():
    return [pltpu.VMEM((GROUP, WIDE), BF), pltpu.SemaphoreType.DMA((9,)), pltpu.SemaphoreType.DMA((9,))]


def add_rows(dst, start, src, src_start, count):
    def body(index):
        at = rows_at(start + index * 16, 16)
        dst[at, :] = (dst[at, :].astype(F32) + src[rows_at(src_start + index * 16, 16), :].astype(F32)).astype(BF)

    loop(count // 16, body)


class Weights:
    def __init__(self, place, piece, full, by_rows, cut, send, recv):
        self.place, self.piece, self.full, self.by_rows = place, piece, full, by_rows
        self.send, self.recv = send, recv
        size = piece.shape[1] if by_rows else piece.shape[0]
        self.parts = (pl.ds(0, cut), pl.ds(cut, size - cut))

    def source(self, half):
        part = self.parts[half]
        return self.piece.at[:, part] if self.by_rows else self.piece.at[part, :]

    def slot(self, index, count, half):
        span = lanes_at(index * 128, count * 128)
        part = self.parts[half]
        return self.full.at[span, part] if self.by_rows else self.full.at[part, span]

    def column(self, dz):
        return lax.rem(self.place.z + dz, 4)

    def first(self):
        p = self.place
        marks = (self.recv.at[p.xl * 2 + p.c], self.recv.at[4 + p.z * 2 + p.c])
        slots = (self.slot(p.dp, 1, 0), self.slot(p.dp, 1, 1))
        for d in (2, 1, 3):
            remote(self.source(0), slots[0], self.send.at[d], marks[0], p.in_row(d, p.g)).start()
            remote(self.source(1), slots[1], self.send.at[4 + d], marks[1], p.at(z=self.column(d), c=p.g)).start()

        @pl.when(p.home)
        def _():
            for half in range(2):
                pltpu.make_async_copy(self.source(half), slots[half], marks[half]).start()

        @pl.when(p.away)
        def _():
            for half in range(2):
                remote(self.source(half), slots[half], self.send.at[4 * half], marks[half], p.sib).start()

    def landed(self, slot, mark):
        remote(slot, slot, self.send.at[0], self.recv.at[mark], self.place.sib).wait_recv()

    def along_z(self, dz):
        block = self.slot(self.place.z * 4, 4, 0)
        return remote(block, block, self.send.at[7 + dz], self.recv.at[11 + dz], self.place.at(z=self.column(dz)))

    def along_x(self, dz, dx):
        p = self.place
        z = self.column(dz)
        pair = self.slot(z * 4 + p.xl * 2, 2, 1)
        return remote(
            pair, pair, self.send.at[10 + dz * 3 + dx], self.recv.at[15 + p.xl * 4 + z], p.in_row(dx, p.c)
        )

    def second(self):
        p = self.place
        for index in range(4):
            self.landed(self.slot(p.z * 4 + index, 1, 0), index)
        for dz in (2, 1, 3):
            self.along_z(dz).start()

        @pl.when(p.home)
        def _():
            for dz in range(4):
                z = self.column(dz)
                for core in range(2):
                    self.landed(self.slot(z * 4 + p.xl * 2 + core, 1, 1), 4 + z * 2 + core)
                for dx in (2, 1, 3):
                    self.along_x(dz, dx).start()

    def arrived(self):
        p = self.place
        for dz in range(1, 4):
            self.landed(self.slot(self.column(4 - dz) * 4, 4, 0), 11 + dz)
        for z in range(4):
            self.landed(self.slot(z * 4 + (1 - p.xl) * 2, 2, 1), 15 + (1 - p.xl) * 4 + z)

        @pl.when(p.away)
        def _():
            for z in range(4):
                self.landed(self.slot(z * 4 + p.xl * 2, 2, 1), 15 + p.xl * 4 + z)

    def end(self):
        p = self.place
        for d in (1, 2, 3):
            for half in range(2):
                slot = self.slot(p.dp, 1, half)
                remote(self.source(half), slot, self.send.at[4 * half + d], self.recv.at[0], p.sib).wait_send()
            self.along_z(d).wait_send()

        @pl.when(p.away)
        def _():
            for half in range(2):
                slot = self.slot(p.dp, 1, half)
                remote(self.source(half), slot, self.send.at[4 * half], self.recv.at[0], p.sib).wait_send()

        @pl.when(p.home)
        def _():
            for dz in range(4):
                for dx in (1, 2, 3):
                    self.along_x(dz, dx).wait_send()


def weight_marks():
    return [pltpu.SemaphoreType.DMA((23,)), pltpu.SemaphoreType.DMA((23,))]


class Swap:
    def __init__(self, place, pairs, send, recv):
        self.place, self.pairs, self.send, self.recv = place, pairs, send, recv

    def begin(self, i):
        src, dst = self.pairs[i]
        p = self.place

        @pl.when(p.home)
        def _():
            pltpu.make_async_copy(src, dst, self.recv.at[i]).start()

        @pl.when(p.away)
        def _():
            remote(src, dst, self.send.at[i], self.recv.at[i], p.partner).start()

    def arrived(self, i):
        src, dst = self.pairs[i]
        remote(src, dst, self.send.at[i], self.recv.at[i], self.place.sib).wait_recv()

    def end(self):
        @pl.when(self.place.away)
        def _():
            for i, (src, dst) in enumerate(self.pairs):
                remote(src, dst, self.send.at[i], self.recv.at[i], self.place.sib).wait_send()


def swap_marks(count):
    return [pltpu.SemaphoreType.DMA((count,)), pltpu.SemaphoreType.DMA((count,))]


def normalise(value):
    mean = jnp.mean(value, axis=-1, keepdims=True)
    center = value - mean
    inverse = lax.rsqrt(jnp.mean(center * center, axis=-1, keepdims=True) + EPS)
    return center * inverse, inverse


def norm_back(value, gain, grad):
    normed, inverse = normalise(value)
    e = grad * gain
    return (e - jnp.mean(e, axis=-1, keepdims=True) - normed * jnp.mean(e * normed, axis=-1, keepdims=True)) * inverse


def pair_rows(place, dy):
    return rows_at(lax.rem(place.y + dy + 4, 4) * PAIR, PAIR)


def wide_product(put, make):
    loop(4, lambda j: put(lanes_at(j * 512, 512), make(lanes_at(j * 512, 512))))
    put(pl.ds(WIDTH, LANES), make(pl.ds(WIDTH, LANES)))


def call(kernel, collective, ins, specs, outs, out_specs, scratch):
    return pl.pallas_call(
        kernel,
        name=kernel.__name__,
        out_shape=outs,
        in_specs=specs,
        out_specs=out_specs,
        scratch_shapes=scratch,
        compiler_params=pltpu.CompilerParams(
            collective_id=collective, has_side_effects=True, vmem_limit_bytes=VMEM_LIMIT
        ),
    )(*ins)


def shape(*dims, kind=BF):
    return jax.ShapeDtypeStruct(dims, kind)


def identity():
    row = lax.broadcasted_iota(jnp.int32, (LANES, LANES), 0)
    return jnp.where(row == lax.broadcasted_iota(jnp.int32, (LANES, LANES), 1), 1.0, 0.0).astype(BF)


def query_info(token_row, start_row):
    token_high = jnp.floor(token_row * (1.0 / 16.0))
    start_high = jnp.floor(start_row * (1.0 / 16.0))
    digit = lax.broadcasted_iota(jnp.int32, (16, GROUP), 0)
    digits = jnp.where(digit == 0, token_high, 0.0)
    digits = jnp.where(digit == 1, token_row - 16.0 * token_high, digits)
    digits = jnp.where(digit == 2, start_high, digits)
    digits = jnp.where(digit == 3, start_row - 16.0 * start_high, digits)
    row = lax.broadcasted_iota(jnp.int32, (16, LANES), 0)
    lane = lax.broadcasted_iota(jnp.int32, (16, LANES), 1)
    worth = jnp.where((row == 0) & (lane == 0) | (row == 2) & (lane == 1), 16.0, 0.0)
    worth = worth + jnp.where((row == 1) & (lane == 0) | (row == 3) & (lane == 1), 1.0, 0.0)
    return tn(digits.astype(BF), worth.astype(BF))


def slope_row(place, head, tokens_row):
    number = (place.ring(0, True) * 2 + head + 1).astype(F32)
    slope = jnp.exp2(jnp.full((1, GROUP), -0.5, F32) * number)
    return slope * LOG2E * tokens_row


def forward_kernel(
    gain, shift, joined_reduce, down_expand, joined_expand, joined_shift, order, output_expand, output_shift,
    second_gain, second_shift, up_reduce, lengths, adapters,
    tokens, cotangent, up_shift, joined_piece, output_piece, output_reduce, up_piece, up_expand, down_piece, down_reduce,
    normed, middle, side_o, context, qkv, mask_own,
    probs_out, side_q, normed_own, gathered_grad, cot_own, joined_full, output_full, up_full, down_full, tokens_own,
    up_shift_own,
    tok_here, aux, aux_here, half_expand, shift_here, joined_here, output_here, info, mask_all, probs,
    rows, rows_send, rows_recv, grads, grads_send, grads_recv, part, sib_in, relay, near, s_send, s_recv,
    w_send, w_recv, o_send, o_recv, u_send, u_recv, d_send, d_recv, swap_send, swap_recv, out_sem, probs_sem,
):
    p = Place()
    greet([p.sib, p.up, p.down] + p.row_mates() + p.column_mates())
    joined = Weights(p, joined_piece, joined_here.at[pl.ds(0, WIDTH)], True, 512, w_send, w_recv)
    output = Weights(p, output_piece, output_here.at[:, pl.ds(0, WIDTH)], False, 128, o_send, o_recv)
    up = Weights(p, up_piece, up_full.at[pl.ds(0, WIDTH)], True, 640, u_send, u_recv)
    down = Weights(p, down_piece, down_full.at[:, pl.ds(0, WIDTH)], False, 512, d_send, d_recv)
    own_rows = rows_at(p.ring(0, True) * ROWS, ROWS)
    their_rows = rows_at((p.y * 2 + p.g) * ROWS, ROWS)
    swap = Swap(
        p,
        [
            (tokens, tok_here),
            (aux, aux_here),
            (half_expand, joined_here.at[pl.ds(WIDTH, LANES)]),
            (joined_shift, shift_here),
            (cotangent, grads.at[their_rows, pl.ds(0, WIDTH)]),
            (output_reduce, output_here.at[:, pl.ds(WIDTH, LANES)]),
            (up_expand, up_full.at[pl.ds(WIDTH, LANES)]),
            (down_reduce, down_full.at[:, pl.ds(WIDTH, LANES)]),
            (up_shift, up_shift_own),
        ],
        swap_send,
        swap_recv,
    )
    swap.begin(0)
    joined.first()
    token = order[...]
    first_end = lengths[0, 0]
    second_end = first_end + lengths[0, 1]
    later = token >= second_end
    late = token >= first_end
    start = jnp.where(later, second_end, jnp.where(late, first_end, 0))
    adapter = jnp.where(later, adapters[0, 2], jnp.where(late, adapters[0, 1], adapters[0, 0]))
    for i, row in enumerate((token, start, adapter)):
        aux[:, pl.ds(i * GROUP, GROUP)] = jnp.broadcast_to(row.astype(F32), (8, GROUP))
    half_expand[...] = (SCALE * joined_expand[...].astype(F32)).astype(BF)
    for i in (1, 2, 3, 4):
        swap.begin(i)
    swap.arrived(1)
    token_row = aux_here[0:1, pl.ds(0, GROUP)]
    info[...] = query_info(token_row, aux_here[0:1, pl.ds(GROUP, GROUP)])
    column = lax.shift_right_logical(lax.broadcasted_iota(jnp.int32, (LANES, GROUP), 0), 4).astype(F32)
    chosen = jnp.where(column == aux_here[0:1, pl.ds(2 * GROUP, GROUP)], 1.0, 0.0).astype(BF)
    mask_all[...] = tn(chosen, identity()).astype(BF)
    mask_own[...] = mask_all[own_rows, :]
    mask_rows = mask_all[own_rows, :].astype(F32)
    joined.second()
    swap.arrived(0)

    def norm_block(index):
        at = rows_at(index * BLOCK, BLOCK)
        value, _ = normalise(tok_here[at, :].astype(F32))
        rows[rows_at(p.ring(0, True) * ROWS + index * BLOCK, BLOCK), pl.ds(0, WIDTH)] = (
            value * gain[...] + shift[...]
        ).astype(BF)

    loop(ROWS // BLOCK, norm_block)
    rows[own_rows, pl.ds(WIDTH, LANES)] = (
        mask_rows * nn(rows[own_rows, pl.ds(0, WIDTH)], joined_reduce[...])
    ).astype(BF)
    gather = Gather(p, rows, rows_send, rows_recv)
    gather_grad = Gather(p, grads, grads_send, grads_recv)
    gather.begin()
    output.first()
    up.first()
    for i in range(5, 9):
        swap.begin(i)
    swap.arrived(4)
    grads[own_rows, pl.ds(WIDTH, LANES)] = (
        mask_rows * (SCALE * nt(grads[own_rows, pl.ds(0, WIDTH)], down_expand[...]))
    ).astype(BF)
    copies = [
        pltpu.make_async_copy(tok_here, tokens_own, out_sem.at[0]),
        pltpu.make_async_copy(grads.at[own_rows, pl.ds(0, WIDTH)], cot_own, out_sem.at[1]),
        pltpu.make_async_copy(rows.at[own_rows, pl.ds(0, WIDTH)], normed_own, out_sem.at[2]),
    ]
    for copy in copies:
        copy.start()
    gather.near()
    gather_grad.begin()
    output.second()
    up.second()
    down.first()
    swap.arrived(2)
    swap.arrived(3)
    joined.arrived()
    copies.append(pltpu.make_async_copy(joined_here, joined_full, out_sem.at[3]))
    copies[-1].start()

    def project(dy):
        at = pair_rows(p, dy)

        def body(j):
            lanes = lanes_at(j * 256, 256)
            qkv[at, lanes] = (nn(rows[at, :], joined_here[:, lanes]) + shift_here[:, lanes]).astype(BF)

        loop(QKV // 256, body)

    gather.own_pair()
    project(0)
    gather.near_pairs()
    project(1)
    project(-1)
    gather.far()
    gather.far_pair()
    project(2)
    copies.append(pltpu.make_async_copy(rows.at[:, pl.ds(WIDTH, LANES)], side_q, out_sem.at[4]))
    copies[-1].start()
    output.arrived()
    swap.arrived(5)
    copies.append(pltpu.make_async_copy(output_here, output_full, out_sem.at[5]))
    copies[-1].start()
    probs_copies = []

    def attend(dy, same):
        at = rows_at(p.ring(dy, same) * ROWS, ROWS)
        n = len(probs_copies)
        if n >= 2:
            probs_copies[n - 2].wait()
        query_token = info[at, 0:1]
        query_start = info[at, 1:2]
        allowed = (token_row <= query_token) & (token_row >= query_start)
        for head in range(2):
            first = head * 3 * HEAD
            scores = nt(qkv[at, first : first + HEAD], qkv[:, first + HEAD : first + 2 * HEAD])
            scores = scores * (LOG2E / math.sqrt(HEAD)) + slope_row(p, head, token_row)
            scores = jnp.where(allowed, scores, MASKED)
            top = jnp.max(scores, axis=-1, keepdims=True)
            weights = jnp.exp2(scores - top)
            total = jnp.sum(weights, axis=-1, keepdims=True)
            weights = (weights * (1.0 / total)).astype(BF)
            probs[n % 2, head] = weights
            context[at, head * HEAD : (head + 1) * HEAD] = nn(
                weights, qkv[:, first + 2 * HEAD : first + 3 * HEAD]
            ).astype(BF)
        copy = pltpu.make_async_copy(probs.at[n % 2], probs_out.at[:, at], probs_sem.at[n])
        copy.start()
        probs_copies.append(copy)

        def put(lanes, value):
            part[at, lanes] = value.astype(BF)

        wide_product(put, lambda lanes: nn(context[at, :], output_here[:, lanes]))

    scatter = Scatter(p, part, sib_in, relay, near, s_send, s_recv)
    attend(2, False)
    scatter.exchange(2)
    attend(2, True)
    scatter.combine(2)
    scatter.relay_out()
    gather_grad.near()
    down.second()
    attend(1, False)
    scatter.exchange(1)
    attend(1, True)
    scatter.combine(1)
    scatter.near_free(1)
    attend(-1, False)
    scatter.exchange(-1)
    attend(-1, True)
    scatter.combine(-1)
    scatter.near_free(-1)
    gather_grad.far()
    attend(0, False)
    scatter.exchange(0)
    scatter.near_rest()
    attend(0, True)
    scatter.combine(0)
    gather_grad.own_pair()
    gather_grad.near_pairs()
    gather_grad.far_pair()
    copies.append(pltpu.make_async_copy(grads, gathered_grad, out_sem.at[6]))
    copies[-1].start()
    scatter.arrived()
    side = (mask_rows * scatter.total(0, ROWS, pl.ds(WIDTH, LANES))).astype(BF)
    side_o[...] = side

    def add_tile(j):
        lanes = lanes_at(j * 512, 512)
        middle[:, lanes] = (
            tok_here[:, lanes].astype(F32)
            + scatter.total(0, ROWS, lanes)
            + output_shift[:, lanes]
            + SCALE * nn(side, output_expand[:, lanes])
        )

    loop(4, add_tile)

    def second_block(index):
        at = rows_at(index * BLOCK, BLOCK)
        value, _ = normalise(middle[at, :])
        normed[at, pl.ds(0, WIDTH)] = (value * second_gain[...] + second_shift[...]).astype(BF)

    loop(ROWS // BLOCK, second_block)
    normed[:, pl.ds(WIDTH, LANES)] = (mask_rows * nn(normed[:, pl.ds(0, WIDTH)], up_reduce[...])).astype(BF)
    up.arrived()
    down.arrived()
    for i in range(6, 9):
        swap.arrived(i)
    swap.end()
    for sender in (gather, gather_grad, scatter, joined, output, up, down):
        sender.end()
    for copy in copies + probs_copies[-2:]:
        copy.wait()


def forward_call(ins):
    outs = [
        shape(ROWS, WIDE), shape(ROWS, WIDTH, kind=F32), shape(ROWS, LANES), shape(GROUP, CTX), shape(GROUP, QKV),
        shape(ROWS, LANES),
        shape(2, GROUP, GROUP), shape(GROUP, LANES), shape(ROWS, WIDTH), shape(GROUP, WIDE), shape(ROWS, WIDTH),
        shape(WIDE, QKV), shape(CTX, WIDE), shape(WIDE, UNITS), shape(UNITS, WIDE), shape(ROWS, WIDTH),
        shape(1, UNITS, kind=F32),
    ]
    return call(
        forward_kernel,
        1,
        ins,
        [IN_VMEM] * 12 + [IN_SMEM] * 2 + [ANYWHERE] * 10,
        outs,
        [IN_VMEM] * 6 + [ANYWHERE] * 11,
        [
            pltpu.VMEM((ROWS, WIDTH), BF), pltpu.VMEM((8, 3 * GROUP), F32), pltpu.VMEM((8, 3 * GROUP), F32),
            pltpu.VMEM((LANES, QKV), BF), pltpu.VMEM((1, QKV), F32), pltpu.VMEM((WIDE, QKV), BF),
            pltpu.VMEM((CTX, WIDE), BF), pltpu.VMEM((GROUP, LANES), F32), pltpu.VMEM((GROUP, LANES), BF),
            pltpu.VMEM((2, 2, ROWS, GROUP), BF), *gather_scratch(), *gather_scratch(), *scatter_scratch(),
            *weight_marks(), *weight_marks(), *weight_marks(), *weight_marks(), *swap_marks(9),
            pltpu.SemaphoreType.DMA((7,)), pltpu.SemaphoreType.DMA((8,)),
        ],
    )


def feed_kernel(
    normed, middle, up_shift, mask, gain, up_reduce, output_expand,
    gathered_grad, up_weights, down_weights,
    grad_out, grad_stage, side_u, by_shard, out_parts,
    up_full, down_full, grads, rows, rows_send, rows_recv, act, slope, part, sib_in, relay, near, s_send, s_recv,
    part_out, sib_in_out, t_send, t_recv, own_sem,
):
    p = Place()
    own_rows = rows_at(p.ring(0, True) * ROWS, ROWS)
    stage = pltpu.make_async_copy(normed, rows.at[own_rows], own_sem.at[0])
    stage.start()
    load_down = pltpu.make_async_copy(down_weights, down_full, own_sem.at[1])
    load_down.start()
    load_grads = pltpu.make_async_copy(gathered_grad, grads, own_sem.at[2])
    load_grads.start()
    load_up = pltpu.make_async_copy(up_weights, up_full, own_sem.at[3])
    load_up.start()
    greet([p.sib, p.up, p.down])
    gather = Gather(p, rows, rows_send, rows_recv)
    stage.wait()
    gather.begin()

    def lift(dy):
        at = pair_rows(p, dy)

        def body(j):
            lanes = lanes_at(j * 256, 256)
            slope[at, lanes] = nt(grads[at, :], down_full[lanes, :]).astype(BF)

        loop(UNITS // 256, body)

    def hide(dy):
        at = pair_rows(p, dy)

        def body(j):
            lanes = lanes_at(j * 256, 256)
            v = nn(rows[at, :], up_full[:, lanes]) + up_shift[:, lanes]
            square = v * v
            t = jnp.tanh(v * (0.7978845608028654 + 0.7978845608028654 * 0.044715 * square))
            half = 0.5 + 0.5 * t
            act[at, lanes] = (v * half).astype(BF)
            bend = half + v * (1.0 - t * t) * (
                0.5 * 0.7978845608028654 + 0.5 * 0.7978845608028654 * 3.0 * 0.044715 * square
            )
            slope[at, lanes] = (slope[at, lanes].astype(F32) * bend).astype(BF)

        loop(UNITS // 256, body)

    def back(dy, same):
        at = rows_at(p.ring(dy, same) * ROWS, ROWS)

        def put(lanes, value):
            part[at, lanes] = value.astype(BF)

        wide_product(put, lambda lanes: nt(slope[at, :], up_full[lanes, :]))

    def forth(dy):
        at = pair_rows(p, dy)

        def put(lanes, value):
            part_out[at, lanes] = value.astype(BF)

        wide_product(put, lambda lanes: nn(act[at, :], down_full[:, lanes]))

    load_down.wait()
    load_grads.wait()
    lift(0)
    lift(1)
    load_up.wait()
    expand = pl.ds(WIDTH, LANES)
    up_full[expand, :] = (SCALE * up_full[expand, :].astype(F32)).astype(BF)
    gather.own_pair()
    hide(0)
    lift(-1)
    gather.near()
    lift(2)
    gather.near_pairs()
    hide(1)
    gather.far()
    hide(-1)
    gather.far_pair()
    hide(2)
    scatter = Scatter(p, part, sib_in, relay, near, s_send, s_recv)
    back(2, False)
    scatter.exchange(2)
    back(2, True)
    scatter.combine(2)
    scatter.relay_out()
    back(1, False)
    scatter.exchange(1)
    back(1, True)
    scatter.combine(1)
    scatter.near_free(1)
    back(-1, False)
    scatter.exchange(-1)
    back(-1, True)
    scatter.combine(-1)
    scatter.near_free(-1)
    back(0, False)
    scatter.exchange(0)
    back(0, True)
    scatter_out = Scatter(p, part_out, sib_in_out, None, None, t_send, t_recv)
    forth(2)
    scatter_out.exchange(2)
    scatter.near_rest()
    scatter.combine(0)
    for dy in (1, -1, 0):
        forth(dy)
        scatter_out.exchange(dy)

    def by_unit(j):
        at = lanes_at(j * 256, 256)
        by_shard[at, :] = tn(act[:, at], grads[:, pl.ds(WIDTH, LANES)]).astype(BF)
        by_shard[lanes_at(UNITS + j * 256, 256), :] = (
            SCALE * tn(slope[:, at], rows[:, pl.ds(WIDTH, LANES)])
        ).astype(BF)

    loop(UNITS // 256, by_unit)
    copies = []
    for dy in (2, 1, -1, 0):
        scatter_out.combine(dy)
        copy = pltpu.make_async_copy(
            scatter_out.mine(dy), out_parts.at[pl.ds(dy % 4 * ROWS, ROWS)], own_sem.at[4 + dy % 4]
        )
        copy.start()
        copies.append(copy)
    scatter.arrived()
    mask_rows = mask[...].astype(F32)
    side_u[...] = (mask_rows * scatter.total(0, ROWS, pl.ds(WIDTH, LANES))).astype(BF)

    def norm_block(index):
        at = rows_at(index * BLOCK, BLOCK)
        mine = rows_at(p.ring(0, True) * ROWS + index * BLOCK, BLOCK)
        grad = scatter.total(index * BLOCK, BLOCK, pl.ds(0, WIDTH)) + nt(side_u[at, :], up_reduce[...])
        grad = grads[mine, pl.ds(0, WIDTH)].astype(F32) + norm_back(middle[at, :], gain[...], grad)
        grad_out[at, :] = grad
        grad_stage[at, pl.ds(0, WIDTH)] = grad.astype(BF)

    loop(ROWS // BLOCK, norm_block)
    grad_stage[:, pl.ds(WIDTH, LANES)] = (
        mask_rows * (SCALE * nt(grad_stage[:, pl.ds(0, WIDTH)], output_expand[...]))
    ).astype(BF)
    gather.end()
    scatter.end()
    for dy in range(4):
        scatter_out.copy(dy).wait_send()
    for copy in copies:
        copy.wait()


def feed_call(ins):
    outs = [
        shape(ROWS, WIDTH, kind=F32), shape(ROWS, WIDE), shape(ROWS, LANES), shape(2 * UNITS, LANES),
        shape(4 * ROWS, WIDE),
    ]
    scratch = scatter_scratch()
    return call(
        feed_kernel,
        2,
        ins,
        [IN_VMEM] * 7 + [ANYWHERE] * 3,
        outs,
        [IN_VMEM] * 4 + [ANYWHERE],
        [
            pltpu.VMEM((WIDE, UNITS), BF), pltpu.VMEM((UNITS, WIDE), BF), pltpu.VMEM((GROUP, WIDE), BF),
            *gather_scratch(), pltpu.VMEM((GROUP, UNITS), BF), pltpu.VMEM((GROUP, UNITS), BF), *scratch,
            scratch[0], scratch[1], scratch[4], scratch[5], pltpu.SemaphoreType.DMA((8,)),
        ],
    )


class Reducer:
    def __init__(self, place, by_shard, whole, refs):
        self.p, self.by_shard, self.whole = place, by_shard, whole
        (
            self.shard_in, self.shard_sum, self.shard_all, self.sib_in, self.here, self.slices_in, self.slice_sum,
            self.bits_in, self.bit_sum, self.whole_all,
            self.a_send, self.a_recv, self.b_send, self.b_recv, self.c_send, self.c_recv, self.d_send, self.d_recv,
            self.e_send, self.e_recv, self.f_send, self.f_recv, self.g_send, self.g_recv, self.mark,
        ) = refs
        self.m = place.z * 4 + place.x
        self.cut = by_shard.shape[0] // 16
        self.half = whole.shape[0] // 2
        self.slice = self.half // 16
        self.bit = self.slice // 4
        self.sent = []

    @staticmethod
    def scratch(shard_rows, whole_rows):
        dma = pltpu.SemaphoreType.DMA
        cut, half = shard_rows // 16, whole_rows // 2
        piece = half // 16
        return [
            pltpu.VMEM((16, cut, LANES), BF), pltpu.VMEM((cut, LANES), BF), pltpu.VMEM((shard_rows, LANES), BF),
            pltpu.VMEM((half, LANES), BF), pltpu.VMEM((half, LANES), BF), pltpu.VMEM((16, piece, LANES), BF),
            pltpu.VMEM((piece, LANES), BF), pltpu.VMEM((4, piece // 4, LANES), BF), pltpu.VMEM((piece // 4, LANES), BF),
            pltpu.VMEM((whole_rows, LANES), BF),
            dma((16,)), dma((16,)), dma((16,)), dma((16,)), dma((16,)), dma((16,)), dma((4,)), dma((4,)),
            dma((4,)), dma((4,)), dma((2,)), dma((2,)), dma((16,)), dma((16,)), dma((1,)),
        ]

    @staticmethod
    def mates(place):
        m = place.z * 4 + place.x
        mates = []
        for k in range(1, 16):
            other = lax.rem(m + k, 16)
            for core in (0, 1):
                mates.append(place.at(z=lax.div(other, 4), x=lax.rem(other, 4), c=core))
        return mates + [place.at(y=lax.rem(place.y + 2, 4))]

    def member(self, k):
        other = lax.rem(self.m + k, 16)
        return other, self.p.at(z=lax.div(other, 4), x=lax.rem(other, 4))

    def push(self, src, dst, send, recv, device):
        copy = remote(src, dst, send, recv, device)
        copy.start()
        self.sent.append(copy)
        return copy

    def await_at(self, dst, recv):
        remote(dst, dst, self.f_send.at[0], recv, self.p.sib).wait_recv()

    def open(self):
        there = rows_at((1 - self.p.c) * self.half, self.half)
        self.push(self.whole.at[there], self.sib_in, self.f_send.at[0], self.f_recv.at[0], self.p.sib)
        self.open_shard()

    def open_shard(self):
        for k in range(1, 16):
            other, device = self.member(k)
            piece = self.by_shard.at[rows_at(other * self.cut, self.cut)]
            self.push(piece, self.shard_in.at[k], self.a_send.at[k], self.a_recv.at[k], device)

    def halves(self):
        self.await_at(self.sib_in, self.f_recv.at[0])

        def body(index):
            at = rows_at(index * 128, 128)
            mine = self.whole[rows_at(self.p.c * self.half + index * 128, 128), :].astype(F32)
            self.here[at, :] = (mine + self.sib_in[at, :].astype(F32)).astype(BF)

        loop(self.half // 128, body)
        for k in range(1, 16):
            other, device = self.member(k)
            piece = self.here.at[rows_at(other * self.slice, self.slice)]
            self.push(piece, self.slices_in.at[k], self.b_send.at[k], self.b_recv.at[k], device)

    def shards(self):
        p = self.p
        total = self.by_shard[rows_at(self.m * self.cut, self.cut), :].astype(F32)
        for k in range(1, 16):
            self.await_at(self.shard_in.at[k], self.a_recv.at[k])
            total = total + self.shard_in[k].astype(F32)
        self.shard_sum[...] = total.astype(BF)
        mine = self.shard_all.at[rows_at(self.m * self.cut, self.cut)]
        mark = self.c_recv.at[self.m]
        for n in range(1, 16):
            device = p.at(
                z=lax.rem(p.z + n // 4, 4), xl=lax.rem(p.xl + n // 2 % 2, 2), g=p.c, c=lax.rem(p.c + n % 2, 2)
            )
            self.push(self.shard_sum, mine, self.c_send.at[n], mark, device)
        self.swapped = remote(self.shard_sum, mine, self.c_send.at[0], mark, p.at(g=p.c))
        pl.when(p.away)(self.swapped.start)
        pl.when(p.home)(pltpu.make_async_copy(self.shard_sum, mine, mark).start)

    def slices(self):
        total = self.here[rows_at(self.m * self.slice, self.slice), :].astype(F32)
        for k in range(1, 16):
            self.await_at(self.slices_in.at[k], self.b_recv.at[k])
            total = total + self.slices_in[k].astype(F32)
        self.slice_sum[...] = total.astype(BF)
        for dy in (2, 1, 3):
            other = lax.rem(self.p.y + dy, 4)
            piece = self.slice_sum.at[rows_at(other * self.bit, self.bit)]
            self.push(piece, self.bits_in.at[dy], self.d_send.at[dy], self.d_recv.at[dy], self.p.at(y=other))

    def bits(self):
        total = self.slice_sum[rows_at(self.p.y * self.bit, self.bit), :].astype(F32)
        for dy in (1, 3, 2):
            self.await_at(self.bits_in.at[dy], self.d_recv.at[dy])
            total = total + self.bits_in[dy].astype(F32)
        self.bit_sum[...] = total.astype(BF)
        self.base = self.p.c * self.half + self.m * self.slice
        own = self.whole_all.at[rows_at(self.base + self.p.y * self.bit, self.bit)]
        self.placed = pltpu.make_async_copy(self.bit_sum, own, self.mark.at[0])
        self.placed.start()
        for dy in (2, 1, 3):
            device = self.p.at(y=lax.rem(self.p.y + dy, 4))
            self.push(self.bit_sum, own, self.e_send.at[dy], self.e_recv.at[dy], device)

    def slices_back(self):
        self.placed.wait()
        for dy in (1, 3, 2):
            source = lax.rem(self.p.y + 4 - dy, 4)
            self.await_at(self.whole_all.at[rows_at(self.base + source * self.bit, self.bit)], self.e_recv.at[dy])
        own = self.whole_all.at[rows_at(self.base, self.slice)]
        for k in range(1, 16):
            self.push(own, own, self.g_send.at[k], self.g_recv.at[k], self.member(k)[1])

    def halves_back(self):
        for k in range(1, 16):
            source = lax.rem(self.m + 16 - k, 16)
            landing = self.whole_all.at[rows_at(self.p.c * self.half + source * self.slice, self.slice)]
            self.await_at(landing, self.g_recv.at[k])
        half = self.whole_all.at[rows_at(self.p.c * self.half, self.half)]
        self.push(half, half, self.f_send.at[1], self.f_recv.at[1], self.p.sib)

    def close(self):
        for index in range(16):
            self.await_at(self.shard_all.at[pl.ds(index * self.cut, self.cut)], self.c_recv.at[index])
        self.await_at(self.whole_all.at[rows_at((1 - self.p.c) * self.half, self.half)], self.f_recv.at[1])
        for copy in self.sent:
            copy.wait_send()
        pl.when(self.p.away)(self.swapped.wait_send)


def back_kernel(
    grad_stage, output_full, qkv, tokens, gain, mask, cotangent, down_shift, down_expand, joined_reduce, normed, side_q,
    grad, middle, context, second_normed, side_u, side_o, shard_early,
    joined_weights, out_parts, probs_in,
    block_out, input_grad, by_shard, whole, shard_done, whole_done,
    rows, rows_send, rows_recv, probs, key_grad, value_grad, joined_grad, result, block_own, joined_full, whole_early,
    part, sib_in, relay, near, s_send, s_recv, parts, relay_out, near_out, t_send, t_recv, swap_send, swap_recv, own_sem,
    *reduce_refs,
):
    p = Place()
    own_rows = rows_at(p.ring(0, True) * ROWS, ROWS)
    stage = pltpu.make_async_copy(grad_stage, rows.at[own_rows], own_sem.at[0])
    stage.start()
    loads = []
    for dy in (0, 1, -1, 2):
        at = pair_rows(p, dy)
        load = pltpu.make_async_copy(probs_in.at[:, at], probs.at[:, at], own_sem.at[1 + dy % 4])
        load.start()
        loads.append(load)
    load_parts = pltpu.make_async_copy(out_parts, parts, own_sem.at[5])
    load_parts.start()
    load_joined = pltpu.make_async_copy(joined_weights, joined_full, own_sem.at[6])
    load_joined.start()
    greet([p.sib, p.up, p.down] + Reducer.mates(p))
    gather = Gather(p, rows, rows_send, rows_recv)
    stage.wait()
    gather.begin()
    swap = Swap(p, [(block_own, block_out), (result, input_grad)], swap_send, swap_recv)
    reducer = Reducer(p, shard_early, whole_early, reduce_refs)

    def early_column(j):
        lanes = lanes_at(j * 256, 256)
        whole_early[lanes, :] = tn(second_normed[:, lanes], side_u[...]).astype(BF)
        whole_early[lanes_at(WIDTH + j * 256, 256), :] = (SCALE * tn(grad_stage[:, lanes], side_o[...])).astype(BF)

    loop(WIDTH // 256, early_column)
    reducer.open()

    def back(dy):
        base = lax.rem(p.y + dy + 4, 4) * PAIR

        def body(index):
            at = rows_at(base + index * ROWS, ROWS)
            context_grad = nt(rows[at, :], output_full[...]).astype(BF)
            for head in range(2):
                start = head * 3 * HEAD
                query = qkv[at, start : start + HEAD]
                key = qkv[:, start + HEAD : start + 2 * HEAD]
                value = qkv[:, start + 2 * HEAD : start + 3 * HEAD]
                own = context_grad[:, head * HEAD : (head + 1) * HEAD]
                weights = probs[head, at, :]
                mean = jnp.sum(
                    own.astype(F32) * context[at, head * HEAD : (head + 1) * HEAD].astype(F32), axis=-1, keepdims=True
                )
                score_grad = weights * (nt(own, value) - mean).astype(BF)
                joined_grad[at, start : start + HEAD] = (nn(score_grad, key) * (1.0 / math.sqrt(HEAD))).astype(BF)
                value_grad[head] = value_grad[head] + tn(own, weights)
                key_grad[head] = key_grad[head] + tn(query, score_grad)

        loop(2, body)

    value_grad[...] = jnp.zeros_like(value_grad)
    key_grad[...] = jnp.zeros_like(key_grad)
    scatter_out = Scatter(p, parts, None, relay_out, near_out, t_send, t_recv, lambda dy: dy % 4 * ROWS)
    gather.own_pair()
    loads[0].wait()
    back(0)
    reducer.halves()
    gather.near()
    load_parts.wait()
    scatter_out.relay_out()
    scatter_out.near_free(1)
    scatter_out.near_free(-1)
    gather.near_pairs()
    loads[1].wait()
    back(1)
    gather.far()
    reducer.shards()
    loads[2].wait()
    back(-1)
    reducer.slices()
    gather.far_pair()
    loads[3].wait()
    back(2)
    reducer.bits()
    scatter_out.near_rest()
    turn = identity()
    for head in range(2):
        start = head * 3 * HEAD
        joined_grad[:, start + HEAD : start + 2 * HEAD] = tn(
            (key_grad[head] * (1.0 / math.sqrt(HEAD))).astype(BF), turn
        ).astype(BF)
        joined_grad[:, start + 2 * HEAD : start + 3 * HEAD] = tn(value_grad[head].astype(BF), turn).astype(BF)
    load_joined.wait()

    def product(dy, same):
        at = rows_at(p.ring(dy, same) * ROWS, ROWS)

        def put(lanes, value):
            part[at, lanes] = value.astype(BF)

        wide_product(put, lambda lanes: nt(joined_grad[at, :], joined_full[lanes, :]))

    scatter = Scatter(p, part, sib_in, relay, near, s_send, s_recv)
    product(2, False)
    scatter.exchange(2)
    product(2, True)
    scatter.combine(2)
    scatter.relay_out()
    product(1, False)
    scatter.exchange(1)
    product(1, True)
    scatter.combine(1)
    scatter.near_free(1)
    product(-1, False)
    scatter.exchange(-1)
    product(-1, True)
    scatter.combine(-1)
    scatter.near_free(-1)
    product(0, False)
    scatter.exchange(0)
    product(0, True)
    reducer.slices_back()
    scatter.near_rest()
    scatter.combine(0)
    by_shard[pl.ds(0, CTX), :] = tn(context[...], rows[:, pl.ds(WIDTH, LANES)]).astype(BF)

    def by_lane(j):
        lanes = lanes_at(j * 256, 256)
        by_shard[lanes_at(CTX + j * 256, 256), :] = (SCALE * tn(joined_grad[:, lanes], side_q[...])).astype(BF)

    loop(QKV // 256, by_lane)
    scatter_out.arrived()
    mask_rows = mask[...].astype(F32)
    side_d = (mask_rows * scatter_out.total(0, ROWS, pl.ds(WIDTH, LANES))).astype(BF)

    def add_tile(j):
        lanes = lanes_at(j * 256, 256)
        block_own[:, lanes] = (
            middle[:, lanes]
            + scatter_out.total(0, ROWS, lanes)
            + down_shift[:, lanes]
            + SCALE * nn(side_d, down_expand[:, lanes])
        ).astype(BF)
        whole[lanes, :] = (SCALE * tn(cotangent[:, lanes], side_d)).astype(BF)

    loop(WIDTH // 256, add_tile)
    swap.begin(0)
    reducer.halves_back()
    scatter.arrived()
    side = (mask_rows * scatter.total(0, ROWS, pl.ds(WIDTH, LANES))).astype(BF)

    def norm_block(index):
        at = rows_at(index * BLOCK, BLOCK)
        side_rows = (mask[at, :].astype(F32) * scatter.total(index * BLOCK, BLOCK, pl.ds(WIDTH, LANES))).astype(BF)
        back_grad = scatter.total(index * BLOCK, BLOCK, pl.ds(0, WIDTH)) + nt(side_rows, joined_reduce[...])
        result[at, :] = (grad[at, :] + norm_back(tokens[at, :].astype(F32), gain[...], back_grad)).astype(BF)

    loop(ROWS // BLOCK, norm_block)
    swap.begin(1)

    def by_column(j):
        lanes = lanes_at(j * 256, 256)
        whole[lanes_at(WIDTH + j * 256, 256), :] = tn(normed[:, lanes], side).astype(BF)

    loop(WIDTH // 256, by_column)
    reducer.close()
    shard_done[...] = reducer.shard_all[...]
    whole_done[...] = reducer.whole_all[...]
    gather.end()
    scatter.end()
    scatter_out.end(4)
    swap.arrived(0)
    swap.arrived(1)
    swap.end()


def back_call(ins):
    outs = [
        shape(ROWS, WIDTH), shape(ROWS, WIDTH), shape(CTX + QKV, LANES), shape(2 * WIDTH, LANES),
        shape(2 * UNITS, LANES), shape(2 * WIDTH, LANES),
    ]
    scratch = scatter_scratch()
    return call(
        back_kernel,
        3,
        ins,
        [IN_VMEM] * 19 + [ANYWHERE] * 3,
        outs,
        [ANYWHERE] * 2 + [IN_VMEM] * 4,
        [
            *gather_scratch(), pltpu.VMEM((2, GROUP, GROUP), BF), pltpu.VMEM((2, HEAD, GROUP), F32),
            pltpu.VMEM((2, HEAD, GROUP), F32), pltpu.VMEM((GROUP, QKV), BF), pltpu.VMEM((ROWS, WIDTH), BF),
            pltpu.VMEM((ROWS, WIDTH), BF), pltpu.VMEM((WIDE, QKV), BF), pltpu.VMEM((2 * WIDTH, LANES), BF), *scratch,
            pltpu.VMEM((4 * ROWS, WIDE), BF), *scratch[2:], *swap_marks(2), pltpu.SemaphoreType.DMA((7,)),
            *Reducer.scratch(2 * UNITS, 2 * WIDTH),
        ],
    )


def reduce_kernel(by_shard, whole, shard_out, whole_out, *refs):
    p = Place()
    greet([p.sib, p.up, p.down] + Reducer.mates(p))
    reducer = Reducer(p, by_shard, whole, refs)
    reducer.open()
    reducer.halves()
    reducer.shards()
    reducer.slices()
    reducer.bits()
    reducer.slices_back()
    reducer.halves_back()
    reducer.close()
    shard_out[...] = reducer.shard_all[...]
    whole_out[...] = reducer.whole_all[...]


def reduce_call(ins):
    return call(
        reduce_kernel,
        4,
        ins,
        [IN_VMEM] * 2,
        [shape(CTX + QKV, LANES), shape(2 * WIDTH, LANES)],
        [IN_VMEM] * 2,
        Reducer.scratch(CTX + QKV, 2 * WIDTH),
    )


def finish_kernel(
    shard_early, whole_early, shard_late, whole_late, block_in, grad_in,
    block_out, input_grad, qkv_a, qkv_b, out_a, out_b, up_a, up_b, down_a, down_b,
):
    turn = identity()

    def turned(source, start, out, count):
        def body(j):
            out[0, :, lanes_at(j * 256, 256)] = nt(turn, source[lanes_at(start + j * 256, 256), :])

        loop(count // 256, body)

    def widened(source, out):
        def body(index):
            at = rows_at(index * BLOCK, BLOCK)
            out[at, :] = source[at, :].astype(F32)

        loop(ROWS // BLOCK, body)

    widened(block_in, block_out)
    widened(grad_in, input_grad)
    down_a[0] = shard_early[pl.ds(0, UNITS), :].astype(F32)
    turned(shard_early, UNITS, up_b, UNITS)
    out_a[0] = shard_late[pl.ds(0, CTX), :].astype(F32)
    turned(shard_late, CTX, qkv_b, QKV)
    up_a[0] = whole_early[pl.ds(0, WIDTH), :].astype(F32)
    turned(whole_early, WIDTH, out_b, WIDTH)
    turned(whole_late, 0, down_b, WIDTH)
    qkv_a[0] = whole_late[pl.ds(WIDTH, WIDTH), :].astype(F32)


def finish_call(ins):
    return pl.pallas_call(
        finish_kernel,
        name="finish_kernel",
        out_shape=[
            shape(ROWS, WIDTH, kind=F32), shape(ROWS, WIDTH, kind=F32), shape(1, WIDTH, LANES, kind=F32),
            shape(1, LANES, QKV, kind=F32), shape(1, CTX, LANES, kind=F32), shape(1, LANES, WIDTH, kind=F32),
            shape(1, WIDTH, LANES, kind=F32), shape(1, LANES, UNITS, kind=F32), shape(1, UNITS, LANES, kind=F32),
            shape(1, LANES, WIDTH, kind=F32),
        ],
        in_specs=[IN_VMEM] * 6,
        out_specs=[IN_VMEM] * 10,
        compiler_params=pltpu.CompilerParams(vmem_limit_bytes=VMEM_LIMIT),
    )(*ins)


def shards(
    tokens, lengths, order, sequence_adapter, first_norm_gain, first_norm_bias, second_norm_gain, second_norm_bias,
    joined_matrix, joined_offset_bias, output_matrix, output_offset_bias, up_matrix, up_offset_bias, down_matrix,
    down_offset_bias, joined_adapter_reduce, joined_adapter_expand, output_adapter_reduce, output_adapter_expand,
    up_adapter_reduce, up_adapter_expand, down_adapter_reduce, down_adapter_expand, cotangent,
):
    (
        normed, middle, side_o, context, qkv, mask_own, probs, side_q, normed_first, gathered_grad, cot_own,
        joined_full, output_full, up_full, down_full, tokens_own, up_shift_own,
    ) = forward_call(
        (
            first_norm_gain, first_norm_bias, joined_adapter_reduce[0], down_adapter_expand[0],
            joined_adapter_expand[0], joined_offset_bias, order, output_adapter_expand[0], output_offset_bias,
            second_norm_gain, second_norm_bias, up_adapter_reduce[0], lengths, sequence_adapter,
            tokens, cotangent, up_offset_bias, joined_matrix[0], output_matrix[0], output_adapter_reduce[0],
            up_matrix[0], up_adapter_expand[0], down_matrix[0], down_adapter_reduce[0],
        )
    )
    grad, grad_stage, side_u, shard_feed, out_parts = feed_call(
        (
            normed, middle, up_shift_own, mask_own, second_norm_gain, up_adapter_reduce[0],
            output_adapter_expand[0], gathered_grad, up_full, down_full,
        )
    )
    block_own, input_own, shard_back, whole_back, shard_early, whole_early = back_call(
        (
            grad_stage, output_full, qkv, tokens_own, first_norm_gain, mask_own, cot_own, down_offset_bias,
            down_adapter_expand[0], joined_adapter_reduce[0], normed_first, side_q, grad, middle, context,
            normed, side_u, side_o, shard_feed, joined_full, out_parts, probs,
        )
    )
    shard_late, whole_late = reduce_call((shard_back, whole_back))
    return tuple(finish_call((shard_early, whole_early, shard_late, whole_late, block_own, input_own)))


def solution(mesh):
    spread = P(("dp", "tensor"), None)
    by_dp = P("dp", None)
    rows = P(None, "dp", "tensor")
    cols = P(None, "tensor", "dp")
    last = P(None, None, "tensor")
    middle = P(None, "tensor", None)
    vector = P(None, "tensor")
    return jax.shard_map(
        shards,
        mesh=mesh,
        in_specs=(
            spread, by_dp, by_dp, by_dp, P(), P(), P(), P(), rows, vector, cols, P(), rows, vector, cols, P(),
            P(), last, middle, P(), P(), last, middle, P(), spread,
        ),
        out_specs=(spread, spread, P(), last, middle, P(), P(), last, middle, P()),
        check_vma=False,
    )
```

```python
import functools
import math

import jax
import jax.numpy as jnp
from jax import lax
from jax.experimental import pallas as pl
from jax.experimental.pallas import tpu as pltpu
from jax.sharding import PartitionSpec as P

HEAD = 128
WIDTH = 2048
LANES = 128
WIDE = WIDTH + LANES
ROWS = 160
HALF = ROWS // 2
PAIR = 2 * ROWS
GROUP = 8 * ROWS
QKV = 768
UNITS = 1024
CTX = 256
BLOCK = 32
SCALE = 0.5
EPS = 1e-05
MASKED = -1e30
LOG2E = 1.4426950408889634
VMEM_LIMIT = 60 * 2**20
BF = jnp.bfloat16
F32 = jnp.float32
BY_MESH = pl.DeviceIdType.MESH
ANYWHERE = pl.BlockSpec(memory_space=pl.ANY)
IN_VMEM = pl.BlockSpec(memory_space=pltpu.VMEM)
IN_SMEM = pl.BlockSpec(memory_space=pltpu.SMEM)


def nn(left, right):
    return jnp.dot(left, right, preferred_element_type=F32)


def nt(left, right):
    return lax.dot_general(left, right, (((1,), (1,)), ((), ())), preferred_element_type=F32)


def tn(left, right):
    return lax.dot_general(left, right, (((0,), (0,)), ((), ())), preferred_element_type=F32)


def rows_at(start, size):
    return pl.ds(pl.multiple_of(start, 16), size)


def lanes_at(start, size):
    return pl.ds(pl.multiple_of(start, 128), size)


def loop(count, body):
    def step(index, carry):
        body(index)
        return carry

    lax.fori_loop(0, count, step, 0)


class Place:
    def __init__(self):
        dp = lax.axis_index("dp")
        tensor = lax.axis_index("tensor")
        self.dp = dp
        self.z = lax.div(dp, 4)
        self.xl = lax.rem(lax.div(dp, 2), 2)
        self.c = lax.rem(dp, 2)
        self.y = lax.div(tensor, 2)
        self.g = lax.rem(tensor, 2)
        self.x = self.g * 2 + self.xl
        self.sib = self.at(c=1 - self.c)
        self.up = self.at(y=lax.rem(self.y + 1, 4))
        self.down = self.at(y=lax.rem(self.y + 3, 4))
        self.z_up = self.at(z=lax.rem(self.z + 1, 4))
        self.z_down = self.at(z=lax.rem(self.z + 3, 4))
        self.partner = self.at(g=self.c, c=self.g)
        self.home = self.c == self.g
        self.away = self.c != self.g

    def at(self, z=None, x=None, xl=None, c=None, y=None, g=None):
        z = self.z if z is None else z
        c = self.c if c is None else c
        y = self.y if y is None else y
        if x is None:
            xl = self.xl if xl is None else xl
            g = self.g if g is None else g
        else:
            xl = lax.rem(x, 2)
            g = lax.div(x, 2)
        return (z * 4 + xl * 2 + c, y * 2 + g)

    def in_row(self, dx, core):
        return self.at(x=lax.rem(self.x + dx, 4), c=core)

    def row_mates(self):
        return [self.in_row(dx, core) for dx in (1, 2, 3) for core in (0, 1)]

    def column_mates(self):
        return [self.at(z=lax.rem(self.z + dz, 4), c=core) for dz in (1, 2, 3) for core in (0, 1)]

    def ring_mates(self):
        mates = [self.sib]
        for dy in (1, 2, 3):
            y = lax.rem(self.y + dy, 4)
            mates += [self.at(y=y), self.at(y=y, c=1 - self.c)]
        return mates

    def ring(self, dy, same):
        return lax.rem(self.y + dy + 4, 4) * 2 + (self.c if same else 1 - self.c)


def greet(devices):
    barrier = pltpu.get_barrier_semaphore()
    for device in devices:
        pl.semaphore_signal(barrier, 1, device_id=device, device_id_type=BY_MESH)
    pl.semaphore_wait(barrier, len(devices))


def remote(src, dst, send, recv, device):
    return pltpu.make_async_remote_copy(
        src_ref=src, dst_ref=dst, send_sem=send, recv_sem=recv, device_id=device, device_id_type=BY_MESH
    )


class Gather:
    SENDS = (
        (0, True, None),
        (0, True, None),
        (0, True, None),
        (-1, True, 0),
        (1, True, 1),
        (-1, True, None),
        (1, True, None),
        (2, True, 0),
        (2, True, 1),
    )
    LANDS = (
        (0, False, None),
        (-1, True, None),
        (1, True, None),
        (2, True, 0),
        (2, True, 1),
        (-1, False, None),
        (1, False, None),
        (2, False, 0),
        (2, False, 1),
    )

    def __init__(self, place, buf, send, recv):
        self.place, self.buf, self.send, self.recv = place, buf, send, recv
        p = place
        self.to = (p.sib, p.up, p.down, p.up, p.down, p.sib, p.sib, p.sib, p.sib)

    def piece(self, what):
        dy, same, half = what
        start = self.place.ring(dy, same) * ROWS
        if half is None:
            return self.buf.at[rows_at(start, ROWS)]
        return self.buf.at[rows_at(start + half * HALF, HALF)]

    def copy(self, i):
        piece = self.piece(self.SENDS[i])
        return remote(piece, piece, self.send.at[i], self.recv.at[i], self.to[i])

    def landed(self, i):
        piece = self.piece(self.LANDS[i])
        remote(piece, piece, self.send.at[i], self.recv.at[i], self.to[i]).wait_recv()

    def begin(self):
        for i in (1, 2, 0):
            self.copy(i).start()

    def near(self):
        self.landed(1)
        self.copy(3).start()
        self.copy(5).start()
        self.landed(2)
        self.copy(4).start()
        self.copy(6).start()

    def far(self):
        self.landed(3)
        self.copy(7).start()
        self.landed(4)
        self.copy(8).start()

    def own_pair(self):
        self.landed(0)

    def near_pairs(self):
        self.landed(5)
        self.landed(6)

    def far_pair(self):
        self.landed(7)
        self.landed(8)

    def end(self):
        for i in range(9):
            self.copy(i).wait_send()


class Scatter:
    def __init__(self, place, part, sib_in, relay, near, send, recv, start=None):
        self.place, self.part, self.sib_in, self.relay, self.near = place, part, sib_in, relay, near
        self.send, self.recv = send, recv
        self.start = start or (lambda dy: place.ring(dy, True) * ROWS)

    def mine(self, dy, half=None):
        start = self.start(dy)
        if half is None:
            return self.part.at[rows_at(start, ROWS)]
        return self.part.at[rows_at(start + half * HALF, HALF)]

    def others(self, dy):
        return self.part.at[rows_at(self.place.ring(dy, False) * ROWS, ROWS)]

    def copy(self, i):
        p = self.place
        if i < 4:
            src, dst, to = self.others(i), self.sib_in.at[i], p.sib
        elif i == 4:
            src, dst, to = self.mine(2, 0), self.relay.at[0], p.up
        elif i == 5:
            src, dst, to = self.mine(2, 1), self.relay.at[1], p.down
        elif i == 6:
            src, dst, to = self.mine(1, 1), self.near.at[0, pl.ds(HALF, HALF)], p.up
        elif i == 7:
            src, dst, to = self.mine(-1, 0), self.near.at[1, pl.ds(0, HALF)], p.down
        elif i == 8:
            src, dst, to = self.mine(1, 0), self.near.at[0, pl.ds(0, HALF)], p.up
        else:
            src, dst, to = self.mine(-1, 1), self.near.at[1, pl.ds(HALF, HALF)], p.down
        return remote(src, dst, self.send.at[i], self.recv.at[i], to)

    def exchange(self, dy):
        self.copy(dy % 4).start()

    def combine(self, dy):
        self.copy(dy % 4).wait_recv()
        add_rows(self.part, self.start(dy), self.sib_in.at[dy % 4], 0, ROWS)

    def relay_out(self):
        self.copy(4).start()
        self.copy(5).start()

    def near_free(self, dy):
        self.copy(6 if dy == 1 else 7).start()

    def near_rest(self):
        self.copy(4).wait_recv()
        add_rows(self.part, self.start(1), self.relay.at[0], 0, HALF)
        self.copy(8).start()
        self.copy(5).wait_recv()
        add_rows(self.part, self.start(-1) + HALF, self.relay.at[1], 0, HALF)
        self.copy(9).start()

    def arrived(self):
        for i in (6, 7, 8, 9):
            self.copy(i).wait_recv()

    def total(self, start, size, lanes):
        own = self.part[rows_at(self.start(0) + start, size), lanes].astype(F32)
        return (
            own
            + self.near[0, rows_at(start, size), lanes].astype(F32)
            + self.near[1, rows_at(start, size), lanes].astype(F32)
        )

    def end(self, first=0, last=10):
        for i in range(first, last):
            self.copy(i).wait_send()


def scatter_scratch(width=WIDE):
    return [
        pltpu.VMEM((GROUP, width), BF),
        pltpu.VMEM((4, ROWS, width), BF),
        pltpu.VMEM((2, HALF, width), BF),
        pltpu.VMEM((2, ROWS, width), BF),
        pltpu.SemaphoreType.DMA((10,)),
        pltpu.SemaphoreType.DMA((10,)),
    ]


def gather_scratch():
    return [pltpu.VMEM((GROUP, WIDE), BF), pltpu.SemaphoreType.DMA((9,)), pltpu.SemaphoreType.DMA((9,))]


def add_rows(dst, start, src, src_start, count):
    def body(index):
        at = rows_at(start + index * 16, 16)
        dst[at, :] = (dst[at, :].astype(F32) + src[rows_at(src_start + index * 16, 16), :].astype(F32)).astype(BF)

    loop(count // 16, body)


class Weights:
    def __init__(self, place, piece, full, by_rows, cut, send, recv):
        self.place, self.piece, self.full, self.by_rows = place, piece, full, by_rows
        self.send, self.recv = send, recv
        size = piece.shape[1] if by_rows else piece.shape[0]
        self.parts = (pl.ds(0, cut), pl.ds(cut, size - cut))

    def source(self, half):
        part = self.parts[half]
        return self.piece.at[:, part] if self.by_rows else self.piece.at[part, :]

    def slot(self, index, count, half):
        span = lanes_at(index * 128, count * 128)
        part = self.parts[half]
        return self.full.at[span, part] if self.by_rows else self.full.at[part, span]

    def column(self, dz):
        return lax.rem(self.place.z + dz, 4)

    def first(self):
        p = self.place
        marks = (self.recv.at[p.xl * 2 + p.c], self.recv.at[4 + p.z * 2 + p.c])
        slots = (self.slot(p.dp, 1, 0), self.slot(p.dp, 1, 1))
        for d in (2, 1, 3):
            remote(self.source(0), slots[0], self.send.at[d], marks[0], p.in_row(d, p.g)).start()
            remote(self.source(1), slots[1], self.send.at[4 + d], marks[1], p.at(z=self.column(d), c=p.g)).start()

        @pl.when(p.home)
        def _():
            for half in range(2):
                pltpu.make_async_copy(self.source(half), slots[half], marks[half]).start()

        @pl.when(p.away)
        def _():
            for half in range(2):
                remote(self.source(half), slots[half], self.send.at[4 * half], marks[half], p.sib).start()

    def landed(self, slot, mark):
        remote(slot, slot, self.send.at[0], self.recv.at[mark], self.place.sib).wait_recv()

    def along_z(self, i):
        p = self.place
        z, first, count, to = (
            (p.z, 0, 4, p.z_up),
            (p.z, 0, 4, p.z_down),
            (self.column(3), 0, 2, p.z_up),
            (self.column(1), 2, 2, p.z_down),
        )[i]
        block = self.slot(z * 4 + first, count, 0)
        return remote(block, block, self.send.at[8 + i], self.recv.at[12 + i], to)

    def along_x(self, z, dx):
        p = self.place
        pair = self.slot(z * 4 + p.xl * 2, 2, 1)
        mark = self.send.at[12 + z * 2 + dx // 2]
        return remote(pair, pair, mark, self.recv.at[16 + p.xl * 4 + z], p.in_row(dx, p.c))

    def second(self):
        p = self.place
        for index in range(4):
            self.landed(self.slot(p.z * 4 + index, 1, 0), index)
        self.along_z(0).start()
        self.along_z(1).start()

        @pl.when(p.home)
        def _():
            for z in range(4):
                for core in range(2):
                    self.landed(self.slot(z * 4 + p.xl * 2 + core, 1, 1), 4 + z * 2 + core)
                self.along_x(z, 1).start()
                self.along_x(z, 3).start()

    def passed_on(self, i):
        p = self.place
        home = 1 - lax.rem(p.c + p.g, 2)
        plus = 1 - lax.rem(p.xl + home, 2)
        z = (1 - plus) * 2 + i
        pair = self.slot(z * 4 + (1 - p.xl) * 2, 2, 1)
        mark = self.recv.at[16 + (1 - p.xl) * 4 + z]
        return remote(pair, pair, self.send.at[20 + i], mark, p.in_row(3 - 2 * plus, p.c))

    def third(self):
        p = self.place
        self.landed(self.slot(self.column(3) * 4, 4, 0), 12)
        self.along_z(2).start()
        self.landed(self.slot(self.column(1) * 4, 4, 0), 13)
        self.along_z(3).start()
        for z in range(4):
            self.landed(self.slot(z * 4 + (1 - p.xl) * 2, 2, 1), 16 + (1 - p.xl) * 4 + z)
        for i in range(2):
            self.passed_on(i).start()

    def arrived(self):
        p = self.place
        self.landed(self.slot(self.column(2) * 4, 2, 0), 14)
        self.landed(self.slot(self.column(2) * 4 + 2, 2, 0), 15)

        @pl.when(p.away)
        def _():
            for z in range(4):
                self.landed(self.slot(z * 4 + p.xl * 2, 2, 1), 16 + p.xl * 4 + z)

    def end(self):
        p = self.place
        for d in (1, 2, 3):
            for half in range(2):
                slot = self.slot(p.dp, 1, half)
                remote(self.source(half), slot, self.send.at[4 * half + d], self.recv.at[0], p.sib).wait_send()
        for i in range(4):
            self.along_z(i).wait_send()
        for i in range(2):
            self.passed_on(i).wait_send()

        @pl.when(p.away)
        def _():
            for half in range(2):
                slot = self.slot(p.dp, 1, half)
                remote(self.source(half), slot, self.send.at[4 * half], self.recv.at[0], p.sib).wait_send()

        @pl.when(p.home)
        def _():
            for z in range(4):
                self.along_x(z, 1).wait_send()
                self.along_x(z, 3).wait_send()


def weight_marks():
    return [pltpu.SemaphoreType.DMA((22,)), pltpu.SemaphoreType.DMA((24,))]


class Swap:
    def __init__(self, place, pairs, send, recv):
        self.place, self.pairs, self.send, self.recv = place, pairs, send, recv

    def begin(self, i):
        src, dst = self.pairs[i]
        p = self.place

        @pl.when(p.home)
        def _():
            pltpu.make_async_copy(src, dst, self.recv.at[i]).start()

        @pl.when(p.away)
        def _():
            remote(src, dst, self.send.at[i], self.recv.at[i], p.partner).start()

    def arrived(self, i):
        src, dst = self.pairs[i]
        remote(src, dst, self.send.at[i], self.recv.at[i], self.place.sib).wait_recv()

    def end(self):
        @pl.when(self.place.away)
        def _():
            for i, (src, dst) in enumerate(self.pairs):
                remote(src, dst, self.send.at[i], self.recv.at[i], self.place.sib).wait_send()


def swap_marks(count):
    return [pltpu.SemaphoreType.DMA((count,)), pltpu.SemaphoreType.DMA((count,))]


def normalise(value):
    mean = jnp.mean(value, axis=-1, keepdims=True)
    center = value - mean
    inverse = lax.rsqrt(jnp.mean(center * center, axis=-1, keepdims=True) + EPS)
    return center * inverse, inverse


def norm_back(value, gain, grad):
    normed, inverse = normalise(value)
    e = grad * gain
    return (e - jnp.mean(e, axis=-1, keepdims=True) - normed * jnp.mean(e * normed, axis=-1, keepdims=True)) * inverse


def pair_rows(place, dy):
    return rows_at(lax.rem(place.y + dy + 4, 4) * PAIR, PAIR)


def wide_product(put, make):
    loop(4, lambda j: put(lanes_at(j * 512, 512), make(lanes_at(j * 512, 512))))
    put(pl.ds(WIDTH, LANES), make(pl.ds(WIDTH, LANES)))


def call(kernel, collective, ins, specs, outs, out_specs, scratch):
    return pl.pallas_call(
        kernel,
        name=kernel.__name__,
        out_shape=outs,
        in_specs=specs,
        out_specs=out_specs,
        scratch_shapes=scratch,
        compiler_params=pltpu.CompilerParams(
            collective_id=collective, has_side_effects=True, vmem_limit_bytes=VMEM_LIMIT
        ),
    )(*ins)


def shape(*dims, kind=BF):
    return jax.ShapeDtypeStruct(dims, kind)


def identity():
    row = lax.broadcasted_iota(jnp.int32, (LANES, LANES), 0)
    return jnp.where(row == lax.broadcasted_iota(jnp.int32, (LANES, LANES), 1), 1.0, 0.0).astype(BF)


def query_info(token_row, start_row):
    token_high = jnp.floor(token_row * (1.0 / 16.0))
    start_high = jnp.floor(start_row * (1.0 / 16.0))
    digit = lax.broadcasted_iota(jnp.int32, (16, GROUP), 0)
    digits = jnp.where(digit == 0, token_high, 0.0)
    digits = jnp.where(digit == 1, token_row - 16.0 * token_high, digits)
    digits = jnp.where(digit == 2, start_high, digits)
    digits = jnp.where(digit == 3, start_row - 16.0 * start_high, digits)
    row = lax.broadcasted_iota(jnp.int32, (16, LANES), 0)
    lane = lax.broadcasted_iota(jnp.int32, (16, LANES), 1)
    worth = jnp.where((row == 0) & (lane == 0) | (row == 2) & (lane == 1), 16.0, 0.0)
    worth = worth + jnp.where((row == 1) & (lane == 0) | (row == 3) & (lane == 1), 1.0, 0.0)
    return tn(digits.astype(BF), worth.astype(BF))


def slope_row(place, head, tokens_row):
    number = (place.ring(0, True) * 2 + head + 1).astype(F32)
    slope = jnp.exp2(jnp.full((1, GROUP), -0.5, F32) * number)
    return slope * LOG2E * tokens_row


def forward_kernel(
    gain, shift, joined_reduce, down_expand, joined_expand, joined_shift, order, output_expand, output_shift,
    second_gain, second_shift, up_reduce, lengths, adapters,
    tokens, cotangent, up_shift, joined_piece, output_piece, output_reduce, up_piece, up_expand, down_piece, down_reduce,
    normed, middle, side_o, context, qkv, mask_own,
    probs_out, side_q, normed_own, gathered_grad, cot_own, joined_full, output_full, up_full, down_full, tokens_own,
    up_shift_own,
    tok_here, aux, aux_here, half_expand, shift_here, joined_here, output_here, info, mask_all, probs,
    rows, rows_send, rows_recv, grads, grads_send, grads_recv, part, sib_in, relay, near, s_send, s_recv,
    w_send, w_recv, o_send, o_recv, u_send, u_recv, d_send, d_recv, swap_send, swap_recv, out_sem, probs_sem,
):
    p = Place()
    greet([p.sib, p.up, p.down] + p.row_mates() + p.column_mates())
    joined = Weights(p, joined_piece, joined_here.at[pl.ds(0, WIDTH)], True, 512, w_send, w_recv)
    output = Weights(p, output_piece, output_here.at[:, pl.ds(0, WIDTH)], False, 160, o_send, o_recv)
    up = Weights(p, up_piece, up_full.at[pl.ds(0, WIDTH)], True, 640, u_send, u_recv)
    down = Weights(p, down_piece, down_full.at[:, pl.ds(0, WIDTH)], False, 640, d_send, d_recv)
    own_rows = rows_at(p.ring(0, True) * ROWS, ROWS)
    their_rows = rows_at((p.y * 2 + p.g) * ROWS, ROWS)
    swap = Swap(
        p,
        [
            (tokens, tok_here),
            (aux, aux_here),
            (half_expand, joined_here.at[pl.ds(WIDTH, LANES)]),
            (joined_shift, shift_here),
            (cotangent, grads.at[their_rows, pl.ds(0, WIDTH)]),
            (output_reduce, output_here.at[:, pl.ds(WIDTH, LANES)]),
            (up_expand, up_full.at[pl.ds(WIDTH, LANES)]),
            (down_reduce, down_full.at[:, pl.ds(WIDTH, LANES)]),
            (up_shift, up_shift_own),
        ],
        swap_send,
        swap_recv,
    )
    joined.first()
    swap.begin(0)
    token = order[...]
    first_end = lengths[0, 0]
    second_end = first_end + lengths[0, 1]
    later = token >= second_end
    late = token >= first_end
    start = jnp.where(later, second_end, jnp.where(late, first_end, 0))
    adapter = jnp.where(later, adapters[0, 2], jnp.where(late, adapters[0, 1], adapters[0, 0]))
    for i, row in enumerate((token, start, adapter)):
        aux[:, pl.ds(i * GROUP, GROUP)] = jnp.broadcast_to(row.astype(F32), (8, GROUP))
    half_expand[...] = (SCALE * joined_expand[...].astype(F32)).astype(BF)
    for i in (1, 2, 3):
        swap.begin(i)
    swap.arrived(1)
    token_row = aux_here[0:1, pl.ds(0, GROUP)]
    info[...] = query_info(token_row, aux_here[0:1, pl.ds(GROUP, GROUP)])
    column = lax.shift_right_logical(lax.broadcasted_iota(jnp.int32, (LANES, GROUP), 0), 4).astype(F32)
    chosen = jnp.where(column == aux_here[0:1, pl.ds(2 * GROUP, GROUP)], 1.0, 0.0).astype(BF)
    mask_all[...] = tn(chosen, identity()).astype(BF)
    mask_own[...] = mask_all[own_rows, :]
    mask_rows = mask_all[own_rows, :].astype(F32)
    joined.second()
    swap.arrived(0)

    def norm_block(index):
        at = rows_at(index * BLOCK, BLOCK)
        value, _ = normalise(tok_here[at, :].astype(F32))
        rows[rows_at(p.ring(0, True) * ROWS + index * BLOCK, BLOCK), pl.ds(0, WIDTH)] = (
            value * gain[...] + shift[...]
        ).astype(BF)

    loop(ROWS // BLOCK, norm_block)
    rows[own_rows, pl.ds(WIDTH, LANES)] = (
        mask_rows * nn(rows[own_rows, pl.ds(0, WIDTH)], joined_reduce[...])
    ).astype(BF)
    gather = Gather(p, rows, rows_send, rows_recv)
    gather_grad = Gather(p, grads, grads_send, grads_recv)
    gather.begin()
    swap.begin(4)
    output.first()
    joined.third()
    up.first()
    down.first()
    for i in range(5, 9):
        swap.begin(i)
    output.second()
    swap.arrived(4)
    grads[own_rows, pl.ds(WIDTH, LANES)] = (
        mask_rows * (SCALE * nt(grads[own_rows, pl.ds(0, WIDTH)], down_expand[...]))
    ).astype(BF)
    copies = [
        pltpu.make_async_copy(tok_here, tokens_own, out_sem.at[0]),
        pltpu.make_async_copy(grads.at[own_rows, pl.ds(0, WIDTH)], cot_own, out_sem.at[1]),
        pltpu.make_async_copy(rows.at[own_rows, pl.ds(0, WIDTH)], normed_own, out_sem.at[2]),
    ]
    for copy in copies:
        copy.start()
    gather.near()
    gather_grad.begin()
    up.second()
    swap.arrived(2)
    swap.arrived(3)
    joined.arrived()
    copies.append(pltpu.make_async_copy(joined_here, joined_full, out_sem.at[3]))
    copies[-1].start()

    def project(dy):
        at = pair_rows(p, dy)

        def body(j):
            lanes = lanes_at(j * 256, 256)
            qkv[at, lanes] = (nn(rows[at, :], joined_here[:, lanes]) + shift_here[:, lanes]).astype(BF)

        loop(QKV // 256, body)

    gather.own_pair()
    project(0)
    gather.near_pairs()
    project(1)
    output.third()
    project(-1)
    gather.far()
    down.second()
    gather.far_pair()
    project(2)
    up.third()
    copies.append(pltpu.make_async_copy(rows.at[:, pl.ds(WIDTH, LANES)], side_q, out_sem.at[4]))
    copies[-1].start()
    output.arrived()
    swap.arrived(5)
    copies.append(pltpu.make_async_copy(output_here, output_full, out_sem.at[5]))
    copies[-1].start()
    probs_copies = []

    def attend(dy, same):
        at = rows_at(p.ring(dy, same) * ROWS, ROWS)
        n = len(probs_copies)
        if n >= 2:
            probs_copies[n - 2].wait()
        query_token = info[at, 0:1]
        query_start = info[at, 1:2]
        allowed = (token_row <= query_token) & (token_row >= query_start)
        for head in range(2):
            first = head * 3 * HEAD
            scores = nt(qkv[at, first : first + HEAD], qkv[:, first + HEAD : first + 2 * HEAD])
            scores = scores * (LOG2E / math.sqrt(HEAD)) + slope_row(p, head, token_row)
            scores = jnp.where(allowed, scores, MASKED)
            top = jnp.max(scores, axis=-1, keepdims=True)
            weights = jnp.exp2(scores - top)
            total = jnp.sum(weights, axis=-1, keepdims=True)
            weights = (weights * (1.0 / total)).astype(BF)
            probs[n % 2, head] = weights
            context[at, head * HEAD : (head + 1) * HEAD] = nn(
                weights, qkv[:, first + 2 * HEAD : first + 3 * HEAD]
            ).astype(BF)
        copy = pltpu.make_async_copy(probs.at[n % 2], probs_out.at[:, at], probs_sem.at[n])
        copy.start()
        probs_copies.append(copy)

        def put(lanes, value):
            part[at, lanes] = value.astype(BF)

        wide_product(put, lambda lanes: nn(context[at, :], output_here[:, lanes]))

    scatter = Scatter(p, part, sib_in, relay, near, s_send, s_recv)
    attend(2, False)
    scatter.exchange(2)
    attend(2, True)
    scatter.combine(2)
    scatter.relay_out()
    gather_grad.near()
    attend(1, False)
    scatter.exchange(1)
    attend(1, True)
    scatter.combine(1)
    scatter.near_free(1)
    down.third()
    attend(-1, False)
    scatter.exchange(-1)
    attend(-1, True)
    scatter.combine(-1)
    scatter.near_free(-1)
    gather_grad.far()
    attend(0, False)
    scatter.exchange(0)
    scatter.near_rest()
    attend(0, True)
    scatter.combine(0)
    gather_grad.own_pair()
    gather_grad.near_pairs()
    gather_grad.far_pair()
    copies.append(pltpu.make_async_copy(grads, gathered_grad, out_sem.at[6]))
    copies[-1].start()
    scatter.arrived()
    side = (mask_rows * scatter.total(0, ROWS, pl.ds(WIDTH, LANES))).astype(BF)
    side_o[...] = side

    def add_tile(j):
        lanes = lanes_at(j * 512, 512)
        middle[:, lanes] = (
            tok_here[:, lanes].astype(F32)
            + scatter.total(0, ROWS, lanes)
            + output_shift[:, lanes]
            + SCALE * nn(side, output_expand[:, lanes])
        )

    loop(4, add_tile)

    def second_block(index):
        at = rows_at(index * BLOCK, BLOCK)
        value, _ = normalise(middle[at, :])
        normed[at, pl.ds(0, WIDTH)] = (value * second_gain[...] + second_shift[...]).astype(BF)

    loop(ROWS // BLOCK, second_block)
    normed[:, pl.ds(WIDTH, LANES)] = (mask_rows * nn(normed[:, pl.ds(0, WIDTH)], up_reduce[...])).astype(BF)
    up.arrived()
    down.arrived()
    for i in range(6, 9):
        swap.arrived(i)
    swap.end()
    for sender in (gather, gather_grad, scatter, joined, output, up, down):
        sender.end()
    for copy in copies + probs_copies[-2:]:
        copy.wait()


def forward_call(ins):
    outs = [
        shape(ROWS, WIDE), shape(ROWS, WIDTH, kind=F32), shape(ROWS, LANES), shape(GROUP, CTX), shape(GROUP, QKV),
        shape(ROWS, LANES),
        shape(2, GROUP, GROUP), shape(GROUP, LANES), shape(ROWS, WIDTH), shape(GROUP, WIDE), shape(ROWS, WIDTH),
        shape(WIDE, QKV), shape(CTX, WIDE), shape(WIDE, UNITS), shape(UNITS, WIDE), shape(ROWS, WIDTH),
        shape(1, UNITS, kind=F32),
    ]
    return call(
        forward_kernel,
        1,
        ins,
        [IN_VMEM] * 12 + [IN_SMEM] * 2 + [ANYWHERE] * 10,
        outs,
        [IN_VMEM] * 6 + [ANYWHERE] * 11,
        [
            pltpu.VMEM((ROWS, WIDTH), BF), pltpu.VMEM((8, 3 * GROUP), F32), pltpu.VMEM((8, 3 * GROUP), F32),
            pltpu.VMEM((LANES, QKV), BF), pltpu.VMEM((1, QKV), F32), pltpu.VMEM((WIDE, QKV), BF),
            pltpu.VMEM((CTX, WIDE), BF), pltpu.VMEM((GROUP, LANES), F32), pltpu.VMEM((GROUP, LANES), BF),
            pltpu.VMEM((2, 2, ROWS, GROUP), BF), *gather_scratch(), *gather_scratch(), *scatter_scratch(),
            *weight_marks(), *weight_marks(), *weight_marks(), *weight_marks(), *swap_marks(9),
            pltpu.SemaphoreType.DMA((7,)), pltpu.SemaphoreType.DMA((8,)),
        ],
    )


def feed_kernel(
    normed, middle, up_shift, mask, gain, up_reduce, output_expand,
    gathered_grad, up_weights, down_weights,
    grad_out, grad_stage, side_u, by_shard, out_parts,
    up_full, down_full, grads, rows, rows_send, rows_recv, act, slope, part, sib_in, relay, near, s_send, s_recv,
    part_out, sib_in_out, t_send, t_recv, own_sem,
):
    p = Place()
    own_rows = rows_at(p.ring(0, True) * ROWS, ROWS)
    stage = pltpu.make_async_copy(normed, rows.at[own_rows], own_sem.at[0])
    stage.start()
    load_down = pltpu.make_async_copy(down_weights, down_full, own_sem.at[1])
    load_down.start()
    load_grads = pltpu.make_async_copy(gathered_grad, grads, own_sem.at[2])
    load_grads.start()
    load_up = pltpu.make_async_copy(up_weights, up_full, own_sem.at[3])
    load_up.start()
    greet([p.sib, p.up, p.down])
    gather = Gather(p, rows, rows_send, rows_recv)
    stage.wait()
    gather.begin()

    def lift(j):
        lanes = lanes_at(j * 256, 256)
        slope[:, lanes] = nt(grads[...], down_full[lanes, :]).astype(BF)

    def hide(dy):
        at = pair_rows(p, dy)

        def body(j):
            lanes = lanes_at(j * 256, 256)
            v = nn(rows[at, :], up_full[:, lanes]) + up_shift[:, lanes]
            square = v * v
            t = jnp.tanh(v * (0.7978845608028654 + 0.7978845608028654 * 0.044715 * square))
            half = 0.5 + 0.5 * t
            act[at, lanes] = (v * half).astype(BF)
            bend = half + v * (1.0 - t * t) * (
                0.5 * 0.7978845608028654 + 0.5 * 0.7978845608028654 * 3.0 * 0.044715 * square
            )
            slope[at, lanes] = (slope[at, lanes].astype(F32) * bend).astype(BF)

        loop(UNITS // 256, body)

    def back(dy):
        at = pair_rows(p, dy)

        def put(lanes, value):
            part[at, lanes] = value.astype(BF)

        wide_product(put, lambda lanes: nt(slope[at, :], up_full[lanes, :]))

    def forth(dy):
        at = pair_rows(p, dy)

        def put(lanes, value):
            part_out[at, lanes] = value.astype(BF)

        wide_product(put, lambda lanes: nn(act[at, :], down_full[:, lanes]))

    load_down.wait()
    load_grads.wait()
    loop(UNITS // 256, lift)
    load_up.wait()
    expand = pl.ds(WIDTH, LANES)
    up_full[expand, :] = (SCALE * up_full[expand, :].astype(F32)).astype(BF)
    scatter = Scatter(p, part, sib_in, relay, near, s_send, s_recv)
    scatter_out = Scatter(p, part_out, sib_in_out, None, None, t_send, t_recv)
    gather.own_pair()
    hide(0)
    gather.near()
    gather.near_pairs()
    hide(1)
    hide(-1)
    gather.far()
    gather.far_pair()
    hide(2)
    back(2)
    scatter.exchange(2)
    back(1)
    scatter.exchange(1)
    scatter.combine(2)
    scatter.relay_out()
    back(-1)
    scatter.exchange(-1)
    scatter.combine(1)
    scatter.near_free(1)
    scatter.combine(-1)
    scatter.near_free(-1)
    back(0)
    scatter.exchange(0)
    forth(2)
    scatter_out.exchange(2)
    scatter.near_rest()
    scatter.combine(0)
    for dy in (1, -1, 0):
        forth(dy)
        scatter_out.exchange(dy)

    def by_unit(j):
        at = lanes_at(j * 256, 256)
        by_shard[at, :] = tn(act[:, at], grads[:, pl.ds(WIDTH, LANES)]).astype(BF)
        by_shard[lanes_at(UNITS + j * 256, 256), :] = (
            SCALE * tn(slope[:, at], rows[:, pl.ds(WIDTH, LANES)])
        ).astype(BF)

    loop(UNITS // 256, by_unit)
    for dy in range(4):
        scatter_out.combine(dy)
    copies = []

    def hand_on(src, start, count):
        copy = pltpu.make_async_copy(src, out_parts.at[pl.ds(start, count)], own_sem.at[4 + len(copies)])
        copy.start()
        copies.append(copy)

    for dy in range(4):
        hand_on(scatter_out.mine(dy), dy * ROWS, ROWS)
    scatter.arrived()
    mask_rows = mask[...].astype(F32)
    side_u[...] = (mask_rows * scatter.total(0, ROWS, pl.ds(WIDTH, LANES))).astype(BF)

    def norm_block(index):
        at = rows_at(index * BLOCK, BLOCK)
        mine = rows_at(p.ring(0, True) * ROWS + index * BLOCK, BLOCK)
        grad = scatter.total(index * BLOCK, BLOCK, pl.ds(0, WIDTH)) + nt(side_u[at, :], up_reduce[...])
        grad = grads[mine, pl.ds(0, WIDTH)].astype(F32) + norm_back(middle[at, :], gain[...], grad)
        grad_out[at, :] = grad
        grad_stage[at, pl.ds(0, WIDTH)] = grad.astype(BF)

    loop(ROWS // BLOCK, norm_block)
    grad_stage[:, pl.ds(WIDTH, LANES)] = (
        mask_rows * (SCALE * nt(grad_stage[:, pl.ds(0, WIDTH)], output_expand[...]))
    ).astype(BF)
    gather.end()
    scatter.end()
    scatter_out.end(0, 4)
    for copy in copies:
        copy.wait()


def feed_call(ins):
    outs = [
        shape(ROWS, WIDTH, kind=F32), shape(ROWS, WIDE), shape(ROWS, LANES), shape(2 * UNITS, LANES),
        shape(4 * ROWS, WIDE),
    ]
    scratch = scatter_scratch()
    return call(
        feed_kernel,
        2,
        ins,
        [IN_VMEM] * 7 + [ANYWHERE] * 3,
        outs,
        [IN_VMEM] * 4 + [ANYWHERE],
        [
            pltpu.VMEM((WIDE, UNITS), BF), pltpu.VMEM((UNITS, WIDE), BF), pltpu.VMEM((GROUP, WIDE), BF),
            *gather_scratch(), pltpu.VMEM((GROUP, UNITS), BF), pltpu.VMEM((GROUP, UNITS), BF), *scratch,
            scratch[0], scratch[1], scratch[4], scratch[5], pltpu.SemaphoreType.DMA((8,)),
        ],
    )


class Reducer:
    def __init__(self, place, source, sib_mark):
        self.p, self.source, self.sib_mark = place, source, sib_mark
        self.m = place.z * 4 + place.x
        self.sent = []

    @staticmethod
    def mates(place):
        m = place.z * 4 + place.x
        mates = []
        for k in range(1, 16):
            other = lax.rem(m + k, 16)
            for core in (0, 1):
                mates.append(place.at(z=lax.div(other, 4), x=lax.rem(other, 4), c=core))
        return mates

    def member(self, k):
        other = lax.rem(self.m + k, 16)
        return other, self.p.at(z=lax.div(other, 4), x=lax.rem(other, 4))

    def push(self, src, dst, send, recv, device):
        copy = remote(src, dst, send, recv, device)
        copy.start()
        self.sent.append(copy)

    def await_at(self, dst, recv):
        remote(dst, dst, self.sib_mark, recv, self.p.sib).wait_recv()

    def close(self):
        for copy in self.sent:
            copy.wait_send()


class ShardSum(Reducer):
    def __init__(self, place, source, refs):
        (
            self.landing, self.total, self.all, self.a_send, self.a_recv, self.c_send, self.c_recv,
        ) = refs
        super().__init__(place, source, self.a_send.at[0])
        self.cut = source.shape[0] // 16

    @staticmethod
    def scratch(count):
        dma = pltpu.SemaphoreType.DMA
        cut = count // 16
        return [
            pltpu.VMEM((16, cut, LANES), BF), pltpu.VMEM((cut, LANES), BF), pltpu.VMEM((count, LANES), BF),
            dma((16,)), dma((16,)), dma((16,)), dma((16,)),
        ]

    def open(self):
        for k in range(1, 16):
            other, device = self.member(k)
            piece = self.source.at[rows_at(other * self.cut, self.cut)]
            self.push(piece, self.landing.at[k], self.a_send.at[k], self.a_recv.at[k], device)

    def spread(self):
        p = self.p
        total = self.source[rows_at(self.m * self.cut, self.cut), :].astype(F32)
        for k in range(1, 16):
            self.await_at(self.landing.at[k], self.a_recv.at[k])
            total = total + self.landing[k].astype(F32)
        self.total[...] = total.astype(BF)
        mine = self.all.at[rows_at(self.m * self.cut, self.cut)]
        mark = self.c_recv.at[self.m]
        for n in range(1, 16):
            device = p.at(
                z=lax.rem(p.z + n // 4, 4), xl=lax.rem(p.xl + n // 2 % 2, 2), g=p.c, c=lax.rem(p.c + n % 2, 2)
            )
            self.push(self.total, mine, self.c_send.at[n], mark, device)
        self.swapped = remote(self.total, mine, self.c_send.at[0], mark, p.at(g=p.c))
        pl.when(p.away)(self.swapped.start)
        pl.when(p.home)(pltpu.make_async_copy(self.total, mine, mark).start)

    def close(self):
        for index in range(16):
            self.await_at(self.all.at[pl.ds(index * self.cut, self.cut)], self.c_recv.at[index])
        super().close()
        pl.when(self.p.away)(self.swapped.wait_send)


class WholeSum(Reducer):
    def __init__(self, place, source, refs):
        (
            self.sib_in, self.here, self.landing, self.slice_sum, self.bits_in, self.bit_sum, self.all,
            self.b_send, self.b_recv, self.d_send, self.d_recv, self.e_send, self.e_recv, self.f_send, self.f_recv,
            self.g_send, self.g_recv, self.mark,
        ) = refs
        super().__init__(place, source, self.f_send.at[0])
        self.half = source.shape[0] // 2
        self.slice = self.half // 16
        self.bit = self.slice // 4
        self.base = place.c * self.half + self.m * self.slice

    @staticmethod
    def scratch(count):
        dma = pltpu.SemaphoreType.DMA
        half = count // 2
        piece = half // 16
        return [
            pltpu.VMEM((half, LANES), BF), pltpu.VMEM((half, LANES), BF), pltpu.VMEM((16, piece, LANES), BF),
            pltpu.VMEM((piece, LANES), BF), pltpu.VMEM((4, piece // 4, LANES), BF), pltpu.VMEM((piece // 4, LANES), BF),
            pltpu.VMEM((count, LANES), BF),
            dma((16,)), dma((16,)), dma((4,)), dma((4,)), dma((4,)), dma((4,)), dma((2,)), dma((2,)),
            dma((16,)), dma((16,)), dma((1,)),
        ]

    def open(self):
        there = rows_at((1 - self.p.c) * self.half, self.half)
        self.push(self.source.at[there], self.sib_in, self.f_send.at[0], self.f_recv.at[0], self.p.sib)

    def halves(self):
        self.await_at(self.sib_in, self.f_recv.at[0])

        def body(index):
            at = rows_at(index * 128, 128)
            mine = self.source[rows_at(self.p.c * self.half + index * 128, 128), :].astype(F32)
            self.here[at, :] = (mine + self.sib_in[at, :].astype(F32)).astype(BF)

        loop(self.half // 128, body)
        for k in range(1, 16):
            other, device = self.member(k)
            piece = self.here.at[rows_at(other * self.slice, self.slice)]
            self.push(piece, self.landing.at[k], self.b_send.at[k], self.b_recv.at[k], device)

    def slices(self):
        total = self.here[rows_at(self.m * self.slice, self.slice), :].astype(F32)
        for k in range(1, 16):
            self.await_at(self.landing.at[k], self.b_recv.at[k])
            total = total + self.landing[k].astype(F32)
        self.slice_sum[...] = total.astype(BF)
        for dy in (2, 1, 3):
            other = lax.rem(self.p.y + dy, 4)
            piece = self.slice_sum.at[rows_at(other * self.bit, self.bit)]
            self.push(piece, self.bits_in.at[dy], self.d_send.at[dy], self.d_recv.at[dy], self.p.at(y=other))

    def bits(self):
        total = self.slice_sum[rows_at(self.p.y * self.bit, self.bit), :].astype(F32)
        for dy in (1, 3, 2):
            self.await_at(self.bits_in.at[dy], self.d_recv.at[dy])
            total = total + self.bits_in[dy].astype(F32)
        self.bit_sum[...] = total.astype(BF)
        own = self.all.at[rows_at(self.base + self.p.y * self.bit, self.bit)]
        self.placed = pltpu.make_async_copy(self.bit_sum, own, self.mark.at[0])
        self.placed.start()
        for dy in (2, 1, 3):
            device = self.p.at(y=lax.rem(self.p.y + dy, 4))
            self.push(self.bit_sum, own, self.e_send.at[dy], self.e_recv.at[dy], device)

    def slices_back(self):
        self.placed.wait()
        for dy in (1, 3, 2):
            source = lax.rem(self.p.y + 4 - dy, 4)
            self.await_at(self.all.at[rows_at(self.base + source * self.bit, self.bit)], self.e_recv.at[dy])
        own = self.all.at[rows_at(self.base, self.slice)]
        for k in range(1, 16):
            self.push(own, own, self.g_send.at[k], self.g_recv.at[k], self.member(k)[1])

    def halves_back(self):
        for k in range(1, 16):
            source = lax.rem(self.m + 16 - k, 16)
            landing = self.all.at[rows_at(self.p.c * self.half + source * self.slice, self.slice)]
            self.await_at(landing, self.g_recv.at[k])
        half = self.all.at[rows_at(self.p.c * self.half, self.half)]
        self.push(half, half, self.f_send.at[1], self.f_recv.at[1], self.p.sib)

    def close(self):
        self.await_at(self.all.at[rows_at((1 - self.p.c) * self.half, self.half)], self.f_recv.at[1])
        super().close()


def back_kernel(
    grad_stage, output_full, qkv, tokens, gain, mask, cotangent, down_shift, down_expand, joined_reduce, normed, side_q,
    grad, middle, context, second_normed, side_u, side_o, shard_early,
    joined_weights, out_parts, probs_in,
    block_out, input_grad, shard_done, shard_rest, whole_done, whole_rest,
    rows, rows_send, rows_recv, probs, key_grad, value_grad, joined_grad, result, block_own, joined_full, whole_early,
    shard_late, whole_late, side_part, side_in, side_send, side_recv,
    part, sib_in, relay, near, s_send, s_recv, parts, relay_out, near_out, t_send, t_recv, swap_send, swap_recv, own_sem,
    *refs,
):
    p = Place()
    own_rows = rows_at(p.ring(0, True) * ROWS, ROWS)
    loads = []

    def load(src, dst):
        copy = pltpu.make_async_copy(src, dst, own_sem.at[len(loads)])
        copy.start()
        loads.append(copy)

    load(grad_stage, rows.at[own_rows])
    for dy in (0, 1, -1, 2):
        at = pair_rows(p, dy)
        load(probs_in.at[:, at], probs.at[:, at])
    load(out_parts, parts)
    load(joined_weights, joined_full)
    greet(p.ring_mates() + Reducer.mates(p))
    gather = Gather(p, rows, rows_send, rows_recv)
    loads[0].wait()
    gather.begin()
    swap = Swap(p, [(block_own, block_out), (result, input_grad)], swap_send, swap_recv)
    early_shard = ShardSum(p, shard_early, refs[0:7])
    early_whole = WholeSum(p, whole_early, refs[7:25])
    late_shard = ShardSum(p, shard_late, refs[25:32])
    late_whole = WholeSum(p, whole_late, refs[32:50])
    early_shard.open()

    def early_column(j):
        lanes = lanes_at(j * 256, 256)
        whole_early[lanes, :] = tn(second_normed[:, lanes], side_u[...]).astype(BF)
        whole_early[lanes_at(WIDTH + j * 256, 256), :] = (SCALE * tn(grad_stage[:, lanes], side_o[...])).astype(BF)

    loop(WIDTH // 256, early_column)
    early_whole.open()

    def back(dy):
        base = lax.rem(p.y + dy + 4, 4) * PAIR

        def body(index):
            at = rows_at(base + index * ROWS, ROWS)
            context_grad = nt(rows[at, :], output_full[...]).astype(BF)
            for head in range(2):
                start = head * 3 * HEAD
                query = qkv[at, start : start + HEAD]
                key = qkv[:, start + HEAD : start + 2 * HEAD]
                value = qkv[:, start + 2 * HEAD : start + 3 * HEAD]
                own = context_grad[:, head * HEAD : (head + 1) * HEAD]
                weights = probs[head, at, :]
                mean = jnp.sum(
                    own.astype(F32) * context[at, head * HEAD : (head + 1) * HEAD].astype(F32), axis=-1, keepdims=True
                )
                score_grad = weights * (nt(own, value) - mean).astype(BF)
                joined_grad[at, start : start + HEAD] = (nn(score_grad, key) * (1.0 / math.sqrt(HEAD))).astype(BF)
                value_grad[head] = value_grad[head] + tn(own, weights)
                key_grad[head] = key_grad[head] + tn(query, score_grad)

        loop(2, body)

    value_grad[...] = jnp.zeros_like(value_grad)
    key_grad[...] = jnp.zeros_like(key_grad)
    scatter_out = Scatter(p, parts, None, relay_out, near_out, t_send, t_recv, lambda dy: dy % 4 * ROWS)
    gather.own_pair()
    loads[1].wait()
    back(0)
    early_whole.halves()
    loads[5].wait()
    gather.near()
    scatter_out.relay_out()
    scatter_out.near_free(1)
    scatter_out.near_free(-1)
    gather.near_pairs()
    loads[2].wait()
    back(1)
    gather.far()
    early_shard.spread()
    loads[3].wait()
    back(-1)
    early_whole.slices()
    gather.far_pair()
    scatter_out.near_rest()
    loads[4].wait()
    back(2)
    early_whole.bits()
    turn = identity()
    for head in range(2):
        start = head * 3 * HEAD
        joined_grad[:, start + HEAD : start + 2 * HEAD] = tn(
            (key_grad[head] * (1.0 / math.sqrt(HEAD))).astype(BF), turn
        ).astype(BF)
        joined_grad[:, start + 2 * HEAD : start + 3 * HEAD] = tn(value_grad[head].astype(BF), turn).astype(BF)
    loads[6].wait()

    def product(dy):
        at = pair_rows(p, dy)

        def body(j):
            lanes = lanes_at(j * 512, 512)
            part[at, lanes] = nt(joined_grad[at, :], joined_full[lanes, :]).astype(BF)

        loop(WIDTH // 512, body)

    scatter = Scatter(p, part, sib_in, relay, near, s_send, s_recv)
    product(2)
    scatter.exchange(2)
    side_part[...] = nt(joined_grad[...], joined_full[pl.ds(WIDTH, LANES), :]).astype(BF)
    side_copies = []
    for k in range(1, 8):
        dy, same = k // 2, k % 2 == 0
        y, core = lax.rem(p.y + dy, 4), (p.c if same else 1 - p.c)
        copy = remote(
            side_part.at[rows_at((y * 2 + core) * ROWS, ROWS)], side_in.at[k], side_send.at[k], side_recv.at[k],
            p.at(y=y, c=core),
        )
        copy.start()
        side_copies.append(copy)
    scatter.combine(2)
    scatter.relay_out()
    product(1)
    scatter.exchange(1)
    product(-1)
    scatter.exchange(-1)
    scatter.combine(1)
    scatter.near_free(1)
    scatter.combine(-1)
    scatter.near_free(-1)
    mask_rows = mask[...].astype(F32)
    side_total = side_part[own_rows, :].astype(F32)
    for k in range(1, 8):
        side_copies[k - 1].wait_recv()
        side_total = side_total + side_in[k].astype(F32)
    side_part[own_rows, :] = (mask_rows * side_total).astype(BF)
    scatter_out.arrived()
    side_d = (mask_rows * scatter_out.total(0, ROWS, pl.ds(WIDTH, LANES))).astype(BF)

    def late_column(j):
        lanes = lanes_at(j * 256, 256)
        whole_late[lanes, :] = (SCALE * tn(cotangent[:, lanes], side_d)).astype(BF)
        whole_late[lanes_at(WIDTH + j * 256, 256), :] = tn(normed[:, lanes], side_part[own_rows, :]).astype(BF)

    loop(WIDTH // 256, late_column)
    late_whole.open()
    product(0)
    scatter.exchange(0)
    scatter.near_rest()
    late_whole.halves()
    scatter.combine(0)
    shard_late[pl.ds(0, CTX), :] = tn(context[...], rows[:, pl.ds(WIDTH, LANES)]).astype(BF)

    def late_lane(j):
        lanes = lanes_at(j * 256, 256)
        shard_late[lanes_at(CTX + j * 256, 256), :] = (SCALE * tn(joined_grad[:, lanes], side_q[...])).astype(BF)

    loop(QKV // 256, late_lane)
    late_shard.open()
    early_whole.slices_back()

    def add_tile(j):
        lanes = lanes_at(j * 256, 256)
        block_own[:, lanes] = (
            middle[:, lanes]
            + scatter_out.total(0, ROWS, lanes)
            + down_shift[:, lanes]
            + SCALE * nn(side_d, down_expand[:, lanes])
        ).astype(BF)

    loop(WIDTH // 256, add_tile)
    swap.begin(0)
    late_whole.slices()
    late_shard.spread()
    late_whole.bits()
    late_whole.slices_back()
    scatter.arrived()

    def norm_block(index):
        at = rows_at(index * BLOCK, BLOCK)
        side = side_part[rows_at(p.ring(0, True) * ROWS + index * BLOCK, BLOCK), :]
        back_grad = scatter.total(index * BLOCK, BLOCK, pl.ds(0, WIDTH)) + nt(side, joined_reduce[...])
        result[at, :] = (grad[at, :] + norm_back(tokens[at, :].astype(F32), gain[...], back_grad)).astype(BF)

    loop(ROWS // BLOCK, norm_block)
    swap.begin(1)
    early_whole.halves_back()
    late_whole.halves_back()
    early_shard.close()
    late_shard.close()
    early_whole.close()
    late_whole.close()
    shard_done[...] = early_shard.all[...]
    shard_rest[...] = late_shard.all[...]
    whole_done[...] = early_whole.all[...]
    whole_rest[...] = late_whole.all[...]
    gather.end()
    scatter.end()
    scatter_out.end(4)
    for copy in side_copies:
        copy.wait_send()
    swap.arrived(0)
    swap.arrived(1)
    swap.end()


def back_call(ins):
    outs = [
        shape(ROWS, WIDTH), shape(ROWS, WIDTH), shape(2 * UNITS, LANES), shape(CTX + QKV, LANES),
        shape(2 * WIDTH, LANES), shape(2 * WIDTH, LANES),
    ]
    dma = pltpu.SemaphoreType.DMA
    scratch = scatter_scratch()
    return call(
        back_kernel,
        3,
        ins,
        [IN_VMEM] * 19 + [ANYWHERE] * 3,
        outs,
        [ANYWHERE] * 2 + [IN_VMEM] * 4,
        [
            *gather_scratch(), pltpu.VMEM((2, GROUP, GROUP), BF), pltpu.VMEM((2, HEAD, GROUP), F32),
            pltpu.VMEM((2, HEAD, GROUP), F32), pltpu.VMEM((GROUP, QKV), BF), pltpu.VMEM((ROWS, WIDTH), BF),
            pltpu.VMEM((ROWS, WIDTH), BF), pltpu.VMEM((WIDE, QKV), BF), pltpu.VMEM((2 * WIDTH, LANES), BF),
            pltpu.VMEM((CTX + QKV, LANES), BF), pltpu.VMEM((2 * WIDTH, LANES), BF), pltpu.VMEM((GROUP, LANES), BF),
            pltpu.VMEM((8, ROWS, LANES), BF), dma((8,)), dma((8,)), *scatter_scratch(WIDTH),
            pltpu.VMEM((4 * ROWS, WIDE), BF), *scratch[2:], *swap_marks(2), dma((7,)),
            *ShardSum.scratch(2 * UNITS), *WholeSum.scratch(2 * WIDTH), *ShardSum.scratch(CTX + QKV),
            *WholeSum.scratch(2 * WIDTH),
        ],
    )


def finish_kernel(
    shard_early, whole_early, shard_late, whole_late, block_in, grad_in,
    block_out, input_grad, qkv_a, qkv_b, out_a, out_b, up_a, up_b, down_a, down_b,
    block_here, grad_here, a_here, b_here, out_sem,
):
    turn = identity()
    copies = []

    def send(src, dst):
        copy = pltpu.make_async_copy(src, dst, out_sem.at[len(copies)])
        copy.start()
        copies.append(copy)

    def turned(source, start, base, count):
        def body(j):
            b_here[:, lanes_at(base + j * 256, 256)] = nt(turn, source[lanes_at(start + j * 256, 256), :])

        loop(count // 256, body)

    def widened(source, start, here, base, count, step):
        def body(index):
            here[rows_at(base + index * step, step), :] = source[rows_at(start + index * step, step), :].astype(F32)

        loop(count // step, body)

    widened(block_in, 0, block_here, 0, ROWS, BLOCK)
    send(block_here, block_out)
    widened(grad_in, 0, grad_here, 0, ROWS, BLOCK)
    send(grad_here, input_grad)
    base = 0
    for source, start, out, count in (
        (whole_early, 0, up_a, WIDTH),
        (whole_late, WIDTH, qkv_a, WIDTH),
        (shard_early, 0, down_a, UNITS),
        (shard_late, 0, out_a, CTX),
    ):
        widened(source, start, a_here, base, count, 256)
        send(a_here.at[pl.ds(base, count)], out.at[0])
        base += count
    base = 0
    for source, start, out, count in (
        (whole_early, WIDTH, out_b, WIDTH),
        (whole_late, 0, down_b, WIDTH),
        (shard_early, UNITS, up_b, UNITS),
        (shard_late, CTX, qkv_b, QKV),
    ):
        turned(source, start, base, count)
        send(b_here.at[:, pl.ds(base, count)], out.at[0])
        base += count
    for copy in copies:
        copy.wait()


def finish_call(ins):
    return pl.pallas_call(
        finish_kernel,
        name="finish_kernel",
        out_shape=[
            shape(ROWS, WIDTH, kind=F32), shape(ROWS, WIDTH, kind=F32), shape(1, WIDTH, LANES, kind=F32),
            shape(1, LANES, QKV, kind=F32), shape(1, CTX, LANES, kind=F32), shape(1, LANES, WIDTH, kind=F32),
            shape(1, WIDTH, LANES, kind=F32), shape(1, LANES, UNITS, kind=F32), shape(1, UNITS, LANES, kind=F32),
            shape(1, LANES, WIDTH, kind=F32),
        ],
        in_specs=[IN_VMEM] * 6,
        out_specs=[ANYWHERE] * 10,
        scratch_shapes=[
            pltpu.VMEM((ROWS, WIDTH), F32), pltpu.VMEM((ROWS, WIDTH), F32),
            pltpu.VMEM((2 * WIDTH + UNITS + CTX, LANES), F32), pltpu.VMEM((LANES, 2 * WIDTH + UNITS + QKV), F32),
            pltpu.SemaphoreType.DMA((10,)),
        ],
        compiler_params=pltpu.CompilerParams(vmem_limit_bytes=VMEM_LIMIT),
    )(*ins)


def shards(
    tokens, lengths, order, sequence_adapter, first_norm_gain, first_norm_bias, second_norm_gain, second_norm_bias,
    joined_matrix, joined_offset_bias, output_matrix, output_offset_bias, up_matrix, up_offset_bias, down_matrix,
    down_offset_bias, joined_adapter_reduce, joined_adapter_expand, output_adapter_reduce, output_adapter_expand,
    up_adapter_reduce, up_adapter_expand, down_adapter_reduce, down_adapter_expand, cotangent,
):
    (
        normed, middle, side_o, context, qkv, mask_own, probs, side_q, normed_first, gathered_grad, cot_own,
        joined_full, output_full, up_full, down_full, tokens_own, up_shift_own,
    ) = forward_call(
        (
            first_norm_gain, first_norm_bias, joined_adapter_reduce[0], down_adapter_expand[0],
            joined_adapter_expand[0], joined_offset_bias, order, output_adapter_expand[0], output_offset_bias,
            second_norm_gain, second_norm_bias, up_adapter_reduce[0], lengths, sequence_adapter,
            tokens, cotangent, up_offset_bias, joined_matrix[0], output_matrix[0], output_adapter_reduce[0],
            up_matrix[0], up_adapter_expand[0], down_matrix[0], down_adapter_reduce[0],
        )
    )
    grad, grad_stage, side_u, shard_feed, out_parts = feed_call(
        (
            normed, middle, up_shift_own, mask_own, second_norm_gain, up_adapter_reduce[0],
            output_adapter_expand[0], gathered_grad, up_full, down_full,
        )
    )
    block_own, input_own, shard_early, shard_late, whole_early, whole_late = back_call(
        (
            grad_stage, output_full, qkv, tokens_own, first_norm_gain, mask_own, cot_own, down_offset_bias,
            down_adapter_expand[0], joined_adapter_reduce[0], normed_first, side_q, grad, middle, context,
            normed, side_u, side_o, shard_feed, joined_full, out_parts, probs,
        )
    )
    return tuple(finish_call((shard_early, whole_early, shard_late, whole_late, block_own, input_own)))


def solution(mesh):
    spread = P(("dp", "tensor"), None)
    by_dp = P("dp", None)
    rows = P(None, "dp", "tensor")
    cols = P(None, "tensor", "dp")
    last = P(None, None, "tensor")
    middle = P(None, "tensor", None)
    vector = P(None, "tensor")
    return jax.shard_map(
        shards,
        mesh=mesh,
        in_specs=(
            spread, by_dp, by_dp, by_dp, P(), P(), P(), P(), rows, vector, cols, P(), rows, vector, cols, P(),
            P(), last, middle, P(), P(), last, middle, P(), spread,
        ),
        out_specs=(spread, spread, P(), last, middle, P(), P(), last, middle, P()),
        check_vma=False,
    )
```

```python
import functools
import math

import jax
import jax.numpy as jnp
from jax import lax
from jax.experimental import pallas as pl
from jax.experimental.pallas import tpu as pltpu
from jax.sharding import PartitionSpec as P

HEAD = 128
WIDTH = 2048
LANES = 128
WIDE = WIDTH + LANES
ROWS = 160
HALF = ROWS // 2
PAIR = 2 * ROWS
GROUP = 8 * ROWS
QKV = 768
UNITS = 1024
CTX = 256
BLOCK = 32
SCALE = 0.5
EPS = 1e-05
MASKED = -1e30
LOG2E = 1.4426950408889634
VMEM_LIMIT = 60 * 2**20
BF = jnp.bfloat16
F32 = jnp.float32
BY_MESH = pl.DeviceIdType.MESH
ANYWHERE = pl.BlockSpec(memory_space=pl.ANY)
IN_VMEM = pl.BlockSpec(memory_space=pltpu.VMEM)
IN_SMEM = pl.BlockSpec(memory_space=pltpu.SMEM)


def nn(left, right):
    return jnp.dot(left, right, preferred_element_type=F32)


def nt(left, right):
    return lax.dot_general(left, right, (((1,), (1,)), ((), ())), preferred_element_type=F32)


def tn(left, right):
    return lax.dot_general(left, right, (((0,), (0,)), ((), ())), preferred_element_type=F32)


def rows_at(start, size):
    return pl.ds(pl.multiple_of(start, 16), size)


def lanes_at(start, size):
    return pl.ds(pl.multiple_of(start, 128), size)


def loop(count, body):
    def step(index, carry):
        body(index)
        return carry

    lax.fori_loop(0, count, step, 0)


class Place:
    def __init__(self):
        dp = lax.axis_index("dp")
        tensor = lax.axis_index("tensor")
        self.dp = dp
        self.z = lax.div(dp, 4)
        self.xl = lax.rem(lax.div(dp, 2), 2)
        self.c = lax.rem(dp, 2)
        self.y = lax.div(tensor, 2)
        self.g = lax.rem(tensor, 2)
        self.x = self.g * 2 + self.xl
        self.sib = self.at(c=1 - self.c)
        self.up = self.at(y=lax.rem(self.y + 1, 4))
        self.down = self.at(y=lax.rem(self.y + 3, 4))
        self.z_up = self.at(z=lax.rem(self.z + 1, 4))
        self.z_down = self.at(z=lax.rem(self.z + 3, 4))
        self.partner = self.at(g=self.c, c=self.g)
        self.home = self.c == self.g
        self.away = self.c != self.g

    def at(self, z=None, x=None, xl=None, c=None, y=None, g=None):
        z = self.z if z is None else z
        c = self.c if c is None else c
        y = self.y if y is None else y
        if x is None:
            xl = self.xl if xl is None else xl
            g = self.g if g is None else g
        else:
            xl = lax.rem(x, 2)
            g = lax.div(x, 2)
        return (z * 4 + xl * 2 + c, y * 2 + g)

    def in_row(self, dx, core):
        return self.at(x=lax.rem(self.x + dx, 4), c=core)

    def row_mates(self):
        return [self.in_row(dx, core) for dx in (1, 2, 3) for core in (0, 1)]

    def column_mates(self):
        return [self.at(z=lax.rem(self.z + dz, 4), c=core) for dz in (1, 2, 3) for core in (0, 1)]

    def ring_mates(self):
        mates = [self.sib]
        for dy in (1, 2, 3):
            y = lax.rem(self.y + dy, 4)
            mates += [self.at(y=y), self.at(y=y, c=1 - self.c)]
        return mates

    def ring(self, dy, same):
        return lax.rem(self.y + dy + 4, 4) * 2 + (self.c if same else 1 - self.c)


def greet(devices):
    barrier = pltpu.get_barrier_semaphore()
    for device in devices:
        pl.semaphore_signal(barrier, 1, device_id=device, device_id_type=BY_MESH)
    pl.semaphore_wait(barrier, len(devices))


def remote(src, dst, send, recv, device):
    return pltpu.make_async_remote_copy(
        src_ref=src, dst_ref=dst, send_sem=send, recv_sem=recv, device_id=device, device_id_type=BY_MESH
    )


class Gather:
    SENDS = (
        (0, True, None),
        (0, True, None),
        (0, True, None),
        (-1, True, 0),
        (1, True, 1),
        (-1, True, None),
        (1, True, None),
        (2, True, 0),
        (2, True, 1),
    )
    LANDS = (
        (0, False, None),
        (-1, True, None),
        (1, True, None),
        (2, True, 0),
        (2, True, 1),
        (-1, False, None),
        (1, False, None),
        (2, False, 0),
        (2, False, 1),
    )

    def __init__(self, place, buf, send, recv):
        self.place, self.buf, self.send, self.recv = place, buf, send, recv
        p = place
        self.to = (p.sib, p.up, p.down, p.up, p.down, p.sib, p.sib, p.sib, p.sib)

    def piece(self, what):
        dy, same, half = what
        start = self.place.ring(dy, same) * ROWS
        if half is None:
            return self.buf.at[rows_at(start, ROWS)]
        return self.buf.at[rows_at(start + half * HALF, HALF)]

    def copy(self, i):
        piece = self.piece(self.SENDS[i])
        return remote(piece, piece, self.send.at[i], self.recv.at[i], self.to[i])

    def landed(self, i):
        piece = self.piece(self.LANDS[i])
        remote(piece, piece, self.send.at[i], self.recv.at[i], self.to[i]).wait_recv()

    def begin(self):
        for i in (1, 2, 0):
            self.copy(i).start()

    def near(self):
        self.landed(1)
        self.copy(3).start()
        self.copy(5).start()
        self.landed(2)
        self.copy(4).start()
        self.copy(6).start()

    def far(self):
        self.landed(3)
        self.copy(7).start()
        self.landed(4)
        self.copy(8).start()

    def own_pair(self):
        self.landed(0)

    def near_pairs(self):
        self.landed(5)
        self.landed(6)

    def far_pair(self):
        self.landed(7)
        self.landed(8)

    def end(self):
        for i in range(9):
            self.copy(i).wait_send()


class Scatter:
    def __init__(self, place, part, sib_in, relay, near, send, recv, start=None):
        self.place, self.part, self.sib_in, self.relay, self.near = place, part, sib_in, relay, near
        self.send, self.recv = send, recv
        self.start = start or (lambda dy: place.ring(dy, True) * ROWS)

    def mine(self, dy, half=None):
        start = self.start(dy)
        if half is None:
            return self.part.at[rows_at(start, ROWS)]
        return self.part.at[rows_at(start + half * HALF, HALF)]

    def others(self, dy):
        return self.part.at[rows_at(self.place.ring(dy, False) * ROWS, ROWS)]

    def copy(self, i):
        p = self.place
        if i < 4:
            src, dst, to = self.others(i), self.sib_in.at[i], p.sib
        elif i == 4:
            src, dst, to = self.mine(2, 0), self.relay.at[0], p.up
        elif i == 5:
            src, dst, to = self.mine(2, 1), self.relay.at[1], p.down
        elif i == 6:
            src, dst, to = self.mine(1, 1), self.near.at[0, pl.ds(HALF, HALF)], p.up
        elif i == 7:
            src, dst, to = self.mine(-1, 0), self.near.at[1, pl.ds(0, HALF)], p.down
        elif i == 8:
            src, dst, to = self.mine(1, 0), self.near.at[0, pl.ds(0, HALF)], p.up
        else:
            src, dst, to = self.mine(-1, 1), self.near.at[1, pl.ds(HALF, HALF)], p.down
        return remote(src, dst, self.send.at[i], self.recv.at[i], to)

    def exchange(self, dy):
        self.copy(dy % 4).start()

    def combine(self, dy):
        self.copy(dy % 4).wait_recv()
        add_rows(self.part, self.start(dy), self.sib_in.at[dy % 4], 0, ROWS)

    def relay_out(self):
        self.copy(4).start()
        self.copy(5).start()

    def near_free(self, dy):
        self.copy(6 if dy == 1 else 7).start()

    def near_rest(self):
        self.copy(4).wait_recv()
        add_rows(self.part, self.start(1), self.relay.at[0], 0, HALF)
        self.copy(8).start()
        self.copy(5).wait_recv()
        add_rows(self.part, self.start(-1) + HALF, self.relay.at[1], 0, HALF)
        self.copy(9).start()

    def arrived(self):
        for i in (6, 7, 8, 9):
            self.copy(i).wait_recv()

    def total(self, start, size, lanes):
        own = self.part[rows_at(self.start(0) + start, size), lanes].astype(F32)
        return (
            own
            + self.near[0, rows_at(start, size), lanes].astype(F32)
            + self.near[1, rows_at(start, size), lanes].astype(F32)
        )

    def end(self, first=0, last=10):
        for i in range(first, last):
            self.copy(i).wait_send()


def scatter_scratch(width=WIDE):
    return [
        pltpu.VMEM((GROUP, width), BF),
        pltpu.VMEM((4, ROWS, width), BF),
        pltpu.VMEM((2, HALF, width), BF),
        pltpu.VMEM((2, ROWS, width), BF),
        pltpu.SemaphoreType.DMA((10,)),
        pltpu.SemaphoreType.DMA((10,)),
    ]


def gather_scratch():
    return [pltpu.VMEM((GROUP, WIDE), BF), pltpu.SemaphoreType.DMA((9,)), pltpu.SemaphoreType.DMA((9,))]


def add_rows(dst, start, src, src_start, count):
    def body(index):
        at = rows_at(start + index * 16, 16)
        dst[at, :] = (dst[at, :].astype(F32) + src[rows_at(src_start + index * 16, 16), :].astype(F32)).astype(BF)

    loop(count // 16, body)


class Weights:
    def __init__(self, place, piece, full, by_rows, cut, send, recv):
        self.place, self.piece, self.full, self.by_rows = place, piece, full, by_rows
        self.send, self.recv = send, recv
        size = piece.shape[1] if by_rows else piece.shape[0]
        self.parts = (pl.ds(0, cut), pl.ds(cut, size - cut))

    def source(self, half):
        part = self.parts[half]
        return self.piece.at[:, part] if self.by_rows else self.piece.at[part, :]

    def slot(self, index, count, half):
        span = lanes_at(index * 128, count * 128)
        part = self.parts[half]
        return self.full.at[span, part] if self.by_rows else self.full.at[part, span]

    def column(self, dz):
        return lax.rem(self.place.z + dz, 4)

    def first(self):
        p = self.place
        marks = (self.recv.at[p.xl * 2 + p.c], self.recv.at[4 + p.z * 2 + p.c])
        slots = (self.slot(p.dp, 1, 0), self.slot(p.dp, 1, 1))
        for d in (2, 1, 3):
            remote(self.source(0), slots[0], self.send.at[d], marks[0], p.in_row(d, p.g)).start()
            remote(self.source(1), slots[1], self.send.at[4 + d], marks[1], p.at(z=self.column(d), c=p.g)).start()

        @pl.when(p.home)
        def _():
            for half in range(2):
                pltpu.make_async_copy(self.source(half), slots[half], marks[half]).start()

        @pl.when(p.away)
        def _():
            for half in range(2):
                remote(self.source(half), slots[half], self.send.at[4 * half], marks[half], p.sib).start()

    def landed(self, slot, mark):
        remote(slot, slot, self.send.at[0], self.recv.at[mark], self.place.sib).wait_recv()

    def along_z(self, i):
        p = self.place
        z, first, count, to = (
            (p.z, 0, 4, p.z_up),
            (p.z, 0, 4, p.z_down),
            (self.column(3), 0, 2, p.z_up),
            (self.column(1), 2, 2, p.z_down),
        )[i]
        block = self.slot(z * 4 + first, count, 0)
        return remote(block, block, self.send.at[8 + i], self.recv.at[12 + i], to)

    def along_x(self, z, dx):
        p = self.place
        pair = self.slot(z * 4 + p.xl * 2, 2, 1)
        mark = self.send.at[12 + z * 2 + dx // 2]
        return remote(pair, pair, mark, self.recv.at[16 + p.xl * 4 + z], p.in_row(dx, p.c))

    def second(self):
        p = self.place
        for index in range(4):
            self.landed(self.slot(p.z * 4 + index, 1, 0), index)
        self.along_z(0).start()
        self.along_z(1).start()

        @pl.when(p.home)
        def _():
            for z in range(4):
                for core in range(2):
                    self.landed(self.slot(z * 4 + p.xl * 2 + core, 1, 1), 4 + z * 2 + core)
                self.along_x(z, 1).start()
                self.along_x(z, 3).start()

    def passed_on(self, i):
        p = self.place
        home = 1 - lax.rem(p.c + p.g, 2)
        plus = 1 - lax.rem(p.xl + home, 2)
        z = (1 - plus) * 2 + i
        pair = self.slot(z * 4 + (1 - p.xl) * 2, 2, 1)
        mark = self.recv.at[16 + (1 - p.xl) * 4 + z]
        return remote(pair, pair, self.send.at[20 + i], mark, p.in_row(3 - 2 * plus, p.c))

    def third(self):
        p = self.place
        self.landed(self.slot(self.column(3) * 4, 4, 0), 12)
        self.along_z(2).start()
        self.landed(self.slot(self.column(1) * 4, 4, 0), 13)
        self.along_z(3).start()
        for z in range(4):
            self.landed(self.slot(z * 4 + (1 - p.xl) * 2, 2, 1), 16 + (1 - p.xl) * 4 + z)
        for i in range(2):
            self.passed_on(i).start()

    def arrived(self):
        p = self.place
        self.landed(self.slot(self.column(2) * 4, 2, 0), 14)
        self.landed(self.slot(self.column(2) * 4 + 2, 2, 0), 15)

        @pl.when(p.away)
        def _():
            for z in range(4):
                self.landed(self.slot(z * 4 + p.xl * 2, 2, 1), 16 + p.xl * 4 + z)

    def end(self):
        p = self.place
        for d in (1, 2, 3):
            for half in range(2):
                slot = self.slot(p.dp, 1, half)
                remote(self.source(half), slot, self.send.at[4 * half + d], self.recv.at[0], p.sib).wait_send()
        for i in range(4):
            self.along_z(i).wait_send()
        for i in range(2):
            self.passed_on(i).wait_send()

        @pl.when(p.away)
        def _():
            for half in range(2):
                slot = self.slot(p.dp, 1, half)
                remote(self.source(half), slot, self.send.at[4 * half], self.recv.at[0], p.sib).wait_send()

        @pl.when(p.home)
        def _():
            for z in range(4):
                self.along_x(z, 1).wait_send()
                self.along_x(z, 3).wait_send()


def weight_marks():
    return [pltpu.SemaphoreType.DMA((22,)), pltpu.SemaphoreType.DMA((24,))]


class Swap:
    def __init__(self, place, pairs, send, recv):
        self.place, self.pairs, self.send, self.recv = place, pairs, send, recv

    def begin(self, i):
        src, dst = self.pairs[i]
        p = self.place

        @pl.when(p.home)
        def _():
            pltpu.make_async_copy(src, dst, self.recv.at[i]).start()

        @pl.when(p.away)
        def _():
            remote(src, dst, self.send.at[i], self.recv.at[i], p.partner).start()

    def arrived(self, i):
        src, dst = self.pairs[i]
        remote(src, dst, self.send.at[i], self.recv.at[i], self.place.sib).wait_recv()

    def end(self):
        @pl.when(self.place.away)
        def _():
            for i, (src, dst) in enumerate(self.pairs):
                remote(src, dst, self.send.at[i], self.recv.at[i], self.place.sib).wait_send()


def swap_marks(count):
    return [pltpu.SemaphoreType.DMA((count,)), pltpu.SemaphoreType.DMA((count,))]


def normalise(value):
    mean = jnp.mean(value, axis=-1, keepdims=True)
    center = value - mean
    inverse = lax.rsqrt(jnp.mean(center * center, axis=-1, keepdims=True) + EPS)
    return center * inverse, inverse


def norm_back(value, gain, grad):
    normed, inverse = normalise(value)
    e = grad * gain
    return (e - jnp.mean(e, axis=-1, keepdims=True) - normed * jnp.mean(e * normed, axis=-1, keepdims=True)) * inverse


def pair_rows(place, dy):
    return rows_at(lax.rem(place.y + dy + 4, 4) * PAIR, PAIR)


def wide_product(put, make):
    loop(4, lambda j: put(lanes_at(j * 512, 512), make(lanes_at(j * 512, 512))))
    put(pl.ds(WIDTH, LANES), make(pl.ds(WIDTH, LANES)))


def call(kernel, collective, ins, specs, outs, out_specs, scratch):
    return pl.pallas_call(
        kernel,
        name=kernel.__name__,
        out_shape=outs,
        in_specs=specs,
        out_specs=out_specs,
        scratch_shapes=scratch,
        compiler_params=pltpu.CompilerParams(
            collective_id=collective, has_side_effects=True, vmem_limit_bytes=VMEM_LIMIT
        ),
    )(*ins)


def shape(*dims, kind=BF):
    return jax.ShapeDtypeStruct(dims, kind)


def identity():
    row = lax.broadcasted_iota(jnp.int32, (LANES, LANES), 0)
    return jnp.where(row == lax.broadcasted_iota(jnp.int32, (LANES, LANES), 1), 1.0, 0.0).astype(BF)


def query_info(token_row, start_row):
    token_high = jnp.floor(token_row * (1.0 / 16.0))
    start_high = jnp.floor(start_row * (1.0 / 16.0))
    digit = lax.broadcasted_iota(jnp.int32, (16, GROUP), 0)
    digits = jnp.where(digit == 0, token_high, 0.0)
    digits = jnp.where(digit == 1, token_row - 16.0 * token_high, digits)
    digits = jnp.where(digit == 2, start_high, digits)
    digits = jnp.where(digit == 3, start_row - 16.0 * start_high, digits)
    row = lax.broadcasted_iota(jnp.int32, (16, LANES), 0)
    lane = lax.broadcasted_iota(jnp.int32, (16, LANES), 1)
    worth = jnp.where((row == 0) & (lane == 0) | (row == 2) & (lane == 1), 16.0, 0.0)
    worth = worth + jnp.where((row == 1) & (lane == 0) | (row == 3) & (lane == 1), 1.0, 0.0)
    return tn(digits.astype(BF), worth.astype(BF))


def slope_row(place, head, tokens_row):
    number = (place.ring(0, True) * 2 + head + 1).astype(F32)
    slope = jnp.exp2(jnp.full((1, GROUP), -0.5, F32) * number)
    return slope * LOG2E * tokens_row


def forward_kernel(
    gain, shift, joined_reduce, down_expand, joined_expand, joined_shift, order, output_expand, output_shift,
    second_gain, second_shift, up_reduce, lengths, adapters,
    tokens, cotangent, up_shift, joined_piece, output_piece, output_reduce, up_piece, up_expand, down_piece, down_reduce,
    normed, middle, side_o, context, qkv, mask_own,
    probs_out, side_q, normed_own, gathered_grad, cot_own, joined_full, output_full, up_full, down_full, tokens_own,
    up_shift_own,
    tok_here, aux, aux_here, half_expand, shift_here, joined_here, output_here, info, mask_all, probs,
    rows, rows_send, rows_recv, grads, grads_send, grads_recv, part, sib_in, relay, near, s_send, s_recv,
    w_send, w_recv, o_send, o_recv, u_send, u_recv, d_send, d_recv, swap_send, swap_recv, out_sem, probs_sem,
):
    p = Place()
    greet([p.sib, p.up, p.down] + p.row_mates() + p.column_mates())
    joined = Weights(p, joined_piece, joined_here.at[pl.ds(0, WIDTH)], True, 512, w_send, w_recv)
    output = Weights(p, output_piece, output_here.at[:, pl.ds(0, WIDTH)], False, 160, o_send, o_recv)
    up = Weights(p, up_piece, up_full.at[pl.ds(0, WIDTH)], True, 640, u_send, u_recv)
    down = Weights(p, down_piece, down_full.at[:, pl.ds(0, WIDTH)], False, 640, d_send, d_recv)
    own_rows = rows_at(p.ring(0, True) * ROWS, ROWS)
    their_rows = rows_at((p.y * 2 + p.g) * ROWS, ROWS)
    swap = Swap(
        p,
        [
            (tokens, tok_here),
            (aux, aux_here),
            (half_expand, joined_here.at[pl.ds(WIDTH, LANES)]),
            (joined_shift, shift_here),
            (cotangent, grads.at[their_rows, pl.ds(0, WIDTH)]),
            (output_reduce, output_here.at[:, pl.ds(WIDTH, LANES)]),
            (up_expand, up_full.at[pl.ds(WIDTH, LANES)]),
            (down_reduce, down_full.at[:, pl.ds(WIDTH, LANES)]),
            (up_shift, up_shift_own),
        ],
        swap_send,
        swap_recv,
    )
    joined.first()
    swap.begin(0)
    token = order[...]
    first_end = lengths[0, 0]
    second_end = first_end + lengths[0, 1]
    later = token >= second_end
    late = token >= first_end
    start = jnp.where(later, second_end, jnp.where(late, first_end, 0))
    adapter = jnp.where(later, adapters[0, 2], jnp.where(late, adapters[0, 1], adapters[0, 0]))
    for i, row in enumerate((token, start, adapter)):
        aux[:, pl.ds(i * GROUP, GROUP)] = jnp.broadcast_to(row.astype(F32), (8, GROUP))
    half_expand[...] = (SCALE * joined_expand[...].astype(F32)).astype(BF)
    for i in (1, 2, 3):
        swap.begin(i)
    swap.arrived(1)
    token_row = aux_here[0:1, pl.ds(0, GROUP)]
    info[...] = query_info(token_row, aux_here[0:1, pl.ds(GROUP, GROUP)])
    column = lax.shift_right_logical(lax.broadcasted_iota(jnp.int32, (LANES, GROUP), 0), 4).astype(F32)
    chosen = jnp.where(column == aux_here[0:1, pl.ds(2 * GROUP, GROUP)], 1.0, 0.0).astype(BF)
    mask_all[...] = tn(chosen, identity()).astype(BF)
    mask_own[...] = mask_all[own_rows, :]
    mask_rows = mask_all[own_rows, :].astype(F32)
    joined.second()
    swap.arrived(0)

    def norm_block(index):
        at = rows_at(index * BLOCK, BLOCK)
        value, _ = normalise(tok_here[at, :].astype(F32))
        rows[rows_at(p.ring(0, True) * ROWS + index * BLOCK, BLOCK), pl.ds(0, WIDTH)] = (
            value * gain[...] + shift[...]
        ).astype(BF)

    loop(ROWS // BLOCK, norm_block)
    rows[own_rows, pl.ds(WIDTH, LANES)] = (
        mask_rows * nn(rows[own_rows, pl.ds(0, WIDTH)], joined_reduce[...])
    ).astype(BF)
    gather = Gather(p, rows, rows_send, rows_recv)
    gather_grad = Gather(p, grads, grads_send, grads_recv)
    gather.begin()
    swap.begin(4)
    output.first()
    joined.third()
    up.first()
    down.first()
    for i in range(5, 9):
        swap.begin(i)
    output.second()
    swap.arrived(4)
    grads[own_rows, pl.ds(WIDTH, LANES)] = (
        mask_rows * (SCALE * nt(grads[own_rows, pl.ds(0, WIDTH)], down_expand[...]))
    ).astype(BF)
    copies = [
        pltpu.make_async_copy(tok_here, tokens_own, out_sem.at[0]),
        pltpu.make_async_copy(grads.at[own_rows, pl.ds(0, WIDTH)], cot_own, out_sem.at[1]),
        pltpu.make_async_copy(rows.at[own_rows, pl.ds(0, WIDTH)], normed_own, out_sem.at[2]),
    ]
    for copy in copies:
        copy.start()
    gather.near()
    gather_grad.begin()
    up.second()
    swap.arrived(2)
    swap.arrived(3)
    joined.arrived()
    copies.append(pltpu.make_async_copy(joined_here, joined_full, out_sem.at[3]))
    copies[-1].start()

    def project(dy):
        at = pair_rows(p, dy)

        def body(j):
            lanes = lanes_at(j * 256, 256)
            qkv[at, lanes] = (nn(rows[at, :], joined_here[:, lanes]) + shift_here[:, lanes]).astype(BF)

        loop(QKV // 256, body)

    gather.own_pair()
    project(0)
    gather.near_pairs()
    project(1)
    output.third()
    project(-1)
    gather.far()
    down.second()
    gather.far_pair()
    project(2)
    up.third()
    copies.append(pltpu.make_async_copy(rows.at[:, pl.ds(WIDTH, LANES)], side_q, out_sem.at[4]))
    copies[-1].start()
    output.arrived()
    swap.arrived(5)
    copies.append(pltpu.make_async_copy(output_here, output_full, out_sem.at[5]))
    copies[-1].start()
    probs_copies = []

    def attend(dy, same):
        at = rows_at(p.ring(dy, same) * ROWS, ROWS)
        n = len(probs_copies)
        if n >= 2:
            probs_copies[n - 2].wait()
        query_token = info[at, 0:1]
        query_start = info[at, 1:2]
        allowed = (token_row <= query_token) & (token_row >= query_start)
        for head in range(2):
            first = head * 3 * HEAD
            scores = nt(qkv[at, first : first + HEAD], qkv[:, first + HEAD : first + 2 * HEAD])
            scores = scores * (LOG2E / math.sqrt(HEAD)) + slope_row(p, head, token_row)
            scores = jnp.where(allowed, scores, MASKED)
            top = jnp.max(scores, axis=-1, keepdims=True)
            weights = jnp.exp2(scores - top)
            total = jnp.sum(weights, axis=-1, keepdims=True)
            weights = (weights * (1.0 / total)).astype(BF)
            probs[n % 2, head] = weights
            context[at, head * HEAD : (head + 1) * HEAD] = nn(
                weights, qkv[:, first + 2 * HEAD : first + 3 * HEAD]
            ).astype(BF)
        copy = pltpu.make_async_copy(probs.at[n % 2], probs_out.at[:, at], probs_sem.at[n])
        copy.start()
        probs_copies.append(copy)

        def put(lanes, value):
            part[at, lanes] = value.astype(BF)

        wide_product(put, lambda lanes: nn(context[at, :], output_here[:, lanes]))

    scatter = Scatter(p, part, sib_in, relay, near, s_send, s_recv)
    attend(2, False)
    scatter.exchange(2)
    attend(2, True)
    scatter.combine(2)
    scatter.relay_out()
    gather_grad.near()
    attend(1, False)
    scatter.exchange(1)
    attend(1, True)
    scatter.combine(1)
    scatter.near_free(1)
    down.third()
    attend(-1, False)
    scatter.exchange(-1)
    attend(-1, True)
    scatter.combine(-1)
    scatter.near_free(-1)
    gather_grad.far()
    attend(0, False)
    scatter.exchange(0)
    scatter.near_rest()
    attend(0, True)
    scatter.combine(0)
    gather_grad.own_pair()
    gather_grad.near_pairs()
    gather_grad.far_pair()
    copies.append(pltpu.make_async_copy(grads, gathered_grad, out_sem.at[6]))
    copies[-1].start()
    scatter.arrived()
    side = (mask_rows * scatter.total(0, ROWS, pl.ds(WIDTH, LANES))).astype(BF)
    side_o[...] = side

    def add_tile(j):
        lanes = lanes_at(j * 512, 512)
        middle[:, lanes] = (
            tok_here[:, lanes].astype(F32)
            + scatter.total(0, ROWS, lanes)
            + output_shift[:, lanes]
            + SCALE * nn(side, output_expand[:, lanes])
        )

    loop(4, add_tile)

    def second_block(index):
        at = rows_at(index * BLOCK, BLOCK)
        value, _ = normalise(middle[at, :])
        normed[at, pl.ds(0, WIDTH)] = (value * second_gain[...] + second_shift[...]).astype(BF)

    loop(ROWS // BLOCK, second_block)
    normed[:, pl.ds(WIDTH, LANES)] = (mask_rows * nn(normed[:, pl.ds(0, WIDTH)], up_reduce[...])).astype(BF)
    up.arrived()
    down.arrived()
    for i in range(6, 9):
        swap.arrived(i)
    swap.end()
    for sender in (gather, gather_grad, scatter, joined, output, up, down):
        sender.end()
    for copy in copies + probs_copies[-2:]:
        copy.wait()


def forward_call(ins):
    outs = [
        shape(ROWS, WIDE), shape(ROWS, WIDTH, kind=F32), shape(ROWS, LANES), shape(GROUP, CTX), shape(GROUP, QKV),
        shape(ROWS, LANES),
        shape(2, GROUP, GROUP), shape(GROUP, LANES), shape(ROWS, WIDTH), shape(GROUP, WIDE), shape(ROWS, WIDTH),
        shape(WIDE, QKV), shape(CTX, WIDE), shape(WIDE, UNITS), shape(UNITS, WIDE), shape(ROWS, WIDTH),
        shape(1, UNITS, kind=F32),
    ]
    return call(
        forward_kernel,
        1,
        ins,
        [IN_VMEM] * 12 + [IN_SMEM] * 2 + [ANYWHERE] * 10,
        outs,
        [IN_VMEM] * 6 + [ANYWHERE] * 11,
        [
            pltpu.VMEM((ROWS, WIDTH), BF), pltpu.VMEM((8, 3 * GROUP), F32), pltpu.VMEM((8, 3 * GROUP), F32),
            pltpu.VMEM((LANES, QKV), BF), pltpu.VMEM((1, QKV), F32), pltpu.VMEM((WIDE, QKV), BF),
            pltpu.VMEM((CTX, WIDE), BF), pltpu.VMEM((GROUP, LANES), F32), pltpu.VMEM((GROUP, LANES), BF),
            pltpu.VMEM((2, 2, ROWS, GROUP), BF), *gather_scratch(), *gather_scratch(), *scatter_scratch(),
            *weight_marks(), *weight_marks(), *weight_marks(), *weight_marks(), *swap_marks(9),
            pltpu.SemaphoreType.DMA((7,)), pltpu.SemaphoreType.DMA((8,)),
        ],
    )


class SideSum:
    def __init__(self, place, part, landing, send, recv):
        self.place, self.part, self.landing = place, part, landing
        self.copies = []
        for k in range(1, 8):
            y = lax.rem(place.y + k // 2, 4)
            core = place.c if k % 2 == 0 else 1 - place.c
            piece = part.at[rows_at((y * 2 + core) * ROWS, ROWS)]
            self.copies.append(remote(piece, landing.at[k], send.at[k], recv.at[k], place.at(y=y, c=core)))

    def open(self):
        for copy in self.copies:
            copy.start()

    def total(self):
        total = self.part[rows_at(self.place.ring(0, True) * ROWS, ROWS), :].astype(F32)
        for k in range(1, 8):
            self.copies[k - 1].wait_recv()
            total = total + self.landing[k].astype(F32)
        return total

    def end(self):
        for copy in self.copies:
            copy.wait_send()


def side_scratch():
    dma = pltpu.SemaphoreType.DMA
    return [pltpu.VMEM((GROUP, LANES), BF), pltpu.VMEM((8, ROWS, LANES), BF), dma((8,)), dma((8,))]


def feed_kernel(
    normed, middle, up_shift, mask, gain, up_reduce, output_expand,
    gathered_grad, up_weights, down_weights,
    grad_out, grad_stage, side_u, side_d, by_shard, out_parts,
    up_full, down_full, grads, rows, rows_send, rows_recv, act, slope, part, sib_in, relay, near, s_send, s_recv,
    part_out, sib_in_out, t_send, t_recv, side_part, side_in, side_send, side_recv, own_sem,
):
    p = Place()
    own_rows = rows_at(p.ring(0, True) * ROWS, ROWS)
    stage = pltpu.make_async_copy(normed, rows.at[own_rows], own_sem.at[0])
    stage.start()
    load_down = pltpu.make_async_copy(down_weights, down_full, own_sem.at[1])
    load_down.start()
    load_grads = pltpu.make_async_copy(gathered_grad, grads, own_sem.at[2])
    load_grads.start()
    load_up = pltpu.make_async_copy(up_weights, up_full, own_sem.at[3])
    load_up.start()
    greet(p.ring_mates())
    gather = Gather(p, rows, rows_send, rows_recv)
    stage.wait()
    gather.begin()

    def lift(j):
        lanes = lanes_at(j * 256, 256)
        slope[:, lanes] = nt(grads[...], down_full[lanes, :]).astype(BF)

    def hide(dy):
        at = pair_rows(p, dy)

        def body(j):
            lanes = lanes_at(j * 256, 256)
            v = nn(rows[at, :], up_full[:, lanes]) + up_shift[:, lanes]
            square = v * v
            t = jnp.tanh(v * (0.7978845608028654 + 0.7978845608028654 * 0.044715 * square))
            half = 0.5 + 0.5 * t
            act[at, lanes] = (v * half).astype(BF)
            bend = half + v * (1.0 - t * t) * (
                0.5 * 0.7978845608028654 + 0.5 * 0.7978845608028654 * 3.0 * 0.044715 * square
            )
            slope[at, lanes] = (slope[at, lanes].astype(F32) * bend).astype(BF)

        loop(UNITS // 256, body)

    def back(dy):
        at = pair_rows(p, dy)

        def put(lanes, value):
            part[at, lanes] = value.astype(BF)

        wide_product(put, lambda lanes: nt(slope[at, :], up_full[lanes, :]))

    def forth(dy):
        at = pair_rows(p, dy)

        def body(j):
            lanes = lanes_at(j * 512, 512)
            part_out[at, lanes] = nn(act[at, :], down_full[:, lanes]).astype(BF)

        loop(WIDTH // 512, body)

    load_down.wait()
    load_grads.wait()
    loop(UNITS // 256, lift)
    load_up.wait()
    expand = pl.ds(WIDTH, LANES)
    up_full[expand, :] = (SCALE * up_full[expand, :].astype(F32)).astype(BF)
    scatter = Scatter(p, part, sib_in, relay, near, s_send, s_recv)
    scatter_out = Scatter(p, part_out, sib_in_out, None, None, t_send, t_recv)
    gather.own_pair()
    hide(0)
    gather.near()
    gather.near_pairs()
    hide(1)
    hide(-1)
    gather.far()
    gather.far_pair()
    hide(2)
    back(2)
    scatter.exchange(2)
    back(1)
    scatter.exchange(1)
    scatter.combine(2)
    scatter.relay_out()
    back(-1)
    scatter.exchange(-1)
    scatter.combine(1)
    scatter.near_free(1)
    scatter.combine(-1)
    scatter.near_free(-1)
    back(0)
    scatter.exchange(0)
    forth(2)
    scatter_out.exchange(2)
    scatter.near_rest()
    scatter.combine(0)
    side_part[...] = nn(act[...], down_full[:, pl.ds(WIDTH, LANES)]).astype(BF)
    side = SideSum(p, side_part, side_in, side_send, side_recv)
    side.open()
    for dy in (1, -1, 0):
        forth(dy)
        scatter_out.exchange(dy)

    def by_unit(j):
        at = lanes_at(j * 256, 256)
        by_shard[at, :] = tn(act[:, at], grads[:, pl.ds(WIDTH, LANES)]).astype(BF)
        by_shard[lanes_at(UNITS + j * 256, 256), :] = (
            SCALE * tn(slope[:, at], rows[:, pl.ds(WIDTH, LANES)])
        ).astype(BF)

    loop(UNITS // 256, by_unit)
    mask_rows = mask[...].astype(F32)
    for dy in range(4):
        scatter_out.combine(dy)
    copies = []

    def hand_on(src, start, count):
        copy = pltpu.make_async_copy(src, out_parts.at[pl.ds(start, count)], own_sem.at[4 + len(copies)])
        copy.start()
        copies.append(copy)

    for dy in range(4):
        hand_on(scatter_out.mine(dy), dy * ROWS, ROWS)
    scatter.arrived()
    side_u[...] = (mask_rows * scatter.total(0, ROWS, pl.ds(WIDTH, LANES))).astype(BF)

    def norm_block(index):
        at = rows_at(index * BLOCK, BLOCK)
        mine = rows_at(p.ring(0, True) * ROWS + index * BLOCK, BLOCK)
        grad = scatter.total(index * BLOCK, BLOCK, pl.ds(0, WIDTH)) + nt(side_u[at, :], up_reduce[...])
        grad = grads[mine, pl.ds(0, WIDTH)].astype(F32) + norm_back(middle[at, :], gain[...], grad)
        grad_out[at, :] = grad
        grad_stage[at, pl.ds(0, WIDTH)] = grad.astype(BF)

    loop(ROWS // BLOCK, norm_block)
    grad_stage[:, pl.ds(WIDTH, LANES)] = (
        mask_rows * (SCALE * nt(grad_stage[:, pl.ds(0, WIDTH)], output_expand[...]))
    ).astype(BF)
    side_d[...] = (mask_rows * side.total()).astype(BF)
    gather.end()
    side.end()
    scatter.end()
    scatter_out.end(0, 4)
    for copy in copies:
        copy.wait()


def feed_call(ins):
    outs = [
        shape(ROWS, WIDTH, kind=F32), shape(ROWS, WIDE), shape(ROWS, LANES), shape(ROWS, LANES),
        shape(2 * UNITS, LANES), shape(4 * ROWS, WIDTH),
    ]
    scratch = scatter_scratch(WIDTH)
    return call(
        feed_kernel,
        2,
        ins,
        [IN_VMEM] * 7 + [ANYWHERE] * 3,
        outs,
        [IN_VMEM] * 5 + [ANYWHERE],
        [
            pltpu.VMEM((WIDE, UNITS), BF), pltpu.VMEM((UNITS, WIDE), BF), pltpu.VMEM((GROUP, WIDE), BF),
            *gather_scratch(), pltpu.VMEM((GROUP, UNITS), BF), pltpu.VMEM((GROUP, UNITS), BF), *scatter_scratch(),
            scratch[0], scratch[1], scratch[4], scratch[5], *side_scratch(), pltpu.SemaphoreType.DMA((8,)),
        ],
    )


class Reducer:
    def __init__(self, place, source, sib_mark):
        self.p, self.source, self.sib_mark = place, source, sib_mark
        self.m = place.z * 4 + place.x
        self.sent = []

    @staticmethod
    def mates(place):
        m = place.z * 4 + place.x
        mates = []
        for k in range(1, 16):
            other = lax.rem(m + k, 16)
            for core in (0, 1):
                mates.append(place.at(z=lax.div(other, 4), x=lax.rem(other, 4), c=core))
        return mates

    def member(self, k):
        other = lax.rem(self.m + k, 16)
        return other, self.p.at(z=lax.div(other, 4), x=lax.rem(other, 4))

    def push(self, src, dst, send, recv, device):
        copy = remote(src, dst, send, recv, device)
        copy.start()
        self.sent.append(copy)

    def await_at(self, dst, recv):
        remote(dst, dst, self.sib_mark, recv, self.p.sib).wait_recv()

    def close(self):
        for copy in self.sent:
            copy.wait_send()


class ShardSum(Reducer):
    def __init__(self, place, source, refs):
        (
            self.landing, self.total, self.all, self.a_send, self.a_recv, self.c_send, self.c_recv,
        ) = refs
        super().__init__(place, source, self.a_send.at[0])
        self.cut = source.shape[0] // 16

    @staticmethod
    def scratch(count):
        dma = pltpu.SemaphoreType.DMA
        cut = count // 16
        return [
            pltpu.VMEM((16, cut, LANES), BF), pltpu.VMEM((cut, LANES), BF), pltpu.VMEM((count, LANES), BF),
            dma((16,)), dma((16,)), dma((16,)), dma((16,)),
        ]

    def open(self):
        for k in range(1, 16):
            other, device = self.member(k)
            piece = self.source.at[rows_at(other * self.cut, self.cut)]
            self.push(piece, self.landing.at[k], self.a_send.at[k], self.a_recv.at[k], device)

    def spread(self):
        p = self.p
        total = self.source[rows_at(self.m * self.cut, self.cut), :].astype(F32)
        for k in range(1, 16):
            self.await_at(self.landing.at[k], self.a_recv.at[k])
            total = total + self.landing[k].astype(F32)
        self.total[...] = total.astype(BF)
        mine = self.all.at[rows_at(self.m * self.cut, self.cut)]
        mark = self.c_recv.at[self.m]
        for n in range(1, 16):
            device = p.at(
                z=lax.rem(p.z + n // 4, 4), xl=lax.rem(p.xl + n // 2 % 2, 2), g=p.c, c=lax.rem(p.c + n % 2, 2)
            )
            self.push(self.total, mine, self.c_send.at[n], mark, device)
        self.swapped = remote(self.total, mine, self.c_send.at[0], mark, p.at(g=p.c))
        pl.when(p.away)(self.swapped.start)
        pl.when(p.home)(pltpu.make_async_copy(self.total, mine, mark).start)

    def close(self):
        for index in range(16):
            self.await_at(self.all.at[pl.ds(index * self.cut, self.cut)], self.c_recv.at[index])
        super().close()
        pl.when(self.p.away)(self.swapped.wait_send)


class WholeSum(Reducer):
    def __init__(self, place, source, refs):
        (
            self.sib_in, self.here, self.landing, self.slice_sum, self.bits_in, self.bit_sum, self.all,
            self.b_send, self.b_recv, self.d_send, self.d_recv, self.e_send, self.e_recv, self.f_send, self.f_recv,
            self.g_send, self.g_recv, self.mark,
        ) = refs
        super().__init__(place, source, self.f_send.at[0])
        self.half = source.shape[0] // 2
        self.slice = self.half // 16
        self.bit = self.slice // 4
        self.base = place.c * self.half + self.m * self.slice

    @staticmethod
    def scratch(count):
        dma = pltpu.SemaphoreType.DMA
        half = count // 2
        piece = half // 16
        return [
            pltpu.VMEM((half, LANES), BF), pltpu.VMEM((half, LANES), BF), pltpu.VMEM((16, piece, LANES), BF),
            pltpu.VMEM((piece, LANES), BF), pltpu.VMEM((4, piece // 4, LANES), BF), pltpu.VMEM((piece // 4, LANES), BF),
            pltpu.VMEM((count, LANES), BF),
            dma((16,)), dma((16,)), dma((4,)), dma((4,)), dma((4,)), dma((4,)), dma((2,)), dma((2,)),
            dma((16,)), dma((16,)), dma((1,)),
        ]

    def open(self):
        there = rows_at((1 - self.p.c) * self.half, self.half)
        self.push(self.source.at[there], self.sib_in, self.f_send.at[0], self.f_recv.at[0], self.p.sib)

    def halves(self):
        self.await_at(self.sib_in, self.f_recv.at[0])

        def body(index):
            at = rows_at(index * 128, 128)
            mine = self.source[rows_at(self.p.c * self.half + index * 128, 128), :].astype(F32)
            self.here[at, :] = (mine + self.sib_in[at, :].astype(F32)).astype(BF)

        loop(self.half // 128, body)
        for k in range(1, 16):
            other, device = self.member(k)
            piece = self.here.at[rows_at(other * self.slice, self.slice)]
            self.push(piece, self.landing.at[k], self.b_send.at[k], self.b_recv.at[k], device)

    def slices(self):
        total = self.here[rows_at(self.m * self.slice, self.slice), :].astype(F32)
        for k in range(1, 16):
            self.await_at(self.landing.at[k], self.b_recv.at[k])
            total = total + self.landing[k].astype(F32)
        self.slice_sum[...] = total.astype(BF)
        for dy in (2, 1, 3):
            other = lax.rem(self.p.y + dy, 4)
            piece = self.slice_sum.at[rows_at(other * self.bit, self.bit)]
            self.push(piece, self.bits_in.at[dy], self.d_send.at[dy], self.d_recv.at[dy], self.p.at(y=other))

    def bits(self):
        total = self.slice_sum[rows_at(self.p.y * self.bit, self.bit), :].astype(F32)
        for dy in (1, 3, 2):
            self.await_at(self.bits_in.at[dy], self.d_recv.at[dy])
            total = total + self.bits_in[dy].astype(F32)
        self.bit_sum[...] = total.astype(BF)
        own = self.all.at[rows_at(self.base + self.p.y * self.bit, self.bit)]
        self.placed = pltpu.make_async_copy(self.bit_sum, own, self.mark.at[0])
        self.placed.start()
        for dy in (2, 1, 3):
            device = self.p.at(y=lax.rem(self.p.y + dy, 4))
            self.push(self.bit_sum, own, self.e_send.at[dy], self.e_recv.at[dy], device)

    def slices_back(self):
        self.placed.wait()
        for dy in (1, 3, 2):
            source = lax.rem(self.p.y + 4 - dy, 4)
            self.await_at(self.all.at[rows_at(self.base + source * self.bit, self.bit)], self.e_recv.at[dy])
        own = self.all.at[rows_at(self.base, self.slice)]
        for k in range(1, 16):
            self.push(own, own, self.g_send.at[k], self.g_recv.at[k], self.member(k)[1])

    def halves_back(self):
        for k in range(1, 16):
            source = lax.rem(self.m + 16 - k, 16)
            landing = self.all.at[rows_at(self.p.c * self.half + source * self.slice, self.slice)]
            self.await_at(landing, self.g_recv.at[k])
        half = self.all.at[rows_at(self.p.c * self.half, self.half)]
        self.push(half, half, self.f_send.at[1], self.f_recv.at[1], self.p.sib)

    def close(self):
        self.await_at(self.all.at[rows_at((1 - self.p.c) * self.half, self.half)], self.f_recv.at[1])
        super().close()


class PlaneSum(Reducer):
    def __init__(self, place, source, refs):
        (
            self.landing, self.slice_sum, self.bits_in, self.bit_sum, self.all,
            self.b_send, self.b_recv, self.d_send, self.d_recv, self.e_send, self.e_recv, self.g_send, self.g_recv,
            self.mark,
        ) = refs
        super().__init__(place, source, self.b_send.at[0])
        self.q = self.m * 2 + place.c
        self.slice = source.shape[0] // 32
        self.bit = self.slice // 4
        self.base = self.q * self.slice

    @staticmethod
    def scratch(count):
        dma = pltpu.SemaphoreType.DMA
        piece = count // 32
        return [
            pltpu.VMEM((32, piece, LANES), BF), pltpu.VMEM((piece, LANES), BF), pltpu.VMEM((4, piece // 4, LANES), BF),
            pltpu.VMEM((piece // 4, LANES), BF), pltpu.VMEM((count, LANES), BF),
            dma((32,)), dma((32,)), dma((4,)), dma((4,)), dma((4,)), dma((4,)), dma((32,)), dma((32,)), dma((1,)),
        ]

    def mate(self, k):
        other = lax.rem(self.q + k, 32)
        m = lax.div(other, 2)
        return other, self.p.at(z=lax.div(m, 4), x=lax.rem(m, 4), c=lax.rem(other, 2))

    def open(self):
        for k in range(1, 32):
            other, device = self.mate(k)
            piece = self.source.at[rows_at(other * self.slice, self.slice)]
            self.push(piece, self.landing.at[k], self.b_send.at[k], self.b_recv.at[k], device)

    def slices(self):
        total = self.source[rows_at(self.base, self.slice), :].astype(F32)
        for k in range(1, 32):
            self.await_at(self.landing.at[k], self.b_recv.at[k])
            total = total + self.landing[k].astype(F32)
        self.slice_sum[...] = total.astype(BF)
        for dy in (2, 1, 3):
            other = lax.rem(self.p.y + dy, 4)
            piece = self.slice_sum.at[rows_at(other * self.bit, self.bit)]
            self.push(piece, self.bits_in.at[dy], self.d_send.at[dy], self.d_recv.at[dy], self.p.at(y=other))

    def bits(self):
        total = self.slice_sum[rows_at(self.p.y * self.bit, self.bit), :].astype(F32)
        for dy in (1, 3, 2):
            self.await_at(self.bits_in.at[dy], self.d_recv.at[dy])
            total = total + self.bits_in[dy].astype(F32)
        self.bit_sum[...] = total.astype(BF)
        own = self.all.at[rows_at(self.base + self.p.y * self.bit, self.bit)]
        self.placed = pltpu.make_async_copy(self.bit_sum, own, self.mark.at[0])
        self.placed.start()
        for dy in (2, 1, 3):
            device = self.p.at(y=lax.rem(self.p.y + dy, 4))
            self.push(self.bit_sum, own, self.e_send.at[dy], self.e_recv.at[dy], device)

    def slices_back(self):
        self.placed.wait()
        for dy in (1, 3, 2):
            source = lax.rem(self.p.y + 4 - dy, 4)
            self.await_at(self.all.at[rows_at(self.base + source * self.bit, self.bit)], self.e_recv.at[dy])
        own = self.all.at[rows_at(self.base, self.slice)]
        for k in range(1, 32):
            self.push(own, own, self.g_send.at[k], self.g_recv.at[k], self.mate(k)[1])

    def close(self):
        for k in range(1, 32):
            source = lax.rem(self.q + 32 - k, 32)
            self.await_at(self.all.at[rows_at(source * self.slice, self.slice)], self.g_recv.at[k])
        super().close()


def back_kernel(
    gain, mask, down_shift, side_u, side_o, side_d,
    grad_stage_in, output_in, qkv_in, context_in, tokens_in, cotangent_in, down_expand_in, joined_reduce_in, normed_in,
    side_q_in, grad_in, middle_in, second_in, shard_in, joined_in, out_parts, probs_in,
    block_out, input_grad, shard_done, shard_rest, whole_done, whole_rest,
    grad_stage, output_full, qkv, context, tokens, cotangent, down_expand, joined_reduce, normed, side_q, grad, middle,
    second_normed, shard_early, joined_full, parts, probs, load_sem,
    rows, rows_send, rows_recv, key_grad, value_grad, joined_grad, result, block_own, whole_early, shard_late,
    whole_late, side_part, side_in, side_send, side_recv,
    part, sib_in, relay, near, s_send, s_recv, relay_out, near_out, t_send, t_recv, swap_send, swap_recv,
    *refs,
):
    p = Place()
    own_rows = rows_at(p.ring(0, True) * ROWS, ROWS)
    sources = (
        grad_stage_in, shard_in, second_in, cotangent_in, output_in, qkv_in, context_in, probs_in, out_parts, joined_in,
        side_q_in, normed_in, joined_reduce_in, middle_in, down_expand_in, grad_in, tokens_in,
    )
    targets = (
        grad_stage, shard_early, second_normed, cotangent, output_full, qkv, context, probs, parts, joined_full,
        side_q, normed, joined_reduce, middle, down_expand, grad, tokens,
    )
    loads = [pltpu.make_async_copy(src, dst, load_sem.at[i]) for i, (src, dst) in enumerate(zip(sources, targets))]
    stage = pltpu.make_async_copy(grad_stage_in, rows.at[own_rows], load_sem.at[17])
    stage.start()
    for copy in loads:
        copy.start()
    greet(p.ring_mates() + Reducer.mates(p))
    gather = Gather(p, rows, rows_send, rows_recv)
    stage.wait()
    gather.begin()
    swap = Swap(p, [(block_own, block_out), (result, input_grad)], swap_send, swap_recv)
    early_shard = ShardSum(p, shard_early, refs[0:7])
    early_whole = WholeSum(p, whole_early, refs[7:25])
    late_shard = ShardSum(p, shard_late, refs[25:32])
    late_whole = PlaneSum(p, whole_late, refs[32:46])
    for copy in loads[:4]:
        copy.wait()
    early_shard.open()

    def early_column(j):
        lanes = lanes_at(j * 256, 256)
        whole_early[lanes, :] = tn(second_normed[:, lanes], side_u[...]).astype(BF)
        whole_early[lanes_at(WIDTH + j * 256, 256), :] = (SCALE * tn(grad_stage[:, lanes], side_o[...])).astype(BF)
        whole_early[lanes_at(2 * WIDTH + j * 256, 256), :] = (SCALE * tn(cotangent[:, lanes], side_d[...])).astype(BF)

    loop(WIDTH // 256, early_column)
    early_whole.open()

    def back(dy):
        base = lax.rem(p.y + dy + 4, 4) * PAIR

        def body(index):
            at = rows_at(base + index * ROWS, ROWS)
            context_grad = nt(rows[at, :], output_full[...]).astype(BF)
            for head in range(2):
                start = head * 3 * HEAD
                query = qkv[at, start : start + HEAD]
                key = qkv[:, start + HEAD : start + 2 * HEAD]
                value = qkv[:, start + 2 * HEAD : start + 3 * HEAD]
                own = context_grad[:, head * HEAD : (head + 1) * HEAD]
                weights = probs[head, at, :]
                mean = jnp.sum(
                    own.astype(F32) * context[at, head * HEAD : (head + 1) * HEAD].astype(F32), axis=-1, keepdims=True
                )
                score_grad = weights * (nt(own, value) - mean).astype(BF)
                joined_grad[at, start : start + HEAD] = (nn(score_grad, key) * (1.0 / math.sqrt(HEAD))).astype(BF)
                value_grad[head] = value_grad[head] + tn(own, weights)
                key_grad[head] = key_grad[head] + tn(query, score_grad)

        loop(2, body)

    value_grad[...] = jnp.zeros_like(value_grad)
    key_grad[...] = jnp.zeros_like(key_grad)
    scatter_out = Scatter(p, parts, None, relay_out, near_out, t_send, t_recv, lambda dy: dy % 4 * ROWS)
    gather.own_pair()
    for copy in loads[4:8]:
        copy.wait()
    back(0)
    early_whole.halves()
    loads[8].wait()
    gather.near()
    scatter_out.relay_out()
    scatter_out.near_free(1)
    scatter_out.near_free(-1)
    gather.near_pairs()
    back(1)
    gather.far()
    early_shard.spread()
    back(-1)
    early_whole.slices()
    gather.far_pair()
    scatter_out.near_rest()
    back(2)
    turn = identity()
    for head in range(2):
        start = head * 3 * HEAD
        joined_grad[:, start + HEAD : start + 2 * HEAD] = tn(
            (key_grad[head] * (1.0 / math.sqrt(HEAD))).astype(BF), turn
        ).astype(BF)
        joined_grad[:, start + 2 * HEAD : start + 3 * HEAD] = tn(value_grad[head].astype(BF), turn).astype(BF)
    for copy in loads[9:]:
        copy.wait()

    def product(dy):
        at = pair_rows(p, dy)

        def body(j):
            lanes = lanes_at(j * 512, 512)
            part[at, lanes] = nt(joined_grad[at, :], joined_full[lanes, :]).astype(BF)

        loop(WIDTH // 512, body)

    scatter = Scatter(p, part, sib_in, relay, near, s_send, s_recv)
    product(2)
    scatter.exchange(2)
    side_part[...] = nt(joined_grad[...], joined_full[pl.ds(WIDTH, LANES), :]).astype(BF)
    side = SideSum(p, side_part, side_in, side_send, side_recv)
    side.open()
    early_whole.bits()
    scatter.combine(2)
    scatter.relay_out()
    product(1)
    scatter.exchange(1)
    mask_rows = mask[...].astype(F32)
    side_part[own_rows, :] = (mask_rows * side.total()).astype(BF)

    def late_column(j):
        lanes = lanes_at(j * 256, 256)
        whole_late[lanes, :] = tn(normed[:, lanes], side_part[own_rows, :]).astype(BF)

    loop(WIDTH // 256, late_column)
    late_whole.open()
    product(-1)
    scatter.exchange(-1)
    scatter.combine(1)
    scatter.near_free(1)
    product(0)
    scatter.exchange(0)
    scatter.combine(-1)
    scatter.near_free(-1)
    scatter.near_rest()
    scatter.combine(0)
    shard_late[pl.ds(0, CTX), :] = tn(context[...], rows[:, pl.ds(WIDTH, LANES)]).astype(BF)

    def late_lane(j):
        lanes = lanes_at(j * 256, 256)
        shard_late[lanes_at(CTX + j * 256, 256), :] = (SCALE * tn(joined_grad[:, lanes], side_q[...])).astype(BF)

    loop(QKV // 256, late_lane)
    late_shard.open()
    scatter_out.arrived()

    def add_tile(j):
        lanes = lanes_at(j * 256, 256)
        block_own[:, lanes] = (
            middle[:, lanes]
            + scatter_out.total(0, ROWS, lanes)
            + down_shift[:, lanes]
            + SCALE * nn(side_d[...], down_expand[:, lanes])
        ).astype(BF)

    loop(WIDTH // 256, add_tile)
    swap.begin(0)
    late_whole.slices()
    early_whole.slices_back()
    late_shard.spread()
    late_whole.bits()
    late_whole.slices_back()
    scatter.arrived()

    def norm_block(index):
        at = rows_at(index * BLOCK, BLOCK)
        side_rows = side_part[rows_at(p.ring(0, True) * ROWS + index * BLOCK, BLOCK), :]
        back_grad = scatter.total(index * BLOCK, BLOCK, pl.ds(0, WIDTH)) + nt(side_rows, joined_reduce[...])
        result[at, :] = (grad[at, :] + norm_back(tokens[at, :].astype(F32), gain[...], back_grad)).astype(BF)

    loop(ROWS // BLOCK, norm_block)
    swap.begin(1)
    early_whole.halves_back()
    early_shard.close()
    late_shard.close()
    early_whole.close()
    late_whole.close()
    shard_done[...] = early_shard.all[...]
    shard_rest[...] = late_shard.all[...]
    whole_done[...] = early_whole.all[...]
    whole_rest[...] = late_whole.all[...]
    gather.end()
    scatter.end()
    scatter_out.end(4)
    side.end()
    swap.arrived(0)
    swap.arrived(1)
    swap.end()


def back_call(ins):
    outs = [
        shape(ROWS, WIDTH), shape(ROWS, WIDTH), shape(2 * UNITS, LANES), shape(CTX + QKV, LANES),
        shape(3 * WIDTH, LANES), shape(WIDTH, LANES),
    ]
    dma = pltpu.SemaphoreType.DMA
    vmem = pltpu.VMEM
    return call(
        back_kernel,
        3,
        ins,
        [IN_VMEM] * 6 + [ANYWHERE] * 17,
        outs,
        [ANYWHERE] * 2 + [IN_VMEM] * 4,
        [
            vmem((ROWS, WIDE), BF), vmem((CTX, WIDE), BF), vmem((GROUP, QKV), BF), vmem((GROUP, CTX), BF),
            vmem((ROWS, WIDTH), BF), vmem((ROWS, WIDTH), BF), vmem((LANES, WIDTH), BF), vmem((WIDTH, LANES), BF),
            vmem((ROWS, WIDTH), BF), vmem((GROUP, LANES), BF), vmem((ROWS, WIDTH), F32), vmem((ROWS, WIDTH), F32),
            vmem((ROWS, WIDE), BF), vmem((2 * UNITS, LANES), BF), vmem((WIDE, QKV), BF), vmem((4 * ROWS, WIDTH), BF),
            vmem((2, GROUP, GROUP), BF), dma((18,)),
            *gather_scratch(), vmem((2, HEAD, GROUP), F32), vmem((2, HEAD, GROUP), F32), vmem((GROUP, QKV), BF),
            vmem((ROWS, WIDTH), BF), vmem((ROWS, WIDTH), BF), vmem((3 * WIDTH, LANES), BF),
            vmem((CTX + QKV, LANES), BF), vmem((WIDTH, LANES), BF), *side_scratch(), *scatter_scratch(WIDTH),
            *scatter_scratch(WIDTH)[2:], *swap_marks(2), *ShardSum.scratch(2 * UNITS), *WholeSum.scratch(3 * WIDTH),
            *ShardSum.scratch(CTX + QKV), *PlaneSum.scratch(WIDTH),
        ],
    )


def finish_kernel(
    shard_early, whole_early, shard_late, whole_late, block_in, grad_in,
    block_out, input_grad, qkv_a, qkv_b, out_a, out_b, up_a, up_b, down_a, down_b,
    block_here, grad_here, a_here, b_here, out_sem,
):
    turn = identity()
    copies = []

    def send(src, dst):
        copy = pltpu.make_async_copy(src, dst, out_sem.at[len(copies)])
        copy.start()
        copies.append(copy)

    def turned(source, start, base, count):
        def body(j):
            b_here[:, lanes_at(base + j * 256, 256)] = nt(turn, source[lanes_at(start + j * 256, 256), :])

        loop(count // 256, body)

    def widened(source, start, here, base, count, step):
        def body(index):
            here[rows_at(base + index * step, step), :] = source[rows_at(start + index * step, step), :].astype(F32)

        loop(count // step, body)

    widened(block_in, 0, block_here, 0, ROWS, BLOCK)
    send(block_here, block_out)
    widened(grad_in, 0, grad_here, 0, ROWS, BLOCK)
    send(grad_here, input_grad)
    base = 0
    for source, start, out, count in (
        (whole_early, 0, up_a, WIDTH),
        (whole_late, 0, qkv_a, WIDTH),
        (shard_early, 0, down_a, UNITS),
        (shard_late, 0, out_a, CTX),
    ):
        widened(source, start, a_here, base, count, 256)
        send(a_here.at[pl.ds(base, count)], out.at[0])
        base += count
    base = 0
    for source, start, out, count in (
        (whole_early, WIDTH, out_b, WIDTH),
        (whole_early, 2 * WIDTH, down_b, WIDTH),
        (shard_early, UNITS, up_b, UNITS),
        (shard_late, CTX, qkv_b, QKV),
    ):
        turned(source, start, base, count)
        send(b_here.at[:, pl.ds(base, count)], out.at[0])
        base += count
    for copy in copies:
        copy.wait()


def finish_call(ins):
    return pl.pallas_call(
        finish_kernel,
        name="finish_kernel",
        out_shape=[
            shape(ROWS, WIDTH, kind=F32), shape(ROWS, WIDTH, kind=F32), shape(1, WIDTH, LANES, kind=F32),
            shape(1, LANES, QKV, kind=F32), shape(1, CTX, LANES, kind=F32), shape(1, LANES, WIDTH, kind=F32),
            shape(1, WIDTH, LANES, kind=F32), shape(1, LANES, UNITS, kind=F32), shape(1, UNITS, LANES, kind=F32),
            shape(1, LANES, WIDTH, kind=F32),
        ],
        in_specs=[IN_VMEM] * 6,
        out_specs=[ANYWHERE] * 10,
        scratch_shapes=[
            pltpu.VMEM((ROWS, WIDTH), F32), pltpu.VMEM((ROWS, WIDTH), F32),
            pltpu.VMEM((2 * WIDTH + UNITS + CTX, LANES), F32), pltpu.VMEM((LANES, 2 * WIDTH + UNITS + QKV), F32),
            pltpu.SemaphoreType.DMA((10,)),
        ],
        compiler_params=pltpu.CompilerParams(vmem_limit_bytes=VMEM_LIMIT),
    )(*ins)


def shards(
    tokens, lengths, order, sequence_adapter, first_norm_gain, first_norm_bias, second_norm_gain, second_norm_bias,
    joined_matrix, joined_offset_bias, output_matrix, output_offset_bias, up_matrix, up_offset_bias, down_matrix,
    down_offset_bias, joined_adapter_reduce, joined_adapter_expand, output_adapter_reduce, output_adapter_expand,
    up_adapter_reduce, up_adapter_expand, down_adapter_reduce, down_adapter_expand, cotangent,
):
    (
        normed, middle, side_o, context, qkv, mask_own, probs, side_q, normed_first, gathered_grad, cot_own,
        joined_full, output_full, up_full, down_full, tokens_own, up_shift_own,
    ) = forward_call(
        (
            first_norm_gain, first_norm_bias, joined_adapter_reduce[0], down_adapter_expand[0],
            joined_adapter_expand[0], joined_offset_bias, order, output_adapter_expand[0], output_offset_bias,
            second_norm_gain, second_norm_bias, up_adapter_reduce[0], lengths, sequence_adapter,
            tokens, cotangent, up_offset_bias, joined_matrix[0], output_matrix[0], output_adapter_reduce[0],
            up_matrix[0], up_adapter_expand[0], down_matrix[0], down_adapter_reduce[0],
        )
    )
    grad, grad_stage, side_u, side_d, shard_feed, out_parts = feed_call(
        (
            normed, middle, up_shift_own, mask_own, second_norm_gain, up_adapter_reduce[0],
            output_adapter_expand[0], gathered_grad, up_full, down_full,
        )
    )
    block_own, input_own, shard_early, shard_late, whole_early, whole_late = back_call(
        (
            first_norm_gain, mask_own, down_offset_bias, side_u, side_o, side_d, grad_stage, output_full, qkv, context,
            tokens_own, cot_own, down_adapter_expand[0], joined_adapter_reduce[0], normed_first, side_q, grad, middle,
            normed, shard_feed, joined_full, out_parts, probs,
        )
    )
    return tuple(finish_call((shard_early, whole_early, shard_late, whole_late, block_own, input_own)))


def solution(mesh):
    spread = P(("dp", "tensor"), None)
    by_dp = P("dp", None)
    rows = P(None, "dp", "tensor")
    cols = P(None, "tensor", "dp")
    last = P(None, None, "tensor")
    middle = P(None, "tensor", None)
    vector = P(None, "tensor")
    return jax.shard_map(
        shards,
        mesh=mesh,
        in_specs=(
            spread, by_dp, by_dp, by_dp, P(), P(), P(), P(), rows, vector, cols, P(), rows, vector, cols, P(),
            P(), last, middle, P(), P(), last, middle, P(), spread,
        ),
        out_specs=(spread, spread, P(), last, middle, P(), P(), last, middle, P()),
        check_vma=False,
    )
```

```python
import functools
import math

import jax
import jax.numpy as jnp
from jax import lax
from jax.experimental import pallas as pl
from jax.experimental.pallas import tpu as pltpu
from jax.sharding import PartitionSpec as P

HEAD = 128
WIDTH = 2048
LANES = 128
WIDE = WIDTH + LANES
ROWS = 160
HALF = ROWS // 2
PAIR = 2 * ROWS
GROUP = 8 * ROWS
QKV = 768
UNITS = 1024
CTX = 256
BLOCK = 32
SCALE = 0.5
EPS = 1e-05
MASKED = -1e30
LOG2E = 1.4426950408889634
VMEM_LIMIT = 60 * 2**20
BF = jnp.bfloat16
F32 = jnp.float32
BY_MESH = pl.DeviceIdType.MESH
ANYWHERE = pl.BlockSpec(memory_space=pl.ANY)
IN_VMEM = pl.BlockSpec(memory_space=pltpu.VMEM)
IN_SMEM = pl.BlockSpec(memory_space=pltpu.SMEM)


def nn(left, right):
    return jnp.dot(left, right, preferred_element_type=F32)


def nt(left, right):
    return lax.dot_general(left, right, (((1,), (1,)), ((), ())), preferred_element_type=F32)


def tn(left, right):
    return lax.dot_general(left, right, (((0,), (0,)), ((), ())), preferred_element_type=F32)


def rows_at(start, size):
    return pl.ds(pl.multiple_of(start, 16), size)


def lanes_at(start, size):
    return pl.ds(pl.multiple_of(start, 128), size)


def loop(count, body):
    def step(index, carry):
        body(index)
        return carry

    lax.fori_loop(0, count, step, 0)


class Place:
    def __init__(self):
        dp = lax.axis_index("dp")
        tensor = lax.axis_index("tensor")
        self.dp = dp
        self.z = lax.div(dp, 4)
        self.xl = lax.rem(lax.div(dp, 2), 2)
        self.c = lax.rem(dp, 2)
        self.y = lax.div(tensor, 2)
        self.g = lax.rem(tensor, 2)
        self.x = self.g * 2 + self.xl
        self.sib = self.at(c=1 - self.c)
        self.up = self.at(y=lax.rem(self.y + 1, 4))
        self.down = self.at(y=lax.rem(self.y + 3, 4))
        self.z_up = self.at(z=lax.rem(self.z + 1, 4))
        self.z_down = self.at(z=lax.rem(self.z + 3, 4))
        self.partner = self.at(g=self.c, c=self.g)
        self.beside = self.at(x=lax.rem(self.x + 2 * self.xl + 3, 4), c=self.g)
        self.home = self.c == self.g
        self.away = self.c != self.g

    def at(self, z=None, x=None, xl=None, c=None, y=None, g=None):
        z = self.z if z is None else z
        c = self.c if c is None else c
        y = self.y if y is None else y
        if x is None:
            xl = self.xl if xl is None else xl
            g = self.g if g is None else g
        else:
            xl = lax.rem(x, 2)
            g = lax.div(x, 2)
        return (z * 4 + xl * 2 + c, y * 2 + g)

    def in_row(self, dx, core):
        return self.at(x=lax.rem(self.x + dx, 4), c=core)

    def row_mates(self):
        return [self.in_row(dx, core) for dx in (1, 2, 3) for core in (0, 1)]

    def column_mates(self):
        return [self.at(z=lax.rem(self.z + dz, 4), c=core) for dz in (1, 2, 3) for core in (0, 1)]

    def ring_mates(self):
        mates = [self.sib]
        for dy in (1, 2, 3):
            y = lax.rem(self.y + dy, 4)
            mates += [self.at(y=y), self.at(y=y, c=1 - self.c)]
        return mates

    def ring(self, dy, same):
        return lax.rem(self.y + dy + 4, 4) * 2 + (self.c if same else 1 - self.c)


def greet(devices):
    barrier = pltpu.get_barrier_semaphore()
    for device in devices:
        pl.semaphore_signal(barrier, 1, device_id=device, device_id_type=BY_MESH)
    pl.semaphore_wait(barrier, len(devices))


def remote(src, dst, send, recv, device):
    return pltpu.make_async_remote_copy(
        src_ref=src, dst_ref=dst, send_sem=send, recv_sem=recv, device_id=device, device_id_type=BY_MESH
    )


class Gather:
    SENDS = (
        (0, True, None),
        (0, True, None),
        (0, True, None),
        (-1, True, 0),
        (1, True, 1),
        (-1, True, None),
        (1, True, None),
        (2, True, 0),
        (2, True, 1),
    )
    LANDS = (
        (0, False, None),
        (-1, True, None),
        (1, True, None),
        (2, True, 0),
        (2, True, 1),
        (-1, False, None),
        (1, False, None),
        (2, False, 0),
        (2, False, 1),
    )

    def __init__(self, place, buf, send, recv):
        self.place, self.buf, self.send, self.recv = place, buf, send, recv
        p = place
        self.to = (p.sib, p.up, p.down, p.up, p.down, p.sib, p.sib, p.sib, p.sib)

    def piece(self, what):
        dy, same, half = what
        start = self.place.ring(dy, same) * ROWS
        if half is None:
            return self.buf.at[rows_at(start, ROWS)]
        return self.buf.at[rows_at(start + half * HALF, HALF)]

    def copy(self, i):
        piece = self.piece(self.SENDS[i])
        return remote(piece, piece, self.send.at[i], self.recv.at[i], self.to[i])

    def landed(self, i):
        piece = self.piece(self.LANDS[i])
        remote(piece, piece, self.send.at[i], self.recv.at[i], self.to[i]).wait_recv()

    def begin(self):
        for i in (1, 2, 0):
            self.copy(i).start()

    def near(self):
        self.landed(1)
        self.copy(3).start()
        self.copy(5).start()
        self.landed(2)
        self.copy(4).start()
        self.copy(6).start()

    def far(self):
        self.landed(3)
        self.copy(7).start()
        self.landed(4)
        self.copy(8).start()

    def own_pair(self):
        self.landed(0)

    def near_pairs(self):
        self.landed(5)
        self.landed(6)

    def far_pair(self):
        self.landed(7)
        self.landed(8)

    def end(self):
        for i in range(9):
            self.copy(i).wait_send()


class Scatter:
    def __init__(self, place, part, sib_in, relay, near, send, recv, start=None):
        self.place, self.part, self.sib_in, self.relay, self.near = place, part, sib_in, relay, near
        self.send, self.recv = send, recv
        self.start = start or (lambda dy: place.ring(dy, True) * ROWS)

    def mine(self, dy, half=None):
        start = self.start(dy)
        if half is None:
            return self.part.at[rows_at(start, ROWS)]
        return self.part.at[rows_at(start + half * HALF, HALF)]

    def others(self, dy):
        return self.part.at[rows_at(self.place.ring(dy, False) * ROWS, ROWS)]

    def copy(self, i):
        p = self.place
        if i < 4:
            src, dst, to = self.others(i), self.sib_in.at[i], p.sib
        elif i == 4:
            src, dst, to = self.mine(2, 0), self.relay.at[0], p.up
        elif i == 5:
            src, dst, to = self.mine(2, 1), self.relay.at[1], p.down
        elif i == 6:
            src, dst, to = self.mine(1, 1), self.near.at[0, pl.ds(HALF, HALF)], p.up
        elif i == 7:
            src, dst, to = self.mine(-1, 0), self.near.at[1, pl.ds(0, HALF)], p.down
        elif i == 8:
            src, dst, to = self.mine(1, 0), self.near.at[0, pl.ds(0, HALF)], p.up
        else:
            src, dst, to = self.mine(-1, 1), self.near.at[1, pl.ds(HALF, HALF)], p.down
        return remote(src, dst, self.send.at[i], self.recv.at[i], to)

    def exchange(self, dy):
        self.copy(dy % 4).start()

    def combine(self, dy):
        self.copy(dy % 4).wait_recv()
        add_rows(self.part, self.start(dy), self.sib_in.at[dy % 4], 0, ROWS)

    def relay_out(self):
        self.copy(4).start()
        self.copy(5).start()

    def near_free(self, dy):
        self.copy(6 if dy == 1 else 7).start()

    def near_rest(self):
        self.copy(4).wait_recv()
        add_rows(self.part, self.start(1), self.relay.at[0], 0, HALF)
        self.copy(8).start()
        self.copy(5).wait_recv()
        add_rows(self.part, self.start(-1) + HALF, self.relay.at[1], 0, HALF)
        self.copy(9).start()

    def arrived(self):
        for i in (6, 7, 8, 9):
            self.copy(i).wait_recv()

    def total(self, start, size, lanes):
        own = self.part[rows_at(self.start(0) + start, size), lanes].astype(F32)
        return (
            own
            + self.near[0, rows_at(start, size), lanes].astype(F32)
            + self.near[1, rows_at(start, size), lanes].astype(F32)
        )

    def end(self, first=0, last=10):
        for i in range(first, last):
            self.copy(i).wait_send()


def scatter_scratch(width=WIDE):
    return [
        pltpu.VMEM((GROUP, width), BF),
        pltpu.VMEM((4, ROWS, width), BF),
        pltpu.VMEM((2, HALF, width), BF),
        pltpu.VMEM((2, ROWS, width), BF),
        pltpu.SemaphoreType.DMA((10,)),
        pltpu.SemaphoreType.DMA((10,)),
    ]


def gather_scratch():
    return [pltpu.VMEM((GROUP, WIDE), BF), pltpu.SemaphoreType.DMA((9,)), pltpu.SemaphoreType.DMA((9,))]


def add_rows(dst, start, src, src_start, count):
    def body(index):
        at = rows_at(start + index * 16, 16)
        dst[at, :] = (dst[at, :].astype(F32) + src[rows_at(src_start + index * 16, 16), :].astype(F32)).astype(BF)

    loop(count // 16, body)


class Weights:
    def __init__(self, place, piece, full, by_rows, cut, send, recv):
        self.place, self.piece, self.full, self.by_rows = place, piece, full, by_rows
        self.send, self.recv = send, recv
        size = piece.shape[1] if by_rows else piece.shape[0]
        self.parts = (pl.ds(0, cut), pl.ds(cut, size - cut))

    def source(self, half):
        part = self.parts[half]
        return self.piece.at[:, part] if self.by_rows else self.piece.at[part, :]

    def slot(self, index, count, half):
        span = lanes_at(index * 128, count * 128)
        part = self.parts[half]
        return self.full.at[span, part] if self.by_rows else self.full.at[part, span]

    def column(self, dz):
        return lax.rem(self.place.z + dz, 4)

    def first(self):
        p = self.place
        marks = (self.recv.at[p.xl * 2 + p.c], self.recv.at[4 + p.z * 2 + p.c])
        slots = (self.slot(p.dp, 1, 0), self.slot(p.dp, 1, 1))
        for d in (2, 1, 3):
            remote(self.source(0), slots[0], self.send.at[d], marks[0], p.in_row(d, p.g)).start()
            remote(self.source(1), slots[1], self.send.at[4 + d], marks[1], p.at(z=self.column(d), c=p.g)).start()

        @pl.when(p.home)
        def _():
            for half in range(2):
                pltpu.make_async_copy(self.source(half), slots[half], marks[half]).start()

        @pl.when(p.away)
        def _():
            for half in range(2):
                remote(self.source(half), slots[half], self.send.at[4 * half], marks[half], p.sib).start()

    def landed(self, slot, mark):
        remote(slot, slot, self.send.at[0], self.recv.at[mark], self.place.sib).wait_recv()

    def along_z(self, i):
        p = self.place
        z, first, count, to = (
            (p.z, 0, 4, p.z_up),
            (p.z, 0, 4, p.z_down),
            (self.column(3), 0, 2, p.z_up),
            (self.column(1), 2, 2, p.z_down),
        )[i]
        block = self.slot(z * 4 + first, count, 0)
        return remote(block, block, self.send.at[8 + i], self.recv.at[12 + i], to)

    def along_x(self, z, dx):
        p = self.place
        pair = self.slot(z * 4 + p.xl * 2, 2, 1)
        mark = self.send.at[12 + z * 2 + dx // 2]
        return remote(pair, pair, mark, self.recv.at[16 + p.xl * 4 + z], p.in_row(dx, p.c))

    def second(self):
        p = self.place
        for index in range(4):
            self.landed(self.slot(p.z * 4 + index, 1, 0), index)
        self.along_z(0).start()
        self.along_z(1).start()

        @pl.when(p.home)
        def _():
            for z in range(4):
                for core in range(2):
                    self.landed(self.slot(z * 4 + p.xl * 2 + core, 1, 1), 4 + z * 2 + core)
                self.along_x(z, 1).start()
                self.along_x(z, 3).start()

    def passed_on(self, i):
        p = self.place
        home = 1 - lax.rem(p.c + p.g, 2)
        plus = 1 - lax.rem(p.xl + home, 2)
        z = (1 - plus) * 2 + i
        pair = self.slot(z * 4 + (1 - p.xl) * 2, 2, 1)
        mark = self.recv.at[16 + (1 - p.xl) * 4 + z]
        return remote(pair, pair, self.send.at[20 + i], mark, p.in_row(3 - 2 * plus, p.c))

    def third(self):
        p = self.place
        self.landed(self.slot(self.column(3) * 4, 4, 0), 12)
        self.along_z(2).start()
        self.landed(self.slot(self.column(1) * 4, 4, 0), 13)
        self.along_z(3).start()
        for z in range(4):
            self.landed(self.slot(z * 4 + (1 - p.xl) * 2, 2, 1), 16 + (1 - p.xl) * 4 + z)
        for i in range(2):
            self.passed_on(i).start()

    def arrived(self):
        p = self.place
        self.landed(self.slot(self.column(2) * 4, 2, 0), 14)
        self.landed(self.slot(self.column(2) * 4 + 2, 2, 0), 15)

        @pl.when(p.away)
        def _():
            for z in range(4):
                self.landed(self.slot(z * 4 + p.xl * 2, 2, 1), 16 + p.xl * 4 + z)

    def end(self):
        p = self.place
        for d in (1, 2, 3):
            for half in range(2):
                slot = self.slot(p.dp, 1, half)
                remote(self.source(half), slot, self.send.at[4 * half + d], self.recv.at[0], p.sib).wait_send()
        for i in range(4):
            self.along_z(i).wait_send()
        for i in range(2):
            self.passed_on(i).wait_send()

        @pl.when(p.away)
        def _():
            for half in range(2):
                slot = self.slot(p.dp, 1, half)
                remote(self.source(half), slot, self.send.at[4 * half], self.recv.at[0], p.sib).wait_send()

        @pl.when(p.home)
        def _():
            for z in range(4):
                self.along_x(z, 1).wait_send()
                self.along_x(z, 3).wait_send()


def weight_marks():
    return [pltpu.SemaphoreType.DMA((22,)), pltpu.SemaphoreType.DMA((24,))]


class Swap:
    def __init__(self, place, pairs, send, recv, shared=()):
        self.place, self.pairs, self.send, self.recv, self.shared = place, pairs, send, recv, shared

    def begin(self, i):
        src, dst = self.pairs[i]
        p = self.place

        @pl.when(p.home)
        def _():
            pltpu.make_async_copy(src, dst, self.recv.at[i]).start()

        @pl.when(p.away)
        def _():
            device = p.beside if i in self.shared else p.partner
            remote(src, dst, self.send.at[i], self.recv.at[i], device).start()

    def arrived(self, i):
        src, dst = self.pairs[i]
        remote(src, dst, self.send.at[i], self.recv.at[i], self.place.sib).wait_recv()

    def end(self):
        @pl.when(self.place.away)
        def _():
            for i, (src, dst) in enumerate(self.pairs):
                remote(src, dst, self.send.at[i], self.recv.at[i], self.place.sib).wait_send()


def swap_marks(count):
    return [pltpu.SemaphoreType.DMA((count,)), pltpu.SemaphoreType.DMA((count,))]


def normalise(value):
    mean = jnp.mean(value, axis=-1, keepdims=True)
    center = value - mean
    inverse = lax.rsqrt(jnp.mean(center * center, axis=-1, keepdims=True) + EPS)
    return center * inverse, inverse


def norm_back(value, gain, grad):
    normed, inverse = normalise(value)
    e = grad * gain
    return (e - jnp.mean(e, axis=-1, keepdims=True) - normed * jnp.mean(e * normed, axis=-1, keepdims=True)) * inverse


def pair_rows(place, dy):
    return rows_at(lax.rem(place.y + dy + 4, 4) * PAIR, PAIR)


def wide_product(put, make):
    loop(4, lambda j: put(lanes_at(j * 512, 512), make(lanes_at(j * 512, 512))))
    put(pl.ds(WIDTH, LANES), make(pl.ds(WIDTH, LANES)))


def call(kernel, collective, ins, specs, outs, out_specs, scratch):
    return pl.pallas_call(
        kernel,
        name=kernel.__name__,
        out_shape=outs,
        in_specs=specs,
        out_specs=out_specs,
        scratch_shapes=scratch,
        compiler_params=pltpu.CompilerParams(
            collective_id=collective, has_side_effects=True, vmem_limit_bytes=VMEM_LIMIT
        ),
    )(*ins)


def shape(*dims, kind=BF):
    return jax.ShapeDtypeStruct(dims, kind)


def identity():
    row = lax.broadcasted_iota(jnp.int32, (LANES, LANES), 0)
    return jnp.where(row == lax.broadcasted_iota(jnp.int32, (LANES, LANES), 1), 1.0, 0.0).astype(BF)


def query_info(token_row, start_row):
    token_high = jnp.floor(token_row * (1.0 / 16.0))
    start_high = jnp.floor(start_row * (1.0 / 16.0))
    digit = lax.broadcasted_iota(jnp.int32, (16, GROUP), 0)
    digits = jnp.where(digit == 0, token_high, 0.0)
    digits = jnp.where(digit == 1, token_row - 16.0 * token_high, digits)
    digits = jnp.where(digit == 2, start_high, digits)
    digits = jnp.where(digit == 3, start_row - 16.0 * start_high, digits)
    row = lax.broadcasted_iota(jnp.int32, (16, LANES), 0)
    lane = lax.broadcasted_iota(jnp.int32, (16, LANES), 1)
    worth = jnp.where((row == 0) & (lane == 0) | (row == 2) & (lane == 1), 16.0, 0.0)
    worth = worth + jnp.where((row == 1) & (lane == 0) | (row == 3) & (lane == 1), 1.0, 0.0)
    return tn(digits.astype(BF), worth.astype(BF))


def slope_row(place, head, tokens_row):
    number = (place.ring(0, True) * 2 + head + 1).astype(F32)
    slope = jnp.exp2(jnp.full((1, GROUP), -0.5, F32) * number)
    return slope * LOG2E * tokens_row


def forward_kernel(
    gain, shift, joined_reduce, down_expand, joined_expand, joined_shift, order, output_expand, output_shift,
    second_gain, second_shift, up_reduce, lengths, adapters,
    tokens, cotangent, up_shift, joined_piece, output_piece, output_reduce, up_piece, up_expand, down_piece, down_reduce,
    normed, middle, side_o, context, qkv, mask_own,
    probs_out, side_q, normed_own, gathered_grad, cot_own, joined_full, output_full, up_full, down_full, tokens_own,
    up_shift_own,
    tok_here, aux, aux_here, half_expand, shift_here, joined_here, output_here, info, mask_all, probs,
    rows, rows_send, rows_recv, grads, grads_send, grads_recv, part, sib_in, relay, near, s_send, s_recv,
    w_send, w_recv, o_send, o_recv, u_send, u_recv, d_send, d_recv, swap_send, swap_recv, out_sem, probs_sem,
):
    p = Place()
    greet([p.sib, p.up, p.down] + p.row_mates() + p.column_mates())
    joined = Weights(p, joined_piece, joined_here.at[pl.ds(0, WIDTH)], True, 512, w_send, w_recv)
    output = Weights(p, output_piece, output_here.at[:, pl.ds(0, WIDTH)], False, 160, o_send, o_recv)
    up = Weights(p, up_piece, up_full.at[pl.ds(0, WIDTH)], True, 640, u_send, u_recv)
    down = Weights(p, down_piece, down_full.at[:, pl.ds(0, WIDTH)], False, 640, d_send, d_recv)
    own_rows = rows_at(p.ring(0, True) * ROWS, ROWS)
    their_rows = rows_at((p.y * 2 + p.g) * ROWS, ROWS)
    swap = Swap(
        p,
        [
            (tokens, tok_here),
            (aux, aux_here),
            (half_expand, joined_here.at[pl.ds(WIDTH, LANES)]),
            (joined_shift, shift_here),
            (cotangent, grads.at[their_rows, pl.ds(0, WIDTH)]),
            (output_reduce, output_here.at[:, pl.ds(WIDTH, LANES)]),
            (up_expand, up_full.at[pl.ds(WIDTH, LANES)]),
            (down_reduce, down_full.at[:, pl.ds(WIDTH, LANES)]),
            (up_shift, up_shift_own),
        ],
        swap_send,
        swap_recv,
        (2, 3, 5, 6, 7, 8),
    )
    joined.first()
    swap.begin(0)
    token = order[...]
    first_end = lengths[0, 0]
    second_end = first_end + lengths[0, 1]
    later = token >= second_end
    late = token >= first_end
    start = jnp.where(later, second_end, jnp.where(late, first_end, 0))
    adapter = jnp.where(later, adapters[0, 2], jnp.where(late, adapters[0, 1], adapters[0, 0]))
    for i, row in enumerate((token, start, adapter)):
        aux[:, pl.ds(i * GROUP, GROUP)] = jnp.broadcast_to(row.astype(F32), (8, GROUP))
    half_expand[...] = (SCALE * joined_expand[...].astype(F32)).astype(BF)
    for i in (1, 2, 3):
        swap.begin(i)
    swap.arrived(1)
    token_row = aux_here[0:1, pl.ds(0, GROUP)]
    info[...] = query_info(token_row, aux_here[0:1, pl.ds(GROUP, GROUP)])
    column = lax.shift_right_logical(lax.broadcasted_iota(jnp.int32, (LANES, GROUP), 0), 4).astype(F32)
    chosen = jnp.where(column == aux_here[0:1, pl.ds(2 * GROUP, GROUP)], 1.0, 0.0).astype(BF)
    mask_all[...] = tn(chosen, identity()).astype(BF)
    mask_own[...] = mask_all[own_rows, :]
    mask_rows = mask_all[own_rows, :].astype(F32)
    joined.second()
    swap.arrived(0)

    def norm_block(index):
        at = rows_at(index * BLOCK, BLOCK)
        value, _ = normalise(tok_here[at, :].astype(F32))
        rows[rows_at(p.ring(0, True) * ROWS + index * BLOCK, BLOCK), pl.ds(0, WIDTH)] = (
            value * gain[...] + shift[...]
        ).astype(BF)

    loop(ROWS // BLOCK, norm_block)
    rows[own_rows, pl.ds(WIDTH, LANES)] = (
        mask_rows * nn(rows[own_rows, pl.ds(0, WIDTH)], joined_reduce[...])
    ).astype(BF)
    gather = Gather(p, rows, rows_send, rows_recv)
    gather_grad = Gather(p, grads, grads_send, grads_recv)
    gather.begin()
    swap.begin(4)
    output.first()
    joined.third()
    up.first()
    down.first()
    for i in range(5, 9):
        swap.begin(i)
    output.second()
    swap.arrived(4)
    grads[own_rows, pl.ds(WIDTH, LANES)] = (
        mask_rows * (SCALE * nt(grads[own_rows, pl.ds(0, WIDTH)], down_expand[...]))
    ).astype(BF)
    copies = [
        pltpu.make_async_copy(tok_here, tokens_own, out_sem.at[0]),
        pltpu.make_async_copy(grads.at[own_rows, pl.ds(0, WIDTH)], cot_own, out_sem.at[1]),
        pltpu.make_async_copy(rows.at[own_rows, pl.ds(0, WIDTH)], normed_own, out_sem.at[2]),
    ]
    for copy in copies:
        copy.start()
    gather.near()
    gather_grad.begin()
    up.second()
    swap.arrived(2)
    swap.arrived(3)
    joined.arrived()
    copies.append(pltpu.make_async_copy(joined_here, joined_full, out_sem.at[3]))
    copies[-1].start()

    def project(dy):
        at = pair_rows(p, dy)

        def body(j):
            lanes = lanes_at(j * 256, 256)
            qkv[at, lanes] = (nn(rows[at, :], joined_here[:, lanes]) + shift_here[:, lanes]).astype(BF)

        loop(QKV // 256, body)

    gather.own_pair()
    project(0)
    gather.near_pairs()
    project(1)
    output.third()
    project(-1)
    gather.far()
    down.second()
    gather.far_pair()
    project(2)
    up.third()
    copies.append(pltpu.make_async_copy(rows.at[:, pl.ds(WIDTH, LANES)], side_q, out_sem.at[4]))
    copies[-1].start()
    output.arrived()
    swap.arrived(5)
    copies.append(pltpu.make_async_copy(output_here, output_full, out_sem.at[5]))
    copies[-1].start()
    probs_copies = []

    def attend(dy, same):
        at = rows_at(p.ring(dy, same) * ROWS, ROWS)
        n = len(probs_copies)
        if n >= 2:
            probs_copies[n - 2].wait()
        query_token = info[at, 0:1]
        query_start = info[at, 1:2]
        allowed = (token_row <= query_token) & (token_row >= query_start)
        for head in range(2):
            first = head * 3 * HEAD
            scores = nt(qkv[at, first : first + HEAD], qkv[:, first + HEAD : first + 2 * HEAD])
            scores = scores * (LOG2E / math.sqrt(HEAD)) + slope_row(p, head, token_row)
            scores = jnp.where(allowed, scores, MASKED)
            top = jnp.max(scores, axis=-1, keepdims=True)
            weights = jnp.exp2(scores - top)
            total = jnp.sum(weights, axis=-1, keepdims=True)
            weights = (weights * (1.0 / total)).astype(BF)
            probs[n % 2, head] = weights
            context[at, head * HEAD : (head + 1) * HEAD] = nn(
                weights, qkv[:, first + 2 * HEAD : first + 3 * HEAD]
            ).astype(BF)
        copy = pltpu.make_async_copy(probs.at[n % 2], probs_out.at[:, at], probs_sem.at[n])
        copy.start()
        probs_copies.append(copy)

        def put(lanes, value):
            part[at, lanes] = value.astype(BF)

        wide_product(put, lambda lanes: nn(context[at, :], output_here[:, lanes]))

    scatter = Scatter(p, part, sib_in, relay, near, s_send, s_recv)
    attend(2, False)
    scatter.exchange(2)
    attend(2, True)
    scatter.combine(2)
    scatter.relay_out()
    gather_grad.near()
    attend(1, False)
    scatter.exchange(1)
    attend(1, True)
    scatter.combine(1)
    scatter.near_free(1)
    down.third()
    attend(-1, False)
    scatter.exchange(-1)
    attend(-1, True)
    scatter.combine(-1)
    scatter.near_free(-1)
    gather_grad.far()
    attend(0, False)
    scatter.exchange(0)
    scatter.near_rest()
    attend(0, True)
    scatter.combine(0)
    gather_grad.own_pair()
    gather_grad.near_pairs()
    gather_grad.far_pair()
    copies.append(pltpu.make_async_copy(grads, gathered_grad, out_sem.at[6]))
    copies[-1].start()
    scatter.arrived()
    side = (mask_rows * scatter.total(0, ROWS, pl.ds(WIDTH, LANES))).astype(BF)
    side_o[...] = side

    def add_tile(j):
        lanes = lanes_at(j * 512, 512)
        middle[:, lanes] = (
            tok_here[:, lanes].astype(F32)
            + scatter.total(0, ROWS, lanes)
            + output_shift[:, lanes]
            + SCALE * nn(side, output_expand[:, lanes])
        )

    loop(4, add_tile)

    def second_block(index):
        at = rows_at(index * BLOCK, BLOCK)
        value, _ = normalise(middle[at, :])
        normed[at, pl.ds(0, WIDTH)] = (value * second_gain[...] + second_shift[...]).astype(BF)

    loop(ROWS // BLOCK, second_block)
    normed[:, pl.ds(WIDTH, LANES)] = (mask_rows * nn(normed[:, pl.ds(0, WIDTH)], up_reduce[...])).astype(BF)
    up.arrived()
    down.arrived()
    for i in range(6, 9):
        swap.arrived(i)
    swap.end()
    for sender in (gather, gather_grad, scatter, joined, output, up, down):
        sender.end()
    for copy in copies + probs_copies[-2:]:
        copy.wait()


def forward_call(ins):
    outs = [
        shape(ROWS, WIDE), shape(ROWS, WIDTH, kind=F32), shape(ROWS, LANES), shape(GROUP, CTX), shape(GROUP, QKV),
        shape(ROWS, LANES),
        shape(2, GROUP, GROUP), shape(GROUP, LANES), shape(ROWS, WIDTH), shape(GROUP, WIDE), shape(ROWS, WIDTH),
        shape(WIDE, QKV), shape(CTX, WIDE), shape(WIDE, UNITS), shape(UNITS, WIDE), shape(ROWS, WIDTH),
        shape(1, UNITS, kind=F32),
    ]
    return call(
        forward_kernel,
        1,
        ins,
        [IN_VMEM] * 12 + [IN_SMEM] * 2 + [ANYWHERE] * 10,
        outs,
        [IN_VMEM] * 6 + [ANYWHERE] * 11,
        [
            pltpu.VMEM((ROWS, WIDTH), BF), pltpu.VMEM((8, 3 * GROUP), F32), pltpu.VMEM((8, 3 * GROUP), F32),
            pltpu.VMEM((LANES, QKV), BF), pltpu.VMEM((1, QKV), F32), pltpu.VMEM((WIDE, QKV), BF),
            pltpu.VMEM((CTX, WIDE), BF), pltpu.VMEM((GROUP, LANES), F32), pltpu.VMEM((GROUP, LANES), BF),
            pltpu.VMEM((2, 2, ROWS, GROUP), BF), *gather_scratch(), *gather_scratch(), *scatter_scratch(),
            *weight_marks(), *weight_marks(), *weight_marks(), *weight_marks(), *swap_marks(9),
            pltpu.SemaphoreType.DMA((7,)), pltpu.SemaphoreType.DMA((8,)),
        ],
    )


class SideSum:
    def __init__(self, place, part, landing, send, recv):
        self.place, self.part, self.landing = place, part, landing
        self.copies = []
        for k in range(1, 8):
            y = lax.rem(place.y + k // 2, 4)
            core = place.c if k % 2 == 0 else 1 - place.c
            piece = part.at[rows_at((y * 2 + core) * ROWS, ROWS)]
            self.copies.append(remote(piece, landing.at[k], send.at[k], recv.at[k], place.at(y=y, c=core)))

    def open(self):
        for copy in self.copies:
            copy.start()

    def total(self):
        total = self.part[rows_at(self.place.ring(0, True) * ROWS, ROWS), :].astype(F32)
        for k in range(1, 8):
            self.copies[k - 1].wait_recv()
            total = total + self.landing[k].astype(F32)
        return total

    def end(self):
        for copy in self.copies:
            copy.wait_send()


def side_scratch():
    dma = pltpu.SemaphoreType.DMA
    return [pltpu.VMEM((GROUP, LANES), BF), pltpu.VMEM((8, ROWS, LANES), BF), dma((8,)), dma((8,))]


def feed_kernel(
    normed, middle, up_shift, mask, gain, up_reduce, output_expand,
    gathered_grad, up_weights, down_weights,
    grad_out, grad_stage, side_u, side_d, by_shard, out_parts,
    up_full, down_full, grads, rows, rows_send, rows_recv, act, slope, part, sib_in, relay, near, s_send, s_recv,
    part_out, sib_in_out, t_send, t_recv, side_part, side_in, side_send, side_recv, own_sem,
):
    p = Place()
    own_rows = rows_at(p.ring(0, True) * ROWS, ROWS)
    stage = pltpu.make_async_copy(normed, rows.at[own_rows], own_sem.at[0])
    stage.start()
    load_down = pltpu.make_async_copy(down_weights, down_full, own_sem.at[1])
    load_down.start()
    load_grads = pltpu.make_async_copy(gathered_grad, grads, own_sem.at[2])
    load_grads.start()
    load_up = pltpu.make_async_copy(up_weights, up_full, own_sem.at[3])
    load_up.start()
    greet(p.ring_mates())
    gather = Gather(p, rows, rows_send, rows_recv)
    stage.wait()
    gather.begin()

    def lift(j):
        lanes = lanes_at(j * 256, 256)
        slope[:, lanes] = nt(grads[...], down_full[lanes, :]).astype(BF)

    def hide(dy):
        at = pair_rows(p, dy)

        def body(j):
            lanes = lanes_at(j * 256, 256)
            v = nn(rows[at, :], up_full[:, lanes]) + up_shift[:, lanes]
            square = v * v
            t = jnp.tanh(v * (0.7978845608028654 + 0.7978845608028654 * 0.044715 * square))
            half = 0.5 + 0.5 * t
            act[at, lanes] = (v * half).astype(BF)
            bend = half + v * (1.0 - t * t) * (
                0.5 * 0.7978845608028654 + 0.5 * 0.7978845608028654 * 3.0 * 0.044715 * square
            )
            slope[at, lanes] = (slope[at, lanes].astype(F32) * bend).astype(BF)

        loop(UNITS // 256, body)

    def back(dy):
        at = pair_rows(p, dy)

        def put(lanes, value):
            part[at, lanes] = value.astype(BF)

        wide_product(put, lambda lanes: nt(slope[at, :], up_full[lanes, :]))

    def forth(dy):
        at = pair_rows(p, dy)

        def body(j):
            lanes = lanes_at(j * 512, 512)
            part_out[at, lanes] = nn(act[at, :], down_full[:, lanes]).astype(BF)

        loop(WIDTH // 512, body)

    load_down.wait()
    load_grads.wait()
    loop(UNITS // 256, lift)
    load_up.wait()
    expand = pl.ds(WIDTH, LANES)
    up_full[expand, :] = (SCALE * up_full[expand, :].astype(F32)).astype(BF)
    scatter = Scatter(p, part, sib_in, relay, near, s_send, s_recv)
    scatter_out = Scatter(p, part_out, sib_in_out, None, None, t_send, t_recv)
    gather.own_pair()
    hide(0)
    gather.near()
    gather.near_pairs()
    hide(1)
    hide(-1)
    back(1)
    scatter.exchange(1)
    gather.far()
    back(-1)
    scatter.exchange(-1)
    gather.far_pair()
    scatter.combine(1)
    scatter.near_free(1)
    scatter.combine(-1)
    scatter.near_free(-1)
    hide(2)
    back(2)
    scatter.exchange(2)
    back(0)
    scatter.combine(2)
    scatter.relay_out()
    scatter.exchange(0)
    forth(2)
    scatter_out.exchange(2)
    scatter.near_rest()
    scatter.combine(0)
    side_part[...] = nn(act[...], down_full[:, pl.ds(WIDTH, LANES)]).astype(BF)
    side = SideSum(p, side_part, side_in, side_send, side_recv)
    side.open()
    for dy in (1, -1, 0):
        forth(dy)
        scatter_out.exchange(dy)

    def by_unit(j):
        at = lanes_at(j * 256, 256)
        by_shard[at, :] = tn(act[:, at], grads[:, pl.ds(WIDTH, LANES)]).astype(BF)
        by_shard[lanes_at(UNITS + j * 256, 256), :] = (
            SCALE * tn(slope[:, at], rows[:, pl.ds(WIDTH, LANES)])
        ).astype(BF)

    loop(UNITS // 256, by_unit)
    mask_rows = mask[...].astype(F32)
    for dy in range(4):
        scatter_out.combine(dy)
    copies = []

    def hand_on(src, start, count):
        copy = pltpu.make_async_copy(src, out_parts.at[pl.ds(start, count)], own_sem.at[4 + len(copies)])
        copy.start()
        copies.append(copy)

    for dy in range(4):
        hand_on(scatter_out.mine(dy), dy * ROWS, ROWS)
    scatter.arrived()
    side_u[...] = (mask_rows * scatter.total(0, ROWS, pl.ds(WIDTH, LANES))).astype(BF)

    def norm_block(index):
        at = rows_at(index * BLOCK, BLOCK)
        mine = rows_at(p.ring(0, True) * ROWS + index * BLOCK, BLOCK)
        grad = scatter.total(index * BLOCK, BLOCK, pl.ds(0, WIDTH)) + nt(side_u[at, :], up_reduce[...])
        grad = grads[mine, pl.ds(0, WIDTH)].astype(F32) + norm_back(middle[at, :], gain[...], grad)
        grad_out[at, :] = grad
        grad_stage[at, pl.ds(0, WIDTH)] = grad.astype(BF)

    loop(ROWS // BLOCK, norm_block)
    grad_stage[:, pl.ds(WIDTH, LANES)] = (
        mask_rows * (SCALE * nt(grad_stage[:, pl.ds(0, WIDTH)], output_expand[...]))
    ).astype(BF)
    side_d[...] = (mask_rows * side.total()).astype(BF)
    gather.end()
    side.end()
    scatter.end()
    scatter_out.end(0, 4)
    for copy in copies:
        copy.wait()


def feed_call(ins):
    outs = [
        shape(ROWS, WIDTH, kind=F32), shape(ROWS, WIDE), shape(ROWS, LANES), shape(ROWS, LANES),
        shape(2 * UNITS, LANES), shape(4 * ROWS, WIDTH),
    ]
    scratch = scatter_scratch(WIDTH)
    return call(
        feed_kernel,
        2,
        ins,
        [IN_VMEM] * 7 + [ANYWHERE] * 3,
        outs,
        [IN_VMEM] * 5 + [ANYWHERE],
        [
            pltpu.VMEM((WIDE, UNITS), BF), pltpu.VMEM((UNITS, WIDE), BF), pltpu.VMEM((GROUP, WIDE), BF),
            *gather_scratch(), pltpu.VMEM((GROUP, UNITS), BF), pltpu.VMEM((GROUP, UNITS), BF), *scatter_scratch(),
            scratch[0], scratch[1], scratch[4], scratch[5], *side_scratch(), pltpu.SemaphoreType.DMA((8,)),
        ],
    )


class Reducer:
    def __init__(self, place, source, sib_mark):
        self.p, self.source, self.sib_mark = place, source, sib_mark
        self.m = place.z * 4 + place.x
        self.sent = []

    @staticmethod
    def mates(place):
        m = place.z * 4 + place.x
        mates = []
        for k in range(1, 16):
            other = lax.rem(m + k, 16)
            for core in (0, 1):
                mates.append(place.at(z=lax.div(other, 4), x=lax.rem(other, 4), c=core))
        return mates

    def member(self, k):
        other = lax.rem(self.m + k, 16)
        return other, self.p.at(z=lax.div(other, 4), x=lax.rem(other, 4))

    def push(self, src, dst, send, recv, device):
        copy = remote(src, dst, send, recv, device)
        copy.start()
        self.sent.append(copy)

    def await_at(self, dst, recv):
        remote(dst, dst, self.sib_mark, recv, self.p.sib).wait_recv()

    def close(self):
        for copy in self.sent:
            copy.wait_send()


class ShardSum(Reducer):
    def __init__(self, place, source, refs):
        (
            self.landing, self.total, self.all, self.a_send, self.a_recv, self.c_send, self.c_recv,
        ) = refs
        super().__init__(place, source, self.a_send.at[0])
        self.cut = source.shape[0] // 16

    @staticmethod
    def scratch(count):
        dma = pltpu.SemaphoreType.DMA
        cut = count // 16
        return [
            pltpu.VMEM((16, cut, LANES), BF), pltpu.VMEM((cut, LANES), BF), pltpu.VMEM((count, LANES), BF),
            dma((16,)), dma((16,)), dma((16,)), dma((16,)),
        ]

    def open(self):
        for k in range(1, 16):
            other, device = self.member(k)
            piece = self.source.at[rows_at(other * self.cut, self.cut)]
            self.push(piece, self.landing.at[k], self.a_send.at[k], self.a_recv.at[k], device)

    def spread(self):
        p = self.p
        total = self.source[rows_at(self.m * self.cut, self.cut), :].astype(F32)
        for k in range(1, 16):
            self.await_at(self.landing.at[k], self.a_recv.at[k])
            total = total + self.landing[k].astype(F32)
        self.total[...] = total.astype(BF)
        mine = self.all.at[rows_at(self.m * self.cut, self.cut)]
        mark = self.c_recv.at[self.m]
        for n in range(1, 16):
            device = p.at(
                z=lax.rem(p.z + n // 4, 4), xl=lax.rem(p.xl + n // 2 % 2, 2), g=p.c, c=lax.rem(p.c + n % 2, 2)
            )
            self.push(self.total, mine, self.c_send.at[n], mark, device)
        self.swapped = remote(self.total, mine, self.c_send.at[0], mark, p.at(g=p.c))
        pl.when(p.away)(self.swapped.start)
        pl.when(p.home)(pltpu.make_async_copy(self.total, mine, mark).start)

    def close(self):
        for index in range(16):
            self.await_at(self.all.at[pl.ds(index * self.cut, self.cut)], self.c_recv.at[index])
        super().close()
        pl.when(self.p.away)(self.swapped.wait_send)


class WholeSum(Reducer):
    def __init__(self, place, source, refs):
        (
            self.sib_in, self.here, self.landing, self.slice_sum, self.bits_in, self.bit_sum, self.all,
            self.b_send, self.b_recv, self.d_send, self.d_recv, self.e_send, self.e_recv, self.f_send, self.f_recv,
            self.g_send, self.g_recv, self.mark,
        ) = refs
        super().__init__(place, source, self.f_send.at[0])
        self.half = source.shape[0] // 2
        self.slice = self.half // 16
        self.bit = self.slice // 4
        self.base = place.c * self.half + self.m * self.slice

    @staticmethod
    def scratch(count):
        dma = pltpu.SemaphoreType.DMA
        half = count // 2
        piece = half // 16
        return [
            pltpu.VMEM((half, LANES), BF), pltpu.VMEM((half, LANES), BF), pltpu.VMEM((16, piece, LANES), BF),
            pltpu.VMEM((piece, LANES), BF), pltpu.VMEM((4, piece // 4, LANES), BF), pltpu.VMEM((piece // 4, LANES), BF),
            pltpu.VMEM((count, LANES), BF),
            dma((16,)), dma((16,)), dma((4,)), dma((4,)), dma((4,)), dma((4,)), dma((2,)), dma((2,)),
            dma((16,)), dma((16,)), dma((1,)),
        ]

    def open(self):
        there = rows_at((1 - self.p.c) * self.half, self.half)
        self.push(self.source.at[there], self.sib_in, self.f_send.at[0], self.f_recv.at[0], self.p.sib)

    def halves(self):
        self.await_at(self.sib_in, self.f_recv.at[0])

        def body(index):
            at = rows_at(index * 128, 128)
            mine = self.source[rows_at(self.p.c * self.half + index * 128, 128), :].astype(F32)
            self.here[at, :] = (mine + self.sib_in[at, :].astype(F32)).astype(BF)

        loop(self.half // 128, body)
        for k in range(1, 16):
            other, device = self.member(k)
            piece = self.here.at[rows_at(other * self.slice, self.slice)]
            self.push(piece, self.landing.at[k], self.b_send.at[k], self.b_recv.at[k], device)

    def slices(self):
        total = self.here[rows_at(self.m * self.slice, self.slice), :].astype(F32)
        for k in range(1, 16):
            self.await_at(self.landing.at[k], self.b_recv.at[k])
            total = total + self.landing[k].astype(F32)
        self.slice_sum[...] = total.astype(BF)
        for dy in (2, 1, 3):
            other = lax.rem(self.p.y + dy, 4)
            piece = self.slice_sum.at[rows_at(other * self.bit, self.bit)]
            self.push(piece, self.bits_in.at[dy], self.d_send.at[dy], self.d_recv.at[dy], self.p.at(y=other))

    def bits(self):
        total = self.slice_sum[rows_at(self.p.y * self.bit, self.bit), :].astype(F32)
        for dy in (1, 3, 2):
            self.await_at(self.bits_in.at[dy], self.d_recv.at[dy])
            total = total + self.bits_in[dy].astype(F32)
        self.bit_sum[...] = total.astype(BF)
        own = self.all.at[rows_at(self.base + self.p.y * self.bit, self.bit)]
        self.placed = pltpu.make_async_copy(self.bit_sum, own, self.mark.at[0])
        self.placed.start()
        for dy in (2, 1, 3):
            device = self.p.at(y=lax.rem(self.p.y + dy, 4))
            self.push(self.bit_sum, own, self.e_send.at[dy], self.e_recv.at[dy], device)

    def slices_back(self):
        self.placed.wait()
        for dy in (1, 3, 2):
            source = lax.rem(self.p.y + 4 - dy, 4)
            self.await_at(self.all.at[rows_at(self.base + source * self.bit, self.bit)], self.e_recv.at[dy])
        own = self.all.at[rows_at(self.base, self.slice)]
        for k in range(1, 16):
            self.push(own, own, self.g_send.at[k], self.g_recv.at[k], self.member(k)[1])

    def halves_back(self):
        for k in range(1, 16):
            source = lax.rem(self.m + 16 - k, 16)
            landing = self.all.at[rows_at(self.p.c * self.half + source * self.slice, self.slice)]
            self.await_at(landing, self.g_recv.at[k])
        half = self.all.at[rows_at(self.p.c * self.half, self.half)]
        self.push(half, half, self.f_send.at[1], self.f_recv.at[1], self.p.sib)

    def close(self):
        self.await_at(self.all.at[rows_at((1 - self.p.c) * self.half, self.half)], self.f_recv.at[1])
        super().close()


class PlaneSum(Reducer):
    def __init__(self, place, source, refs):
        (
            self.landing, self.slice_sum, self.bits_in, self.bit_sum, self.all,
            self.b_send, self.b_recv, self.d_send, self.d_recv, self.e_send, self.e_recv, self.g_send, self.g_recv,
            self.mark,
        ) = refs
        super().__init__(place, source, self.b_send.at[0])
        self.q = self.m * 2 + place.c
        self.slice = source.shape[0] // 32
        self.bit = self.slice // 4
        self.base = self.q * self.slice

    @staticmethod
    def scratch(count):
        dma = pltpu.SemaphoreType.DMA
        piece = count // 32
        return [
            pltpu.VMEM((32, piece, LANES), BF), pltpu.VMEM((piece, LANES), BF), pltpu.VMEM((4, piece // 4, LANES), BF),
            pltpu.VMEM((piece // 4, LANES), BF), pltpu.VMEM((count, LANES), BF),
            dma((32,)), dma((32,)), dma((4,)), dma((4,)), dma((4,)), dma((4,)), dma((32,)), dma((32,)), dma((1,)),
        ]

    def mate(self, k):
        other = lax.rem(self.q + k, 32)
        m = lax.div(other, 2)
        return other, self.p.at(z=lax.div(m, 4), x=lax.rem(m, 4), c=lax.rem(other, 2))

    def open(self):
        for k in range(1, 32):
            other, device = self.mate(k)
            piece = self.source.at[rows_at(other * self.slice, self.slice)]
            self.push(piece, self.landing.at[k], self.b_send.at[k], self.b_recv.at[k], device)

    def slices(self):
        total = self.source[rows_at(self.base, self.slice), :].astype(F32)
        for k in range(1, 32):
            self.await_at(self.landing.at[k], self.b_recv.at[k])
            total = total + self.landing[k].astype(F32)
        self.slice_sum[...] = total.astype(BF)
        for dy in (2, 1, 3):
            other = lax.rem(self.p.y + dy, 4)
            piece = self.slice_sum.at[rows_at(other * self.bit, self.bit)]
            self.push(piece, self.bits_in.at[dy], self.d_send.at[dy], self.d_recv.at[dy], self.p.at(y=other))

    def bits(self):
        total = self.slice_sum[rows_at(self.p.y * self.bit, self.bit), :].astype(F32)
        for dy in (1, 3, 2):
            self.await_at(self.bits_in.at[dy], self.d_recv.at[dy])
            total = total + self.bits_in[dy].astype(F32)
        self.bit_sum[...] = total.astype(BF)
        own = self.all.at[rows_at(self.base + self.p.y * self.bit, self.bit)]
        self.placed = pltpu.make_async_copy(self.bit_sum, own, self.mark.at[0])
        self.placed.start()
        for dy in (2, 1, 3):
            device = self.p.at(y=lax.rem(self.p.y + dy, 4))
            self.push(self.bit_sum, own, self.e_send.at[dy], self.e_recv.at[dy], device)

    def slices_back(self):
        self.placed.wait()
        for dy in (1, 3, 2):
            source = lax.rem(self.p.y + 4 - dy, 4)
            self.await_at(self.all.at[rows_at(self.base + source * self.bit, self.bit)], self.e_recv.at[dy])
        own = self.all.at[rows_at(self.base, self.slice)]
        for k in range(1, 32):
            self.push(own, own, self.g_send.at[k], self.g_recv.at[k], self.mate(k)[1])

    def close(self):
        for k in range(1, 32):
            source = lax.rem(self.q + 32 - k, 32)
            self.await_at(self.all.at[rows_at(source * self.slice, self.slice)], self.g_recv.at[k])
        super().close()


def back_kernel(
    gain, mask, down_shift, side_u, side_o, side_d,
    grad_stage_in, output_in, qkv_in, context_in, tokens_in, cotangent_in, down_expand_in, joined_reduce_in, normed_in,
    side_q_in, grad_in, middle_in, second_in, shard_in, joined_in, out_parts, probs_in,
    block_out, input_grad, shard_done, shard_rest, whole_done, whole_rest,
    grad_stage, output_full, qkv, context, tokens, cotangent, down_expand, joined_reduce, normed, side_q, grad, middle,
    second_normed, shard_early, joined_full, parts, probs, load_sem,
    rows, rows_send, rows_recv, key_grad, value_grad, joined_grad, result, block_own, whole_early, shard_late,
    whole_late, side_part, side_in, side_send, side_recv,
    part, sib_in, relay, near, s_send, s_recv, relay_out, near_out, t_send, t_recv, swap_send, swap_recv,
    *refs,
):
    p = Place()
    own_rows = rows_at(p.ring(0, True) * ROWS, ROWS)
    sources = (
        grad_stage_in, shard_in, second_in, cotangent_in, output_in, qkv_in, context_in, probs_in, out_parts, joined_in,
        side_q_in, normed_in, joined_reduce_in, middle_in, down_expand_in, grad_in, tokens_in,
    )
    targets = (
        grad_stage, shard_early, second_normed, cotangent, output_full, qkv, context, probs, parts, joined_full,
        side_q, normed, joined_reduce, middle, down_expand, grad, tokens,
    )
    loads = [pltpu.make_async_copy(src, dst, load_sem.at[i]) for i, (src, dst) in enumerate(zip(sources, targets))]
    stage = pltpu.make_async_copy(grad_stage_in, rows.at[own_rows], load_sem.at[17])
    stage.start()
    for copy in loads:
        copy.start()
    greet(p.ring_mates() + Reducer.mates(p))
    gather = Gather(p, rows, rows_send, rows_recv)
    stage.wait()
    gather.begin()
    swap = Swap(p, [(block_own, block_out), (result, input_grad)], swap_send, swap_recv)
    early_shard = ShardSum(p, shard_early, refs[0:7])
    early_whole = WholeSum(p, whole_early, refs[7:25])
    late_shard = ShardSum(p, shard_late, refs[25:32])
    late_whole = PlaneSum(p, whole_late, refs[32:46])
    for copy in loads[:4]:
        copy.wait()
    early_shard.open()

    def early_column(j):
        lanes = lanes_at(j * 256, 256)
        whole_early[lanes, :] = tn(second_normed[:, lanes], side_u[...]).astype(BF)
        whole_early[lanes_at(WIDTH + j * 256, 256), :] = (SCALE * tn(grad_stage[:, lanes], side_o[...])).astype(BF)
        whole_early[lanes_at(2 * WIDTH + j * 256, 256), :] = (SCALE * tn(cotangent[:, lanes], side_d[...])).astype(BF)

    loop(WIDTH // 256, early_column)
    early_whole.open()

    def back(dy):
        base = lax.rem(p.y + dy + 4, 4) * PAIR

        def body(index):
            at = rows_at(base + index * ROWS, ROWS)
            context_grad = nt(rows[at, :], output_full[...]).astype(BF)
            for head in range(2):
                start = head * 3 * HEAD
                query = qkv[at, start : start + HEAD]
                key = qkv[:, start + HEAD : start + 2 * HEAD]
                value = qkv[:, start + 2 * HEAD : start + 3 * HEAD]
                own = context_grad[:, head * HEAD : (head + 1) * HEAD]
                weights = probs[head, at, :]
                mean = jnp.sum(
                    own.astype(F32) * context[at, head * HEAD : (head + 1) * HEAD].astype(F32), axis=-1, keepdims=True
                )
                score_grad = weights * (nt(own, value) - mean).astype(BF)
                joined_grad[at, start : start + HEAD] = (nn(score_grad, key) * (1.0 / math.sqrt(HEAD))).astype(BF)
                value_grad[head] = value_grad[head] + tn(own, weights)
                key_grad[head] = key_grad[head] + tn(query, score_grad)

        loop(2, body)

    value_grad[...] = jnp.zeros_like(value_grad)
    key_grad[...] = jnp.zeros_like(key_grad)
    scatter_out = Scatter(p, parts, None, relay_out, near_out, t_send, t_recv, lambda dy: dy % 4 * ROWS)
    gather.own_pair()
    for copy in loads[4:8]:
        copy.wait()
    back(0)
    early_whole.halves()
    loads[8].wait()
    gather.near()
    scatter_out.relay_out()
    scatter_out.near_free(1)
    scatter_out.near_free(-1)
    gather.near_pairs()
    back(1)
    gather.far()
    early_shard.spread()
    back(-1)
    early_whole.slices()
    gather.far_pair()
    scatter_out.near_rest()
    back(2)
    turn = identity()
    for head in range(2):
        start = head * 3 * HEAD
        joined_grad[:, start + HEAD : start + 2 * HEAD] = tn(
            (key_grad[head] * (1.0 / math.sqrt(HEAD))).astype(BF), turn
        ).astype(BF)
        joined_grad[:, start + 2 * HEAD : start + 3 * HEAD] = tn(value_grad[head].astype(BF), turn).astype(BF)
    for copy in loads[9:]:
        copy.wait()

    def product(dy):
        at = pair_rows(p, dy)

        def body(j):
            lanes = lanes_at(j * 512, 512)
            part[at, lanes] = nt(joined_grad[at, :], joined_full[lanes, :]).astype(BF)

        loop(WIDTH // 512, body)

    scatter = Scatter(p, part, sib_in, relay, near, s_send, s_recv)
    product(2)
    scatter.exchange(2)
    side_part[...] = nt(joined_grad[...], joined_full[pl.ds(WIDTH, LANES), :]).astype(BF)
    side = SideSum(p, side_part, side_in, side_send, side_recv)
    side.open()
    early_whole.bits()
    scatter.combine(2)
    scatter.relay_out()
    product(1)
    scatter.exchange(1)
    mask_rows = mask[...].astype(F32)
    side_part[own_rows, :] = (mask_rows * side.total()).astype(BF)

    def late_column(j):
        lanes = lanes_at(j * 256, 256)
        whole_late[lanes, :] = tn(normed[:, lanes], side_part[own_rows, :]).astype(BF)

    loop(WIDTH // 256, late_column)
    late_whole.open()
    product(-1)
    scatter.exchange(-1)
    scatter.combine(1)
    scatter.near_free(1)
    product(0)
    scatter.exchange(0)
    scatter.combine(-1)
    scatter.near_free(-1)
    scatter.near_rest()
    scatter.combine(0)
    shard_late[pl.ds(0, CTX), :] = tn(context[...], rows[:, pl.ds(WIDTH, LANES)]).astype(BF)

    def late_lane(j):
        lanes = lanes_at(j * 256, 256)
        shard_late[lanes_at(CTX + j * 256, 256), :] = (SCALE * tn(joined_grad[:, lanes], side_q[...])).astype(BF)

    loop(QKV // 256, late_lane)
    late_shard.open()
    scatter_out.arrived()

    def add_tile(j):
        lanes = lanes_at(j * 256, 256)
        block_own[:, lanes] = (
            middle[:, lanes]
            + scatter_out.total(0, ROWS, lanes)
            + down_shift[:, lanes]
            + SCALE * nn(side_d[...], down_expand[:, lanes])
        ).astype(BF)

    loop(WIDTH // 256, add_tile)
    swap.begin(0)
    late_whole.slices()
    early_whole.slices_back()
    late_shard.spread()
    late_whole.bits()
    late_whole.slices_back()
    scatter.arrived()

    def norm_block(index):
        at = rows_at(index * BLOCK, BLOCK)
        side_rows = side_part[rows_at(p.ring(0, True) * ROWS + index * BLOCK, BLOCK), :]
        back_grad = scatter.total(index * BLOCK, BLOCK, pl.ds(0, WIDTH)) + nt(side_rows, joined_reduce[...])
        result[at, :] = (grad[at, :] + norm_back(tokens[at, :].astype(F32), gain[...], back_grad)).astype(BF)

    loop(ROWS // BLOCK, norm_block)
    swap.begin(1)
    early_whole.halves_back()
    early_shard.close()
    late_shard.close()
    early_whole.close()
    late_whole.close()
    shard_done[...] = early_shard.all[...]
    shard_rest[...] = late_shard.all[...]
    whole_done[...] = early_whole.all[...]
    whole_rest[...] = late_whole.all[...]
    gather.end()
    scatter.end()
    scatter_out.end(4)
    side.end()
    swap.arrived(0)
    swap.arrived(1)
    swap.end()


def back_call(ins):
    outs = [
        shape(ROWS, WIDTH), shape(ROWS, WIDTH), shape(2 * UNITS, LANES), shape(CTX + QKV, LANES),
        shape(3 * WIDTH, LANES), shape(WIDTH, LANES),
    ]
    dma = pltpu.SemaphoreType.DMA
    vmem = pltpu.VMEM
    return call(
        back_kernel,
        3,
        ins,
        [IN_VMEM] * 6 + [ANYWHERE] * 17,
        outs,
        [ANYWHERE] * 2 + [IN_VMEM] * 4,
        [
            vmem((ROWS, WIDE), BF), vmem((CTX, WIDE), BF), vmem((GROUP, QKV), BF), vmem((GROUP, CTX), BF),
            vmem((ROWS, WIDTH), BF), vmem((ROWS, WIDTH), BF), vmem((LANES, WIDTH), BF), vmem((WIDTH, LANES), BF),
            vmem((ROWS, WIDTH), BF), vmem((GROUP, LANES), BF), vmem((ROWS, WIDTH), F32), vmem((ROWS, WIDTH), F32),
            vmem((ROWS, WIDE), BF), vmem((2 * UNITS, LANES), BF), vmem((WIDE, QKV), BF), vmem((4 * ROWS, WIDTH), BF),
            vmem((2, GROUP, GROUP), BF), dma((18,)),
            *gather_scratch(), vmem((2, HEAD, GROUP), F32), vmem((2, HEAD, GROUP), F32), vmem((GROUP, QKV), BF),
            vmem((ROWS, WIDTH), BF), vmem((ROWS, WIDTH), BF), vmem((3 * WIDTH, LANES), BF),
            vmem((CTX + QKV, LANES), BF), vmem((WIDTH, LANES), BF), *side_scratch(), *scatter_scratch(WIDTH),
            *scatter_scratch(WIDTH)[2:], *swap_marks(2), *ShardSum.scratch(2 * UNITS), *WholeSum.scratch(3 * WIDTH),
            *ShardSum.scratch(CTX + QKV), *PlaneSum.scratch(WIDTH),
        ],
    )


def finish_kernel(
    shard_early, whole_early, shard_late, whole_late, block_in, grad_in,
    block_out, input_grad, qkv_a, qkv_b, out_a, out_b, up_a, up_b, down_a, down_b,
    block_here, grad_here, a_here, b_here, out_sem,
):
    turn = identity()
    copies = []

    def send(src, dst):
        copy = pltpu.make_async_copy(src, dst, out_sem.at[len(copies)])
        copy.start()
        copies.append(copy)

    def turned(source, start, base, count):
        def body(j):
            b_here[:, lanes_at(base + j * 256, 256)] = nt(turn, source[lanes_at(start + j * 256, 256), :])

        loop(count // 256, body)

    def widened(source, start, here, base, count, step):
        def body(index):
            here[rows_at(base + index * step, step), :] = source[rows_at(start + index * step, step), :].astype(F32)

        loop(count // step, body)

    widened(block_in, 0, block_here, 0, ROWS, BLOCK)
    send(block_here, block_out)
    widened(grad_in, 0, grad_here, 0, ROWS, BLOCK)
    send(grad_here, input_grad)
    base = 0
    for source, start, out, count in (
        (whole_early, 0, up_a, WIDTH),
        (whole_late, 0, qkv_a, WIDTH),
        (shard_early, 0, down_a, UNITS),
        (shard_late, 0, out_a, CTX),
    ):
        widened(source, start, a_here, base, count, 256)
        send(a_here.at[pl.ds(base, count)], out.at[0])
        base += count
    base = 0
    for source, start, out, count in (
        (whole_early, WIDTH, out_b, WIDTH),
        (whole_early, 2 * WIDTH, down_b, WIDTH),
        (shard_early, UNITS, up_b, UNITS),
        (shard_late, CTX, qkv_b, QKV),
    ):
        turned(source, start, base, count)
        send(b_here.at[:, pl.ds(base, count)], out.at[0])
        base += count
    for copy in copies:
        copy.wait()


def finish_call(ins):
    return pl.pallas_call(
        finish_kernel,
        name="finish_kernel",
        out_shape=[
            shape(ROWS, WIDTH, kind=F32), shape(ROWS, WIDTH, kind=F32), shape(1, WIDTH, LANES, kind=F32),
            shape(1, LANES, QKV, kind=F32), shape(1, CTX, LANES, kind=F32), shape(1, LANES, WIDTH, kind=F32),
            shape(1, WIDTH, LANES, kind=F32), shape(1, LANES, UNITS, kind=F32), shape(1, UNITS, LANES, kind=F32),
            shape(1, LANES, WIDTH, kind=F32),
        ],
        in_specs=[IN_VMEM] * 6,
        out_specs=[ANYWHERE] * 10,
        scratch_shapes=[
            pltpu.VMEM((ROWS, WIDTH), F32), pltpu.VMEM((ROWS, WIDTH), F32),
            pltpu.VMEM((2 * WIDTH + UNITS + CTX, LANES), F32), pltpu.VMEM((LANES, 2 * WIDTH + UNITS + QKV), F32),
            pltpu.SemaphoreType.DMA((10,)),
        ],
        compiler_params=pltpu.CompilerParams(vmem_limit_bytes=VMEM_LIMIT),
    )(*ins)


def shards(
    tokens, lengths, order, sequence_adapter, first_norm_gain, first_norm_bias, second_norm_gain, second_norm_bias,
    joined_matrix, joined_offset_bias, output_matrix, output_offset_bias, up_matrix, up_offset_bias, down_matrix,
    down_offset_bias, joined_adapter_reduce, joined_adapter_expand, output_adapter_reduce, output_adapter_expand,
    up_adapter_reduce, up_adapter_expand, down_adapter_reduce, down_adapter_expand, cotangent,
):
    (
        normed, middle, side_o, context, qkv, mask_own, probs, side_q, normed_first, gathered_grad, cot_own,
        joined_full, output_full, up_full, down_full, tokens_own, up_shift_own,
    ) = forward_call(
        (
            first_norm_gain, first_norm_bias, joined_adapter_reduce[0], down_adapter_expand[0],
            joined_adapter_expand[0], joined_offset_bias, order, output_adapter_expand[0], output_offset_bias,
            second_norm_gain, second_norm_bias, up_adapter_reduce[0], lengths, sequence_adapter,
            tokens, cotangent, up_offset_bias, joined_matrix[0], output_matrix[0], output_adapter_reduce[0],
            up_matrix[0], up_adapter_expand[0], down_matrix[0], down_adapter_reduce[0],
        )
    )
    grad, grad_stage, side_u, side_d, shard_feed, out_parts = feed_call(
        (
            normed, middle, up_shift_own, mask_own, second_norm_gain, up_adapter_reduce[0],
            output_adapter_expand[0], gathered_grad, up_full, down_full,
        )
    )
    block_own, input_own, shard_early, shard_late, whole_early, whole_late = back_call(
        (
            first_norm_gain, mask_own, down_offset_bias, side_u, side_o, side_d, grad_stage, output_full, qkv, context,
            tokens_own, cot_own, down_adapter_expand[0], joined_adapter_reduce[0], normed_first, side_q, grad, middle,
            normed, shard_feed, joined_full, out_parts, probs,
        )
    )
    return tuple(finish_call((shard_early, whole_early, shard_late, whole_late, block_own, input_own)))


def solution(mesh):
    spread = P(("dp", "tensor"), None)
    by_dp = P("dp", None)
    rows = P(None, "dp", "tensor")
    cols = P(None, "tensor", "dp")
    last = P(None, None, "tensor")
    middle = P(None, "tensor", None)
    vector = P(None, "tensor")
    return jax.shard_map(
        shards,
        mesh=mesh,
        in_specs=(
            spread, by_dp, by_dp, by_dp, P(), P(), P(), P(), rows, vector, cols, P(), rows, vector, cols, P(),
            P(), last, middle, P(), P(), last, middle, P(), spread,
        ),
        out_specs=(spread, spread, P(), last, middle, P(), P(), last, middle, P()),
        check_vma=False,
    )
```

```python
import functools
import math

import jax
import jax.numpy as jnp
from jax import lax
from jax.experimental import pallas as pl
from jax.experimental.pallas import tpu as pltpu
from jax.sharding import PartitionSpec as P

HEAD = 128
WIDTH = 2048
LANES = 128
WIDE = WIDTH + LANES
ROWS = 160
HALF = ROWS // 2
PAIR = 2 * ROWS
GROUP = 8 * ROWS
QKV = 768
UNITS = 1024
CTX = 256
BLOCK = 32
SCALE = 0.5
EPS = 1e-05
MASKED = -1e30
LOG2E = 1.4426950408889634
VMEM_LIMIT = 60 * 2**20
BF = jnp.bfloat16
F32 = jnp.float32
BY_MESH = pl.DeviceIdType.MESH
ANYWHERE = pl.BlockSpec(memory_space=pl.ANY)
IN_VMEM = pl.BlockSpec(memory_space=pltpu.VMEM)
IN_SMEM = pl.BlockSpec(memory_space=pltpu.SMEM)


def nn(left, right):
    return jnp.dot(left, right, preferred_element_type=F32)


def nt(left, right):
    return lax.dot_general(left, right, (((1,), (1,)), ((), ())), preferred_element_type=F32)


def tn(left, right):
    return lax.dot_general(left, right, (((0,), (0,)), ((), ())), preferred_element_type=F32)


def rows_at(start, size):
    return pl.ds(pl.multiple_of(start, 16), size)


def lanes_at(start, size):
    return pl.ds(pl.multiple_of(start, 128), size)


def loop(count, body):
    def step(index, carry):
        body(index)
        return carry

    lax.fori_loop(0, count, step, 0)


class Place:
    def __init__(self):
        dp = lax.axis_index("dp")
        tensor = lax.axis_index("tensor")
        self.dp = dp
        self.z = lax.div(dp, 4)
        self.xl = lax.rem(lax.div(dp, 2), 2)
        self.c = lax.rem(dp, 2)
        self.y = lax.div(tensor, 2)
        self.g = lax.rem(tensor, 2)
        self.x = self.g * 2 + self.xl
        self.sib = self.at(c=1 - self.c)
        self.up = self.at(y=lax.rem(self.y + 1, 4))
        self.down = self.at(y=lax.rem(self.y + 3, 4))
        self.z_up = self.at(z=lax.rem(self.z + 1, 4))
        self.z_down = self.at(z=lax.rem(self.z + 3, 4))
        self.partner = self.at(g=self.c, c=self.g)
        self.beside = self.at(x=lax.rem(self.x + 2 * self.xl + 3, 4), c=self.g)
        self.home = self.c == self.g
        self.away = self.c != self.g

    def at(self, z=None, x=None, xl=None, c=None, y=None, g=None):
        z = self.z if z is None else z
        c = self.c if c is None else c
        y = self.y if y is None else y
        if x is None:
            xl = self.xl if xl is None else xl
            g = self.g if g is None else g
        else:
            xl = lax.rem(x, 2)
            g = lax.div(x, 2)
        return (z * 4 + xl * 2 + c, y * 2 + g)

    def in_row(self, dx, core):
        return self.at(x=lax.rem(self.x + dx, 4), c=core)

    def row_mates(self):
        return [self.in_row(dx, core) for dx in (1, 2, 3) for core in (0, 1)]

    def column_mates(self):
        return [self.at(z=lax.rem(self.z + dz, 4), c=core) for dz in (1, 2, 3) for core in (0, 1)]

    def ring_mates(self):
        mates = [self.sib]
        for dy in (1, 2, 3):
            y = lax.rem(self.y + dy, 4)
            mates += [self.at(y=y), self.at(y=y, c=1 - self.c)]
        return mates

    def ring(self, dy, same):
        return lax.rem(self.y + dy + 4, 4) * 2 + (self.c if same else 1 - self.c)


def greet(devices):
    barrier = pltpu.get_barrier_semaphore()
    for device in devices:
        pl.semaphore_signal(barrier, 1, device_id=device, device_id_type=BY_MESH)
    pl.semaphore_wait(barrier, len(devices))


def remote(src, dst, send, recv, device):
    return pltpu.make_async_remote_copy(
        src_ref=src, dst_ref=dst, send_sem=send, recv_sem=recv, device_id=device, device_id_type=BY_MESH
    )


class Gather:
    SENDS = (
        (0, True, None),
        (0, True, None),
        (0, True, None),
        (-1, True, 0),
        (1, True, 1),
        (-1, True, None),
        (1, True, None),
        (2, True, 0),
        (2, True, 1),
    )
    LANDS = (
        (0, False, None),
        (-1, True, None),
        (1, True, None),
        (2, True, 0),
        (2, True, 1),
        (-1, False, None),
        (1, False, None),
        (2, False, 0),
        (2, False, 1),
    )

    def __init__(self, place, buf, send, recv):
        self.place, self.buf, self.send, self.recv = place, buf, send, recv
        p = place
        self.to = (p.sib, p.up, p.down, p.up, p.down, p.sib, p.sib, p.sib, p.sib)

    def piece(self, what):
        dy, same, half = what
        start = self.place.ring(dy, same) * ROWS
        if half is None:
            return self.buf.at[rows_at(start, ROWS)]
        return self.buf.at[rows_at(start + half * HALF, HALF)]

    def copy(self, i):
        piece = self.piece(self.SENDS[i])
        return remote(piece, piece, self.send.at[i], self.recv.at[i], self.to[i])

    def landed(self, i):
        piece = self.piece(self.LANDS[i])
        remote(piece, piece, self.send.at[i], self.recv.at[i], self.to[i]).wait_recv()

    def begin(self):
        for i in (1, 2, 0):
            self.copy(i).start()

    def near(self):
        self.landed(1)
        self.copy(3).start()
        self.copy(5).start()
        self.landed(2)
        self.copy(4).start()
        self.copy(6).start()

    def far(self):
        self.landed(3)
        self.copy(7).start()
        self.landed(4)
        self.copy(8).start()

    def own_pair(self):
        self.landed(0)

    def near_pairs(self):
        self.landed(5)
        self.landed(6)

    def far_pair(self):
        self.landed(7)
        self.landed(8)

    def end(self):
        for i in range(9):
            self.copy(i).wait_send()


class Scatter:
    def __init__(self, place, part, sib_in, relay, near, send, recv, start=None):
        self.place, self.part, self.sib_in, self.relay, self.near = place, part, sib_in, relay, near
        self.send, self.recv = send, recv
        self.start = start or (lambda dy: place.ring(dy, True) * ROWS)

    def mine(self, dy, half=None):
        start = self.start(dy)
        if half is None:
            return self.part.at[rows_at(start, ROWS)]
        return self.part.at[rows_at(start + half * HALF, HALF)]

    def others(self, dy):
        return self.part.at[rows_at(self.place.ring(dy, False) * ROWS, ROWS)]

    def copy(self, i):
        p = self.place
        if i < 4:
            src, dst, to = self.others(i), self.sib_in.at[i], p.sib
        elif i == 4:
            src, dst, to = self.mine(2, 0), self.relay.at[0], p.up
        elif i == 5:
            src, dst, to = self.mine(2, 1), self.relay.at[1], p.down
        elif i == 6:
            src, dst, to = self.mine(1, 1), self.near.at[0, pl.ds(HALF, HALF)], p.up
        elif i == 7:
            src, dst, to = self.mine(-1, 0), self.near.at[1, pl.ds(0, HALF)], p.down
        elif i == 8:
            src, dst, to = self.mine(1, 0), self.near.at[0, pl.ds(0, HALF)], p.up
        else:
            src, dst, to = self.mine(-1, 1), self.near.at[1, pl.ds(HALF, HALF)], p.down
        return remote(src, dst, self.send.at[i], self.recv.at[i], to)

    def exchange(self, dy):
        self.copy(dy % 4).start()

    def combine(self, dy):
        self.copy(dy % 4).wait_recv()
        add_rows(self.part, self.start(dy), self.sib_in.at[dy % 4], 0, ROWS)

    def relay_out(self):
        self.copy(4).start()
        self.copy(5).start()

    def near_free(self, dy):
        self.copy(6 if dy == 1 else 7).start()

    def near_rest(self):
        self.copy(4).wait_recv()
        add_rows(self.part, self.start(1), self.relay.at[0], 0, HALF)
        self.copy(8).start()
        self.copy(5).wait_recv()
        add_rows(self.part, self.start(-1) + HALF, self.relay.at[1], 0, HALF)
        self.copy(9).start()

    def arrived(self):
        for i in (6, 7, 8, 9):
            self.copy(i).wait_recv()

    def total(self, start, size, lanes):
        own = self.part[rows_at(self.start(0) + start, size), lanes].astype(F32)
        return (
            own
            + self.near[0, rows_at(start, size), lanes].astype(F32)
            + self.near[1, rows_at(start, size), lanes].astype(F32)
        )

    def end(self, first=0, last=10):
        for i in range(first, last):
            self.copy(i).wait_send()


def scatter_scratch(width=WIDE):
    return [
        pltpu.VMEM((GROUP, width), BF),
        pltpu.VMEM((4, ROWS, width), BF),
        pltpu.VMEM((2, HALF, width), BF),
        pltpu.VMEM((2, ROWS, width), BF),
        pltpu.SemaphoreType.DMA((10,)),
        pltpu.SemaphoreType.DMA((10,)),
    ]


def gather_scratch():
    return [pltpu.VMEM((GROUP, WIDE), BF), pltpu.SemaphoreType.DMA((9,)), pltpu.SemaphoreType.DMA((9,))]


def add_rows(dst, start, src, src_start, count):
    def body(index):
        at = rows_at(start + index * 16, 16)
        dst[at, :] = (dst[at, :].astype(F32) + src[rows_at(src_start + index * 16, 16), :].astype(F32)).astype(BF)

    loop(count // 16, body)


class Weights:
    def __init__(self, place, piece, full, by_rows, cut, send, recv):
        self.place, self.piece, self.full, self.by_rows = place, piece, full, by_rows
        self.send, self.recv = send, recv
        size = piece.shape[1] if by_rows else piece.shape[0]
        self.parts = (pl.ds(0, cut), pl.ds(cut, size - cut))

    def source(self, half):
        part = self.parts[half]
        return self.piece.at[:, part] if self.by_rows else self.piece.at[part, :]

    def slot(self, index, count, half):
        span = lanes_at(index * 128, count * 128)
        part = self.parts[half]
        return self.full.at[span, part] if self.by_rows else self.full.at[part, span]

    def column(self, dz):
        return lax.rem(self.place.z + dz, 4)

    def first(self):
        p = self.place
        marks = (self.recv.at[p.xl * 2 + p.c], self.recv.at[4 + p.z * 2 + p.c])
        slots = (self.slot(p.dp, 1, 0), self.slot(p.dp, 1, 1))
        for d in (2, 1, 3):
            remote(self.source(0), slots[0], self.send.at[d], marks[0], p.in_row(d, p.g)).start()
            remote(self.source(1), slots[1], self.send.at[4 + d], marks[1], p.at(z=self.column(d), c=p.g)).start()

        @pl.when(p.home)
        def _():
            for half in range(2):
                pltpu.make_async_copy(self.source(half), slots[half], marks[half]).start()

        @pl.when(p.away)
        def _():
            for half in range(2):
                remote(self.source(half), slots[half], self.send.at[4 * half], marks[half], p.sib).start()

    def landed(self, slot, mark):
        remote(slot, slot, self.send.at[0], self.recv.at[mark], self.place.sib).wait_recv()

    def along_z(self, i):
        p = self.place
        z, first, count, to = (
            (p.z, 0, 4, p.z_up),
            (p.z, 0, 4, p.z_down),
            (self.column(3), 0, 2, p.z_up),
            (self.column(1), 2, 2, p.z_down),
        )[i]
        block = self.slot(z * 4 + first, count, 0)
        return remote(block, block, self.send.at[8 + i], self.recv.at[12 + i], to)

    def along_x(self, z, dx):
        p = self.place
        pair = self.slot(z * 4 + p.xl * 2, 2, 1)
        mark = self.send.at[12 + z * 2 + dx // 2]
        return remote(pair, pair, mark, self.recv.at[16 + p.xl * 4 + z], p.in_row(dx, p.c))

    def second(self):
        p = self.place
        for index in range(4):
            self.landed(self.slot(p.z * 4 + index, 1, 0), index)
        self.along_z(0).start()
        self.along_z(1).start()

        @pl.when(p.home)
        def _():
            for z in range(4):
                for core in range(2):
                    self.landed(self.slot(z * 4 + p.xl * 2 + core, 1, 1), 4 + z * 2 + core)
                self.along_x(z, 1).start()
                self.along_x(z, 3).start()

    def passed_on(self, i):
        p = self.place
        home = 1 - lax.rem(p.c + p.g, 2)
        plus = 1 - lax.rem(p.xl + home, 2)
        z = (1 - plus) * 2 + i
        pair = self.slot(z * 4 + (1 - p.xl) * 2, 2, 1)
        mark = self.recv.at[16 + (1 - p.xl) * 4 + z]
        return remote(pair, pair, self.send.at[20 + i], mark, p.in_row(3 - 2 * plus, p.c))

    def third(self):
        p = self.place
        self.landed(self.slot(self.column(3) * 4, 4, 0), 12)
        self.along_z(2).start()
        self.landed(self.slot(self.column(1) * 4, 4, 0), 13)
        self.along_z(3).start()
        for z in range(4):
            self.landed(self.slot(z * 4 + (1 - p.xl) * 2, 2, 1), 16 + (1 - p.xl) * 4 + z)
        for i in range(2):
            self.passed_on(i).start()

    def arrived(self):
        p = self.place
        self.landed(self.slot(self.column(2) * 4, 2, 0), 14)
        self.landed(self.slot(self.column(2) * 4 + 2, 2, 0), 15)

        @pl.when(p.away)
        def _():
            for z in range(4):
                self.landed(self.slot(z * 4 + p.xl * 2, 2, 1), 16 + p.xl * 4 + z)

    def end(self):
        p = self.place
        for d in (1, 2, 3):
            for half in range(2):
                slot = self.slot(p.dp, 1, half)
                remote(self.source(half), slot, self.send.at[4 * half + d], self.recv.at[0], p.sib).wait_send()
        for i in range(4):
            self.along_z(i).wait_send()
        for i in range(2):
            self.passed_on(i).wait_send()

        @pl.when(p.away)
        def _():
            for half in range(2):
                slot = self.slot(p.dp, 1, half)
                remote(self.source(half), slot, self.send.at[4 * half], self.recv.at[0], p.sib).wait_send()

        @pl.when(p.home)
        def _():
            for z in range(4):
                self.along_x(z, 1).wait_send()
                self.along_x(z, 3).wait_send()


def weight_marks():
    return [pltpu.SemaphoreType.DMA((22,)), pltpu.SemaphoreType.DMA((24,))]


class Swap:
    def __init__(self, place, pairs, send, recv, shared=()):
        self.place, self.pairs, self.send, self.recv, self.shared = place, pairs, send, recv, shared

    def begin(self, i):
        src, dst = self.pairs[i]
        p = self.place

        @pl.when(p.home)
        def _():
            pltpu.make_async_copy(src, dst, self.recv.at[i]).start()

        @pl.when(p.away)
        def _():
            device = p.beside if i in self.shared else p.partner
            remote(src, dst, self.send.at[i], self.recv.at[i], device).start()

    def arrived(self, i):
        src, dst = self.pairs[i]
        remote(src, dst, self.send.at[i], self.recv.at[i], self.place.sib).wait_recv()

    def end(self):
        @pl.when(self.place.away)
        def _():
            for i, (src, dst) in enumerate(self.pairs):
                remote(src, dst, self.send.at[i], self.recv.at[i], self.place.sib).wait_send()


def swap_marks(count):
    return [pltpu.SemaphoreType.DMA((count,)), pltpu.SemaphoreType.DMA((count,))]


def normalise(value):
    mean = jnp.mean(value, axis=-1, keepdims=True)
    center = value - mean
    inverse = lax.rsqrt(jnp.mean(center * center, axis=-1, keepdims=True) + EPS)
    return center * inverse, inverse


def norm_back(value, gain, grad):
    normed, inverse = normalise(value)
    e = grad * gain
    return (e - jnp.mean(e, axis=-1, keepdims=True) - normed * jnp.mean(e * normed, axis=-1, keepdims=True)) * inverse


def pair_rows(place, dy):
    return rows_at(lax.rem(place.y + dy + 4, 4) * PAIR, PAIR)


def wide_product(put, make):
    loop(4, lambda j: put(lanes_at(j * 512, 512), make(lanes_at(j * 512, 512))))
    put(pl.ds(WIDTH, LANES), make(pl.ds(WIDTH, LANES)))


def call(kernel, collective, ins, specs, outs, out_specs, scratch):
    return pl.pallas_call(
        kernel,
        name=kernel.__name__,
        out_shape=outs,
        in_specs=specs,
        out_specs=out_specs,
        scratch_shapes=scratch,
        compiler_params=pltpu.CompilerParams(
            collective_id=collective, has_side_effects=True, vmem_limit_bytes=VMEM_LIMIT
        ),
    )(*ins)


def shape(*dims, kind=BF):
    return jax.ShapeDtypeStruct(dims, kind)


def identity():
    row = lax.broadcasted_iota(jnp.int32, (LANES, LANES), 0)
    return jnp.where(row == lax.broadcasted_iota(jnp.int32, (LANES, LANES), 1), 1.0, 0.0).astype(BF)


def query_info(token_row, start_row):
    token_high = jnp.floor(token_row * (1.0 / 16.0))
    start_high = jnp.floor(start_row * (1.0 / 16.0))
    digit = lax.broadcasted_iota(jnp.int32, (16, GROUP), 0)
    digits = jnp.where(digit == 0, token_high, 0.0)
    digits = jnp.where(digit == 1, token_row - 16.0 * token_high, digits)
    digits = jnp.where(digit == 2, start_high, digits)
    digits = jnp.where(digit == 3, start_row - 16.0 * start_high, digits)
    row = lax.broadcasted_iota(jnp.int32, (16, LANES), 0)
    lane = lax.broadcasted_iota(jnp.int32, (16, LANES), 1)
    worth = jnp.where((row == 0) & (lane == 0) | (row == 2) & (lane == 1), 16.0, 0.0)
    worth = worth + jnp.where((row == 1) & (lane == 0) | (row == 3) & (lane == 1), 1.0, 0.0)
    return tn(digits.astype(BF), worth.astype(BF))


def slope_row(place, head, tokens_row):
    number = (place.ring(0, True) * 2 + head + 1).astype(F32)
    slope = jnp.exp2(jnp.full((1, GROUP), -0.5, F32) * number)
    return slope * LOG2E * tokens_row


def forward_kernel(
    gain, shift, joined_reduce, down_expand, joined_expand, joined_shift, order, output_expand, output_shift,
    second_gain, second_shift, up_reduce, lengths, adapters,
    tokens, cotangent, up_shift, joined_piece, output_piece, output_reduce, up_piece, up_expand, down_piece, down_reduce,
    normed, middle, side_o, context, qkv, mask_own,
    probs_out, side_q, normed_own, gathered_grad, cot_own, joined_full, output_full, up_full, down_full, tokens_own,
    up_shift_own,
    tok_here, aux, aux_here, half_expand, shift_here, joined_here, output_here, info, mask_all, probs,
    rows, rows_send, rows_recv, grads, grads_send, grads_recv, part, sib_in, relay, near, s_send, s_recv,
    w_send, w_recv, o_send, o_recv, u_send, u_recv, d_send, d_recv, swap_send, swap_recv, out_sem, probs_sem,
):
    p = Place()
    greet([p.sib, p.up, p.down] + p.row_mates() + p.column_mates())
    joined = Weights(p, joined_piece, joined_here.at[pl.ds(0, WIDTH)], True, 512, w_send, w_recv)
    output = Weights(p, output_piece, output_here.at[:, pl.ds(0, WIDTH)], False, 160, o_send, o_recv)
    up = Weights(p, up_piece, up_full.at[pl.ds(0, WIDTH)], True, 640, u_send, u_recv)
    down = Weights(p, down_piece, down_full.at[:, pl.ds(0, WIDTH)], False, 640, d_send, d_recv)
    own_rows = rows_at(p.ring(0, True) * ROWS, ROWS)
    their_rows = rows_at((p.y * 2 + p.g) * ROWS, ROWS)
    swap = Swap(
        p,
        [
            (tokens, tok_here),
            (aux, aux_here),
            (half_expand, joined_here.at[pl.ds(WIDTH, LANES)]),
            (joined_shift, shift_here),
            (cotangent, grads.at[their_rows, pl.ds(0, WIDTH)]),
            (output_reduce, output_here.at[:, pl.ds(WIDTH, LANES)]),
            (up_expand, up_full.at[pl.ds(WIDTH, LANES)]),
            (down_reduce, down_full.at[:, pl.ds(WIDTH, LANES)]),
            (up_shift, up_shift_own),
        ],
        swap_send,
        swap_recv,
        (2, 3, 5, 6, 7, 8),
    )
    joined.first()
    swap.begin(0)
    token = order[...]
    first_end = lengths[0, 0]
    second_end = first_end + lengths[0, 1]
    later = token >= second_end
    late = token >= first_end
    start = jnp.where(later, second_end, jnp.where(late, first_end, 0))
    adapter = jnp.where(later, adapters[0, 2], jnp.where(late, adapters[0, 1], adapters[0, 0]))
    for i, row in enumerate((token, start, adapter)):
        aux[:, pl.ds(i * GROUP, GROUP)] = jnp.broadcast_to(row.astype(F32), (8, GROUP))
    half_expand[...] = (SCALE * joined_expand[...].astype(F32)).astype(BF)
    for i in (1, 2, 3):
        swap.begin(i)
    swap.arrived(1)
    token_row = aux_here[0:1, pl.ds(0, GROUP)]
    info[...] = query_info(token_row, aux_here[0:1, pl.ds(GROUP, GROUP)])
    column = lax.shift_right_logical(lax.broadcasted_iota(jnp.int32, (LANES, GROUP), 0), 4).astype(F32)
    chosen = jnp.where(column == aux_here[0:1, pl.ds(2 * GROUP, GROUP)], 1.0, 0.0).astype(BF)
    mask_all[...] = tn(chosen, identity()).astype(BF)
    mask_own[...] = mask_all[own_rows, :]
    mask_rows = mask_all[own_rows, :].astype(F32)
    joined.second()
    swap.arrived(0)

    def norm_block(index):
        at = rows_at(index * BLOCK, BLOCK)
        value, _ = normalise(tok_here[at, :].astype(F32))
        rows[rows_at(p.ring(0, True) * ROWS + index * BLOCK, BLOCK), pl.ds(0, WIDTH)] = (
            value * gain[...] + shift[...]
        ).astype(BF)

    loop(ROWS // BLOCK, norm_block)
    rows[own_rows, pl.ds(WIDTH, LANES)] = (
        mask_rows * nn(rows[own_rows, pl.ds(0, WIDTH)], joined_reduce[...])
    ).astype(BF)
    gather = Gather(p, rows, rows_send, rows_recv)
    gather_grad = Gather(p, grads, grads_send, grads_recv)
    gather.begin()
    swap.begin(4)
    output.first()
    joined.third()
    up.first()
    down.first()
    for i in range(5, 9):
        swap.begin(i)
    output.second()
    swap.arrived(4)
    grads[own_rows, pl.ds(WIDTH, LANES)] = (
        mask_rows * (SCALE * nt(grads[own_rows, pl.ds(0, WIDTH)], down_expand[...]))
    ).astype(BF)
    copies = [
        pltpu.make_async_copy(tok_here, tokens_own, out_sem.at[0]),
        pltpu.make_async_copy(grads.at[own_rows, pl.ds(0, WIDTH)], cot_own, out_sem.at[1]),
        pltpu.make_async_copy(rows.at[own_rows, pl.ds(0, WIDTH)], normed_own, out_sem.at[2]),
    ]
    for copy in copies:
        copy.start()
    gather.near()
    gather_grad.begin()
    up.second()
    swap.arrived(2)
    swap.arrived(3)
    joined.arrived()
    copies.append(pltpu.make_async_copy(joined_here, joined_full, out_sem.at[3]))
    copies[-1].start()

    def project(dy):
        at = pair_rows(p, dy)

        def body(j):
            lanes = lanes_at(j * 256, 256)
            qkv[at, lanes] = (nn(rows[at, :], joined_here[:, lanes]) + shift_here[:, lanes]).astype(BF)

        loop(QKV // 256, body)

    gather.own_pair()
    project(0)
    gather.near_pairs()
    project(1)
    output.third()
    project(-1)
    gather.far()
    down.second()
    gather.far_pair()
    project(2)
    up.third()
    copies.append(pltpu.make_async_copy(rows.at[:, pl.ds(WIDTH, LANES)], side_q, out_sem.at[4]))
    copies[-1].start()
    output.arrived()
    swap.arrived(5)
    copies.append(pltpu.make_async_copy(output_here, output_full, out_sem.at[5]))
    copies[-1].start()
    probs_copies = []

    def attend(dy, same):
        at = rows_at(p.ring(dy, same) * ROWS, ROWS)
        n = len(probs_copies)
        if n >= 2:
            probs_copies[n - 2].wait()
        query_token = info[at, 0:1]
        query_start = info[at, 1:2]
        allowed = (token_row <= query_token) & (token_row >= query_start)
        for head in range(2):
            first = head * 3 * HEAD
            scores = nt(qkv[at, first : first + HEAD], qkv[:, first + HEAD : first + 2 * HEAD])
            scores = scores * (LOG2E / math.sqrt(HEAD)) + slope_row(p, head, token_row)
            scores = jnp.where(allowed, scores, MASKED)
            top = jnp.max(scores, axis=-1, keepdims=True)
            weights = jnp.exp2(scores - top)
            total = jnp.sum(weights, axis=-1, keepdims=True)
            weights = (weights * (1.0 / total)).astype(BF)
            probs[n % 2, head] = weights
            context[at, head * HEAD : (head + 1) * HEAD] = nn(
                weights, qkv[:, first + 2 * HEAD : first + 3 * HEAD]
            ).astype(BF)
        copy = pltpu.make_async_copy(probs.at[n % 2], probs_out.at[:, at], probs_sem.at[n])
        copy.start()
        probs_copies.append(copy)

        def put(lanes, value):
            part[at, lanes] = value.astype(BF)

        wide_product(put, lambda lanes: nn(context[at, :], output_here[:, lanes]))

    scatter = Scatter(p, part, sib_in, relay, near, s_send, s_recv)
    attend(2, False)
    scatter.exchange(2)
    attend(2, True)
    scatter.combine(2)
    scatter.relay_out()
    gather_grad.near()
    attend(1, False)
    scatter.exchange(1)
    attend(1, True)
    scatter.combine(1)
    scatter.near_free(1)
    down.third()
    attend(-1, False)
    scatter.exchange(-1)
    attend(-1, True)
    scatter.combine(-1)
    scatter.near_free(-1)
    gather_grad.far()
    attend(0, False)
    scatter.exchange(0)
    scatter.near_rest()
    attend(0, True)
    scatter.combine(0)
    gather_grad.own_pair()
    gather_grad.near_pairs()
    gather_grad.far_pair()
    copies.append(pltpu.make_async_copy(grads, gathered_grad, out_sem.at[6]))
    copies[-1].start()
    scatter.arrived()
    side = (mask_rows * scatter.total(0, ROWS, pl.ds(WIDTH, LANES))).astype(BF)
    side_o[...] = side

    def add_tile(j):
        lanes = lanes_at(j * 512, 512)
        middle[:, lanes] = (
            tok_here[:, lanes].astype(F32)
            + scatter.total(0, ROWS, lanes)
            + output_shift[:, lanes]
            + SCALE * nn(side, output_expand[:, lanes])
        )

    loop(4, add_tile)

    def second_block(index):
        at = rows_at(index * BLOCK, BLOCK)
        value, _ = normalise(middle[at, :])
        normed[at, pl.ds(0, WIDTH)] = (value * second_gain[...] + second_shift[...]).astype(BF)

    loop(ROWS // BLOCK, second_block)
    normed[:, pl.ds(WIDTH, LANES)] = (mask_rows * nn(normed[:, pl.ds(0, WIDTH)], up_reduce[...])).astype(BF)
    up.arrived()
    down.arrived()
    for i in range(6, 9):
        swap.arrived(i)
    swap.end()
    for sender in (gather, gather_grad, scatter, joined, output, up, down):
        sender.end()
    for copy in copies + probs_copies[-2:]:
        copy.wait()


def forward_call(ins):
    outs = [
        shape(ROWS, WIDE), shape(ROWS, WIDTH, kind=F32), shape(ROWS, LANES), shape(GROUP, CTX), shape(GROUP, QKV),
        shape(ROWS, LANES),
        shape(2, GROUP, GROUP), shape(GROUP, LANES), shape(ROWS, WIDTH), shape(GROUP, WIDE), shape(ROWS, WIDTH),
        shape(WIDE, QKV), shape(CTX, WIDE), shape(WIDE, UNITS), shape(UNITS, WIDE), shape(ROWS, WIDTH),
        shape(1, UNITS, kind=F32),
    ]
    return call(
        forward_kernel,
        1,
        ins,
        [IN_VMEM] * 12 + [IN_SMEM] * 2 + [ANYWHERE] * 10,
        outs,
        [IN_VMEM] * 6 + [ANYWHERE] * 11,
        [
            pltpu.VMEM((ROWS, WIDTH), BF), pltpu.VMEM((8, 3 * GROUP), F32), pltpu.VMEM((8, 3 * GROUP), F32),
            pltpu.VMEM((LANES, QKV), BF), pltpu.VMEM((1, QKV), F32), pltpu.VMEM((WIDE, QKV), BF),
            pltpu.VMEM((CTX, WIDE), BF), pltpu.VMEM((GROUP, LANES), F32), pltpu.VMEM((GROUP, LANES), BF),
            pltpu.VMEM((2, 2, ROWS, GROUP), BF), *gather_scratch(), *gather_scratch(), *scatter_scratch(),
            *weight_marks(), *weight_marks(), *weight_marks(), *weight_marks(), *swap_marks(9),
            pltpu.SemaphoreType.DMA((7,)), pltpu.SemaphoreType.DMA((8,)),
        ],
    )


class SideSum:
    def __init__(self, place, part, landing, send, recv):
        self.place, self.part, self.landing = place, part, landing
        self.copies = []
        for k in range(1, 8):
            y = lax.rem(place.y + k // 2, 4)
            core = place.c if k % 2 == 0 else 1 - place.c
            piece = part.at[rows_at((y * 2 + core) * ROWS, ROWS)]
            self.copies.append(remote(piece, landing.at[k], send.at[k], recv.at[k], place.at(y=y, c=core)))

    def open(self):
        for copy in self.copies:
            copy.start()

    def total(self):
        total = self.part[rows_at(self.place.ring(0, True) * ROWS, ROWS), :].astype(F32)
        for k in range(1, 8):
            self.copies[k - 1].wait_recv()
            total = total + self.landing[k].astype(F32)
        return total

    def end(self):
        for copy in self.copies:
            copy.wait_send()


def side_scratch():
    dma = pltpu.SemaphoreType.DMA
    return [pltpu.VMEM((GROUP, LANES), BF), pltpu.VMEM((8, ROWS, LANES), BF), dma((8,)), dma((8,))]


def feed_kernel(
    normed, middle, up_shift, mask, gain, up_reduce, output_expand,
    gathered_grad, up_weights, down_weights,
    grad_out, grad_stage, side_u, side_d, by_shard, out_parts,
    up_full, down_full, grads, rows, rows_send, rows_recv, act, slope, part, sib_in, relay, near, s_send, s_recv,
    part_out, sib_in_out, t_send, t_recv, side_part, side_in, side_send, side_recv, own_sem,
):
    p = Place()
    own_rows = rows_at(p.ring(0, True) * ROWS, ROWS)
    stage = pltpu.make_async_copy(normed, rows.at[own_rows], own_sem.at[0])
    stage.start()
    load_down = pltpu.make_async_copy(down_weights, down_full, own_sem.at[1])
    load_down.start()
    load_grads = pltpu.make_async_copy(gathered_grad, grads, own_sem.at[2])
    load_grads.start()
    load_up = pltpu.make_async_copy(up_weights, up_full, own_sem.at[3])
    load_up.start()
    greet(p.ring_mates())
    gather = Gather(p, rows, rows_send, rows_recv)
    stage.wait()
    gather.begin()

    def lift(j):
        lanes = lanes_at(j * 256, 256)
        slope[:, lanes] = nt(grads[...], down_full[lanes, :]).astype(BF)

    def hide(dy):
        at = pair_rows(p, dy)

        def body(j):
            lanes = lanes_at(j * 256, 256)
            v = nn(rows[at, :], up_full[:, lanes]) + up_shift[:, lanes]
            square = v * v
            t = jnp.tanh(v * (0.7978845608028654 + 0.7978845608028654 * 0.044715 * square))
            half = 0.5 + 0.5 * t
            act[at, lanes] = (v * half).astype(BF)
            bend = half + v * (1.0 - t * t) * (
                0.5 * 0.7978845608028654 + 0.5 * 0.7978845608028654 * 3.0 * 0.044715 * square
            )
            slope[at, lanes] = (slope[at, lanes].astype(F32) * bend).astype(BF)

        loop(UNITS // 256, body)

    def back(dy):
        at = pair_rows(p, dy)

        def put(lanes, value):
            part[at, lanes] = value.astype(BF)

        wide_product(put, lambda lanes: nt(slope[at, :], up_full[lanes, :]))

    def forth(dy):
        at = pair_rows(p, dy)

        def body(j):
            lanes = lanes_at(j * 512, 512)
            part_out[at, lanes] = nn(act[at, :], down_full[:, lanes]).astype(BF)

        loop(WIDTH // 512, body)

    load_down.wait()
    load_grads.wait()
    loop(UNITS // 256, lift)
    load_up.wait()
    expand = pl.ds(WIDTH, LANES)
    up_full[expand, :] = (SCALE * up_full[expand, :].astype(F32)).astype(BF)
    scatter = Scatter(p, part, sib_in, relay, near, s_send, s_recv)
    scatter_out = Scatter(p, part_out, sib_in_out, None, None, t_send, t_recv)
    gather.own_pair()
    hide(0)
    gather.near()
    gather.near_pairs()
    hide(1)
    hide(-1)
    back(1)
    scatter.exchange(1)
    gather.far()
    back(-1)
    scatter.exchange(-1)
    gather.far_pair()
    scatter.combine(1)
    scatter.near_free(1)
    scatter.combine(-1)
    scatter.near_free(-1)
    hide(2)
    back(2)
    scatter.exchange(2)
    back(0)
    scatter.combine(2)
    scatter.relay_out()
    scatter.exchange(0)
    forth(2)
    scatter_out.exchange(2)
    scatter.near_rest()
    scatter.combine(0)
    side_part[...] = nn(act[...], down_full[:, pl.ds(WIDTH, LANES)]).astype(BF)
    side = SideSum(p, side_part, side_in, side_send, side_recv)
    side.open()
    for dy in (1, -1, 0):
        forth(dy)
        scatter_out.exchange(dy)

    def by_unit(j):
        at = lanes_at(j * 256, 256)
        by_shard[at, :] = tn(act[:, at], grads[:, pl.ds(WIDTH, LANES)]).astype(BF)
        by_shard[lanes_at(UNITS + j * 256, 256), :] = (
            SCALE * tn(slope[:, at], rows[:, pl.ds(WIDTH, LANES)])
        ).astype(BF)

    loop(UNITS // 256, by_unit)
    mask_rows = mask[...].astype(F32)
    for dy in range(4):
        scatter_out.combine(dy)
    copies = []

    def hand_on(src, start, count):
        copy = pltpu.make_async_copy(src, out_parts.at[pl.ds(start, count)], own_sem.at[4 + len(copies)])
        copy.start()
        copies.append(copy)

    for dy in range(4):
        hand_on(scatter_out.mine(dy), dy * ROWS, ROWS)
    scatter.arrived()
    side_u[...] = (mask_rows * scatter.total(0, ROWS, pl.ds(WIDTH, LANES))).astype(BF)

    def norm_block(index):
        at = rows_at(index * BLOCK, BLOCK)
        mine = rows_at(p.ring(0, True) * ROWS + index * BLOCK, BLOCK)
        grad = scatter.total(index * BLOCK, BLOCK, pl.ds(0, WIDTH)) + nt(side_u[at, :], up_reduce[...])
        grad = grads[mine, pl.ds(0, WIDTH)].astype(F32) + norm_back(middle[at, :], gain[...], grad)
        grad_out[at, :] = grad
        grad_stage[at, pl.ds(0, WIDTH)] = grad.astype(BF)

    loop(ROWS // BLOCK, norm_block)
    grad_stage[:, pl.ds(WIDTH, LANES)] = (
        mask_rows * (SCALE * nt(grad_stage[:, pl.ds(0, WIDTH)], output_expand[...]))
    ).astype(BF)
    side_d[...] = (mask_rows * side.total()).astype(BF)
    gather.end()
    side.end()
    scatter.end()
    scatter_out.end(0, 4)
    for copy in copies:
        copy.wait()


def feed_call(ins):
    outs = [
        shape(ROWS, WIDTH, kind=F32), shape(ROWS, WIDE), shape(ROWS, LANES), shape(ROWS, LANES),
        shape(2 * UNITS, LANES), shape(4 * ROWS, WIDTH),
    ]
    scratch = scatter_scratch(WIDTH)
    return call(
        feed_kernel,
        2,
        ins,
        [IN_VMEM] * 7 + [ANYWHERE] * 3,
        outs,
        [IN_VMEM] * 5 + [ANYWHERE],
        [
            pltpu.VMEM((WIDE, UNITS), BF), pltpu.VMEM((UNITS, WIDE), BF), pltpu.VMEM((GROUP, WIDE), BF),
            *gather_scratch(), pltpu.VMEM((GROUP, UNITS), BF), pltpu.VMEM((GROUP, UNITS), BF), *scatter_scratch(),
            scratch[0], scratch[1], scratch[4], scratch[5], *side_scratch(), pltpu.SemaphoreType.DMA((8,)),
        ],
    )


class Reducer:
    def __init__(self, place, source, sib_mark):
        self.p, self.source, self.sib_mark = place, source, sib_mark
        self.m = place.z * 4 + place.x
        self.sent = []

    @staticmethod
    def mates(place):
        m = place.z * 4 + place.x
        mates = []
        for k in range(1, 16):
            other = lax.rem(m + k, 16)
            for core in (0, 1):
                mates.append(place.at(z=lax.div(other, 4), x=lax.rem(other, 4), c=core))
        return mates

    def member(self, k):
        other = lax.rem(self.m + k, 16)
        return other, self.p.at(z=lax.div(other, 4), x=lax.rem(other, 4))

    def push(self, src, dst, send, recv, device):
        copy = remote(src, dst, send, recv, device)
        copy.start()
        self.sent.append(copy)

    def await_at(self, dst, recv):
        remote(dst, dst, self.sib_mark, recv, self.p.sib).wait_recv()

    def close(self):
        for copy in self.sent:
            copy.wait_send()


class ShardSum(Reducer):
    def __init__(self, place, source, refs):
        (
            self.landing, self.total, self.all, self.a_send, self.a_recv, self.c_send, self.c_recv,
        ) = refs
        super().__init__(place, source, self.a_send.at[0])
        self.cut = source.shape[0] // 16

    @staticmethod
    def scratch(count):
        dma = pltpu.SemaphoreType.DMA
        cut = count // 16
        return [
            pltpu.VMEM((16, cut, LANES), BF), pltpu.VMEM((cut, LANES), BF), pltpu.VMEM((count, LANES), BF),
            dma((16,)), dma((16,)), dma((16,)), dma((16,)),
        ]

    def open(self):
        for k in range(1, 16):
            other, device = self.member(k)
            piece = self.source.at[rows_at(other * self.cut, self.cut)]
            self.push(piece, self.landing.at[k], self.a_send.at[k], self.a_recv.at[k], device)

    def spread(self):
        p = self.p
        total = self.source[rows_at(self.m * self.cut, self.cut), :].astype(F32)
        for k in range(1, 16):
            self.await_at(self.landing.at[k], self.a_recv.at[k])
            total = total + self.landing[k].astype(F32)
        self.total[...] = total.astype(BF)
        mine = self.all.at[rows_at(self.m * self.cut, self.cut)]
        mark = self.c_recv.at[self.m]
        for n in range(1, 16):
            device = p.at(
                z=lax.rem(p.z + n // 4, 4), xl=lax.rem(p.xl + n // 2 % 2, 2), g=p.c, c=lax.rem(p.c + n % 2, 2)
            )
            self.push(self.total, mine, self.c_send.at[n], mark, device)
        self.swapped = remote(self.total, mine, self.c_send.at[0], mark, p.at(g=p.c))
        pl.when(p.away)(self.swapped.start)
        pl.when(p.home)(pltpu.make_async_copy(self.total, mine, mark).start)

    def close(self):
        for index in range(16):
            self.await_at(self.all.at[pl.ds(index * self.cut, self.cut)], self.c_recv.at[index])
        super().close()
        pl.when(self.p.away)(self.swapped.wait_send)


class WholeSum(Reducer):
    def __init__(self, place, source, refs):
        (
            self.sib_in, self.here, self.landing, self.slice_sum, self.bits_in, self.bit_sum, self.all,
            self.b_send, self.b_recv, self.d_send, self.d_recv, self.e_send, self.e_recv, self.f_send, self.f_recv,
            self.g_send, self.g_recv, self.mark,
        ) = refs
        super().__init__(place, source, self.f_send.at[0])
        self.half = source.shape[0] // 2
        self.slice = self.half // 16
        self.bit = self.slice // 4
        self.base = place.c * self.half + self.m * self.slice

    @staticmethod
    def scratch(count):
        dma = pltpu.SemaphoreType.DMA
        half = count // 2
        piece = half // 16
        return [
            pltpu.VMEM((half, LANES), BF), pltpu.VMEM((half, LANES), BF), pltpu.VMEM((16, piece, LANES), BF),
            pltpu.VMEM((piece, LANES), BF), pltpu.VMEM((4, piece // 4, LANES), BF), pltpu.VMEM((piece // 4, LANES), BF),
            pltpu.VMEM((count, LANES), BF),
            dma((16,)), dma((16,)), dma((4,)), dma((4,)), dma((4,)), dma((4,)), dma((2,)), dma((2,)),
            dma((16,)), dma((16,)), dma((1,)),
        ]

    def open(self):
        there = rows_at((1 - self.p.c) * self.half, self.half)
        self.push(self.source.at[there], self.sib_in, self.f_send.at[0], self.f_recv.at[0], self.p.sib)

    def halves(self):
        self.await_at(self.sib_in, self.f_recv.at[0])

        def body(index):
            at = rows_at(index * 128, 128)
            mine = self.source[rows_at(self.p.c * self.half + index * 128, 128), :].astype(F32)
            self.here[at, :] = (mine + self.sib_in[at, :].astype(F32)).astype(BF)

        loop(self.half // 128, body)
        for k in range(1, 16):
            other, device = self.member(k)
            piece = self.here.at[rows_at(other * self.slice, self.slice)]
            self.push(piece, self.landing.at[k], self.b_send.at[k], self.b_recv.at[k], device)

    def slices(self):
        total = self.here[rows_at(self.m * self.slice, self.slice), :].astype(F32)
        for k in range(1, 16):
            self.await_at(self.landing.at[k], self.b_recv.at[k])
            total = total + self.landing[k].astype(F32)
        self.slice_sum[...] = total.astype(BF)
        for dy in (2, 1, 3):
            other = lax.rem(self.p.y + dy, 4)
            piece = self.slice_sum.at[rows_at(other * self.bit, self.bit)]
            self.push(piece, self.bits_in.at[dy], self.d_send.at[dy], self.d_recv.at[dy], self.p.at(y=other))

    def bits(self):
        total = self.slice_sum[rows_at(self.p.y * self.bit, self.bit), :].astype(F32)
        for dy in (1, 3, 2):
            self.await_at(self.bits_in.at[dy], self.d_recv.at[dy])
            total = total + self.bits_in[dy].astype(F32)
        self.bit_sum[...] = total.astype(BF)
        own = self.all.at[rows_at(self.base + self.p.y * self.bit, self.bit)]
        self.placed = pltpu.make_async_copy(self.bit_sum, own, self.mark.at[0])
        self.placed.start()
        for dy in (2, 1, 3):
            device = self.p.at(y=lax.rem(self.p.y + dy, 4))
            self.push(self.bit_sum, own, self.e_send.at[dy], self.e_recv.at[dy], device)

    def slices_back(self):
        self.placed.wait()
        for dy in (1, 3, 2):
            source = lax.rem(self.p.y + 4 - dy, 4)
            self.await_at(self.all.at[rows_at(self.base + source * self.bit, self.bit)], self.e_recv.at[dy])
        own = self.all.at[rows_at(self.base, self.slice)]
        for k in range(1, 16):
            self.push(own, own, self.g_send.at[k], self.g_recv.at[k], self.member(k)[1])

    def halves_back(self):
        for k in range(1, 16):
            source = lax.rem(self.m + 16 - k, 16)
            landing = self.all.at[rows_at(self.p.c * self.half + source * self.slice, self.slice)]
            self.await_at(landing, self.g_recv.at[k])
        half = self.all.at[rows_at(self.p.c * self.half, self.half)]
        self.push(half, half, self.f_send.at[1], self.f_recv.at[1], self.p.sib)

    def close(self):
        self.await_at(self.all.at[rows_at((1 - self.p.c) * self.half, self.half)], self.f_recv.at[1])
        super().close()


class PlaneSum(Reducer):
    def __init__(self, place, source, refs):
        (
            self.landing, self.slice_sum, self.bits_in, self.bit_sum, self.all,
            self.b_send, self.b_recv, self.d_send, self.d_recv, self.e_send, self.e_recv, self.g_send, self.g_recv,
            self.mark,
        ) = refs
        super().__init__(place, source, self.b_send.at[0])
        self.q = self.m * 2 + place.c
        self.slice = source.shape[0] // 32
        self.bit = self.slice // 4
        self.base = self.q * self.slice

    @staticmethod
    def scratch(count):
        dma = pltpu.SemaphoreType.DMA
        piece = count // 32
        return [
            pltpu.VMEM((32, piece, LANES), BF), pltpu.VMEM((piece, LANES), BF), pltpu.VMEM((4, piece // 4, LANES), BF),
            pltpu.VMEM((piece // 4, LANES), BF), pltpu.VMEM((count, LANES), BF),
            dma((32,)), dma((32,)), dma((4,)), dma((4,)), dma((4,)), dma((4,)), dma((32,)), dma((32,)), dma((1,)),
        ]

    def mate(self, k):
        other = lax.rem(self.q + k, 32)
        m = lax.div(other, 2)
        return other, self.p.at(z=lax.div(m, 4), x=lax.rem(m, 4), c=lax.rem(other, 2))

    def open(self):
        for k in range(1, 32):
            other, device = self.mate(k)
            piece = self.source.at[rows_at(other * self.slice, self.slice)]
            self.push(piece, self.landing.at[k], self.b_send.at[k], self.b_recv.at[k], device)

    def slices(self):
        total = self.source[rows_at(self.base, self.slice), :].astype(F32)
        for k in range(1, 32):
            self.await_at(self.landing.at[k], self.b_recv.at[k])
            total = total + self.landing[k].astype(F32)
        self.slice_sum[...] = total.astype(BF)
        for dy in (2, 1, 3):
            other = lax.rem(self.p.y + dy, 4)
            piece = self.slice_sum.at[rows_at(other * self.bit, self.bit)]
            self.push(piece, self.bits_in.at[dy], self.d_send.at[dy], self.d_recv.at[dy], self.p.at(y=other))

    def bits(self):
        total = self.slice_sum[rows_at(self.p.y * self.bit, self.bit), :].astype(F32)
        for dy in (1, 3, 2):
            self.await_at(self.bits_in.at[dy], self.d_recv.at[dy])
            total = total + self.bits_in[dy].astype(F32)
        self.bit_sum[...] = total.astype(BF)
        own = self.all.at[rows_at(self.base + self.p.y * self.bit, self.bit)]
        self.placed = pltpu.make_async_copy(self.bit_sum, own, self.mark.at[0])
        self.placed.start()
        for dy in (2, 1, 3):
            device = self.p.at(y=lax.rem(self.p.y + dy, 4))
            self.push(self.bit_sum, own, self.e_send.at[dy], self.e_recv.at[dy], device)

    def slices_back(self):
        self.placed.wait()
        for dy in (1, 3, 2):
            source = lax.rem(self.p.y + 4 - dy, 4)
            self.await_at(self.all.at[rows_at(self.base + source * self.bit, self.bit)], self.e_recv.at[dy])
        own = self.all.at[rows_at(self.base, self.slice)]
        for k in range(1, 32):
            self.push(own, own, self.g_send.at[k], self.g_recv.at[k], self.mate(k)[1])

    def close(self):
        for k in range(1, 32):
            source = lax.rem(self.q + 32 - k, 32)
            self.await_at(self.all.at[rows_at(source * self.slice, self.slice)], self.g_recv.at[k])
        super().close()


def back_kernel(
    gain, mask, down_shift, side_u, side_o, side_d,
    grad_stage_in, output_in, qkv_in, context_in, tokens_in, cotangent_in, down_expand_in, joined_reduce_in, normed_in,
    side_q_in, grad_in, middle_in, second_in, shard_in, joined_in, out_parts, probs_in,
    block_out, input_grad, shard_done, shard_rest, whole_done, whole_rest,
    grad_stage, output_full, qkv, context, tokens, cotangent, down_expand, joined_reduce, normed, side_q, grad, middle,
    second_normed, shard_early, joined_full, parts, probs, load_sem,
    rows, rows_send, rows_recv, key_grad, value_grad, joined_grad, result, block_own, whole_early, shard_late,
    whole_late, side_part, side_in, side_send, side_recv,
    part, sib_in, relay, near, s_send, s_recv, relay_out, near_out, t_send, t_recv, swap_send, swap_recv,
    *refs,
):
    p = Place()
    own_rows = rows_at(p.ring(0, True) * ROWS, ROWS)
    sources = (
        grad_stage_in, shard_in, second_in, cotangent_in, output_in, qkv_in, context_in, probs_in, out_parts, joined_in,
        side_q_in, normed_in, joined_reduce_in, middle_in, down_expand_in, grad_in, tokens_in,
    )
    targets = (
        grad_stage, shard_early, second_normed, cotangent, output_full, qkv, context, probs, parts, joined_full,
        side_q, normed, joined_reduce, middle, down_expand, grad, tokens,
    )
    loads = [pltpu.make_async_copy(src, dst, load_sem.at[i]) for i, (src, dst) in enumerate(zip(sources, targets))]
    stage = pltpu.make_async_copy(grad_stage_in, rows.at[own_rows], load_sem.at[17])
    stage.start()
    for copy in loads:
        copy.start()
    greet(p.ring_mates() + Reducer.mates(p))
    gather = Gather(p, rows, rows_send, rows_recv)
    stage.wait()
    gather.begin()
    swap = Swap(p, [(block_own, block_out), (result, input_grad)], swap_send, swap_recv)
    early_shard = ShardSum(p, shard_early, refs[0:7])
    early_whole = WholeSum(p, whole_early, refs[7:25])
    late_shard = ShardSum(p, shard_late, refs[25:32])
    late_whole = PlaneSum(p, whole_late, refs[32:46])
    for copy in loads[:4]:
        copy.wait()
    early_shard.open()

    def early_column(j):
        lanes = lanes_at(j * 256, 256)
        whole_early[lanes, :] = tn(second_normed[:, lanes], side_u[...]).astype(BF)
        whole_early[lanes_at(WIDTH + j * 256, 256), :] = (SCALE * tn(grad_stage[:, lanes], side_o[...])).astype(BF)
        whole_early[lanes_at(2 * WIDTH + j * 256, 256), :] = (SCALE * tn(cotangent[:, lanes], side_d[...])).astype(BF)

    loop(WIDTH // 256, early_column)
    early_whole.open()

    def back(dy):
        base = lax.rem(p.y + dy + 4, 4) * PAIR

        def body(index):
            at = rows_at(base + index * ROWS, ROWS)
            context_grad = nt(rows[at, :], output_full[...]).astype(BF)
            for head in range(2):
                start = head * 3 * HEAD
                query = qkv[at, start : start + HEAD]
                key = qkv[:, start + HEAD : start + 2 * HEAD]
                value = qkv[:, start + 2 * HEAD : start + 3 * HEAD]
                own = context_grad[:, head * HEAD : (head + 1) * HEAD]
                weights = probs[head, at, :]
                mean = jnp.sum(
                    own.astype(F32) * context[at, head * HEAD : (head + 1) * HEAD].astype(F32), axis=-1, keepdims=True
                )
                score_grad = weights * (nt(own, value) - mean).astype(BF)
                joined_grad[at, start : start + HEAD] = (nn(score_grad, key) * (1.0 / math.sqrt(HEAD))).astype(BF)
                value_grad[head] = value_grad[head] + tn(own, weights)
                key_grad[head] = key_grad[head] + tn(query, score_grad)

        loop(2, body)

    value_grad[...] = jnp.zeros_like(value_grad)
    key_grad[...] = jnp.zeros_like(key_grad)
    scatter_out = Scatter(p, parts, None, relay_out, near_out, t_send, t_recv, lambda dy: dy % 4 * ROWS)
    gather.own_pair()
    for copy in loads[4:8]:
        copy.wait()
    back(0)
    early_whole.halves()
    loads[8].wait()
    gather.near()
    scatter_out.relay_out()
    scatter_out.near_free(1)
    scatter_out.near_free(-1)
    gather.near_pairs()
    back(1)
    gather.far()
    early_shard.spread()
    back(-1)
    early_whole.slices()
    gather.far_pair()
    scatter_out.near_rest()
    back(2)
    turn = identity()
    for head in range(2):
        start = head * 3 * HEAD
        joined_grad[:, start + HEAD : start + 2 * HEAD] = tn(
            (key_grad[head] * (1.0 / math.sqrt(HEAD))).astype(BF), turn
        ).astype(BF)
        joined_grad[:, start + 2 * HEAD : start + 3 * HEAD] = tn(value_grad[head].astype(BF), turn).astype(BF)
    for copy in loads[9:]:
        copy.wait()

    def product(dy):
        at = pair_rows(p, dy)

        def body(j):
            lanes = lanes_at(j * 512, 512)
            part[at, lanes] = nt(joined_grad[at, :], joined_full[lanes, :]).astype(BF)

        loop(WIDTH // 512, body)

    scatter = Scatter(p, part, sib_in, relay, near, s_send, s_recv)
    product(2)
    scatter.exchange(2)
    side_part[...] = nt(joined_grad[...], joined_full[pl.ds(WIDTH, LANES), :]).astype(BF)
    side = SideSum(p, side_part, side_in, side_send, side_recv)
    side.open()
    early_whole.bits()
    scatter.combine(2)
    scatter.relay_out()
    product(1)
    scatter.exchange(1)
    mask_rows = mask[...].astype(F32)
    side_part[own_rows, :] = (mask_rows * side.total()).astype(BF)

    def late_column(j):
        lanes = lanes_at(j * 256, 256)
        whole_late[lanes, :] = tn(normed[:, lanes], side_part[own_rows, :]).astype(BF)

    loop(WIDTH // 256, late_column)
    late_whole.open()
    product(-1)
    scatter.exchange(-1)
    scatter.combine(1)
    scatter.near_free(1)
    product(0)
    scatter.exchange(0)
    scatter.combine(-1)
    scatter.near_free(-1)
    scatter.near_rest()
    scatter.combine(0)
    shard_late[pl.ds(0, CTX), :] = tn(context[...], rows[:, pl.ds(WIDTH, LANES)]).astype(BF)

    def late_lane(j):
        lanes = lanes_at(j * 256, 256)
        shard_late[lanes_at(CTX + j * 256, 256), :] = (SCALE * tn(joined_grad[:, lanes], side_q[...])).astype(BF)

    loop(QKV // 256, late_lane)
    late_shard.open()
    scatter_out.arrived()

    def add_tile(j):
        lanes = lanes_at(j * 256, 256)
        block_own[:, lanes] = (
            middle[:, lanes]
            + scatter_out.total(0, ROWS, lanes)
            + down_shift[:, lanes]
            + SCALE * nn(side_d[...], down_expand[:, lanes])
        ).astype(BF)

    loop(WIDTH // 256, add_tile)
    swap.begin(0)
    late_whole.slices()
    early_whole.slices_back()
    late_shard.spread()
    late_whole.bits()
    late_whole.slices_back()
    scatter.arrived()

    def norm_block(index):
        at = rows_at(index * BLOCK, BLOCK)
        side_rows = side_part[rows_at(p.ring(0, True) * ROWS + index * BLOCK, BLOCK), :]
        back_grad = scatter.total(index * BLOCK, BLOCK, pl.ds(0, WIDTH)) + nt(side_rows, joined_reduce[...])
        result[at, :] = (grad[at, :] + norm_back(tokens[at, :].astype(F32), gain[...], back_grad)).astype(BF)

    loop(ROWS // BLOCK, norm_block)
    swap.begin(1)
    early_whole.halves_back()
    early_shard.close()
    late_shard.close()
    early_whole.close()
    late_whole.close()
    shard_done[...] = early_shard.all[...]
    shard_rest[...] = late_shard.all[...]
    whole_done[...] = early_whole.all[...]
    whole_rest[...] = late_whole.all[...]
    gather.end()
    scatter.end()
    scatter_out.end(4)
    side.end()
    swap.arrived(0)
    swap.arrived(1)
    swap.end()


def back_call(ins):
    outs = [
        shape(ROWS, WIDTH), shape(ROWS, WIDTH), shape(2 * UNITS, LANES), shape(CTX + QKV, LANES),
        shape(3 * WIDTH, LANES), shape(WIDTH, LANES),
    ]
    dma = pltpu.SemaphoreType.DMA
    vmem = pltpu.VMEM
    return call(
        back_kernel,
        3,
        ins,
        [IN_VMEM] * 6 + [ANYWHERE] * 17,
        outs,
        [ANYWHERE] * 2 + [IN_VMEM] * 4,
        [
            vmem((ROWS, WIDE), BF), vmem((CTX, WIDE), BF), vmem((GROUP, QKV), BF), vmem((GROUP, CTX), BF),
            vmem((ROWS, WIDTH), BF), vmem((ROWS, WIDTH), BF), vmem((LANES, WIDTH), BF), vmem((WIDTH, LANES), BF),
            vmem((ROWS, WIDTH), BF), vmem((GROUP, LANES), BF), vmem((ROWS, WIDTH), F32), vmem((ROWS, WIDTH), F32),
            vmem((ROWS, WIDE), BF), vmem((2 * UNITS, LANES), BF), vmem((WIDE, QKV), BF), vmem((4 * ROWS, WIDTH), BF),
            vmem((2, GROUP, GROUP), BF), dma((18,)),
            *gather_scratch(), vmem((2, HEAD, GROUP), F32), vmem((2, HEAD, GROUP), F32), vmem((GROUP, QKV), BF),
            vmem((ROWS, WIDTH), BF), vmem((ROWS, WIDTH), BF), vmem((3 * WIDTH, LANES), BF),
            vmem((CTX + QKV, LANES), BF), vmem((WIDTH, LANES), BF), *side_scratch(), *scatter_scratch(WIDTH),
            *scatter_scratch(WIDTH)[2:], *swap_marks(2), *ShardSum.scratch(2 * UNITS), *WholeSum.scratch(3 * WIDTH),
            *ShardSum.scratch(CTX + QKV), *PlaneSum.scratch(WIDTH),
        ],
    )


def finish_kernel(
    shard_early_in, whole_early_in, shard_late_in, whole_late_in, block_from, grad_from,
    block_out, input_grad, qkv_a, qkv_b, out_a, out_b, up_a, up_b, down_a, down_b,
    shard_early, whole_early, shard_late, whole_late, block_in, grad_in, load_sem,
    block_here, grad_here, a_here, b_here, out_sem,
):
    loads = []
    for src, dst in (
        (block_from, block_in), (grad_from, grad_in), (whole_early_in, whole_early), (whole_late_in, whole_late),
        (shard_early_in, shard_early), (shard_late_in, shard_late),
    ):
        loads.append(pltpu.make_async_copy(src, dst, load_sem.at[len(loads)]))
        loads[-1].start()
    turn = identity()
    copies = []

    def send(src, dst):
        copy = pltpu.make_async_copy(src, dst, out_sem.at[len(copies)])
        copy.start()
        copies.append(copy)

    def turned(source, start, base, count):
        def body(j):
            b_here[:, lanes_at(base + j * 256, 256)] = nt(turn, source[lanes_at(start + j * 256, 256), :])

        loop(count // 256, body)

    def widened(source, start, here, base, count, step):
        def body(index):
            here[rows_at(base + index * step, step), :] = source[rows_at(start + index * step, step), :].astype(F32)

        loop(count // step, body)

    loads[0].wait()
    widened(block_in, 0, block_here, 0, ROWS, BLOCK)
    send(block_here, block_out)
    loads[1].wait()
    widened(grad_in, 0, grad_here, 0, ROWS, BLOCK)
    send(grad_here, input_grad)
    for load in loads[2:]:
        load.wait()
    base = 0
    for source, start, out, count in (
        (whole_early, 0, up_a, WIDTH),
        (whole_late, 0, qkv_a, WIDTH),
        (shard_early, 0, down_a, UNITS),
        (shard_late, 0, out_a, CTX),
    ):
        widened(source, start, a_here, base, count, 256)
        send(a_here.at[pl.ds(base, count)], out.at[0])
        base += count
    base = 0
    for source, start, out, count in (
        (whole_early, WIDTH, out_b, WIDTH),
        (whole_early, 2 * WIDTH, down_b, WIDTH),
        (shard_early, UNITS, up_b, UNITS),
        (shard_late, CTX, qkv_b, QKV),
    ):
        turned(source, start, base, count)
        send(b_here.at[:, pl.ds(base, count)], out.at[0])
        base += count
    for copy in copies:
        copy.wait()


def finish_call(ins):
    return pl.pallas_call(
        finish_kernel,
        name="finish_kernel",
        out_shape=[
            shape(ROWS, WIDTH, kind=F32), shape(ROWS, WIDTH, kind=F32), shape(1, WIDTH, LANES, kind=F32),
            shape(1, LANES, QKV, kind=F32), shape(1, CTX, LANES, kind=F32), shape(1, LANES, WIDTH, kind=F32),
            shape(1, WIDTH, LANES, kind=F32), shape(1, LANES, UNITS, kind=F32), shape(1, UNITS, LANES, kind=F32),
            shape(1, LANES, WIDTH, kind=F32),
        ],
        in_specs=[ANYWHERE] * 6,
        out_specs=[ANYWHERE] * 10,
        scratch_shapes=[
            pltpu.VMEM((2 * UNITS, LANES), BF), pltpu.VMEM((3 * WIDTH, LANES), BF), pltpu.VMEM((CTX + QKV, LANES), BF),
            pltpu.VMEM((WIDTH, LANES), BF), pltpu.VMEM((ROWS, WIDTH), BF), pltpu.VMEM((ROWS, WIDTH), BF),
            pltpu.SemaphoreType.DMA((6,)), pltpu.VMEM((ROWS, WIDTH), F32), pltpu.VMEM((ROWS, WIDTH), F32),
            pltpu.VMEM((2 * WIDTH + UNITS + CTX, LANES), F32), pltpu.VMEM((LANES, 2 * WIDTH + UNITS + QKV), F32),
            pltpu.SemaphoreType.DMA((10,)),
        ],
        compiler_params=pltpu.CompilerParams(vmem_limit_bytes=VMEM_LIMIT),
    )(*ins)


def shards(
    tokens, lengths, order, sequence_adapter, first_norm_gain, first_norm_bias, second_norm_gain, second_norm_bias,
    joined_matrix, joined_offset_bias, output_matrix, output_offset_bias, up_matrix, up_offset_bias, down_matrix,
    down_offset_bias, joined_adapter_reduce, joined_adapter_expand, output_adapter_reduce, output_adapter_expand,
    up_adapter_reduce, up_adapter_expand, down_adapter_reduce, down_adapter_expand, cotangent,
):
    (
        normed, middle, side_o, context, qkv, mask_own, probs, side_q, normed_first, gathered_grad, cot_own,
        joined_full, output_full, up_full, down_full, tokens_own, up_shift_own,
    ) = forward_call(
        (
            first_norm_gain, first_norm_bias, joined_adapter_reduce[0], down_adapter_expand[0],
            joined_adapter_expand[0], joined_offset_bias, order, output_adapter_expand[0], output_offset_bias,
            second_norm_gain, second_norm_bias, up_adapter_reduce[0], lengths, sequence_adapter,
            tokens, cotangent, up_offset_bias, joined_matrix[0], output_matrix[0], output_adapter_reduce[0],
            up_matrix[0], up_adapter_expand[0], down_matrix[0], down_adapter_reduce[0],
        )
    )
    grad, grad_stage, side_u, side_d, shard_feed, out_parts = feed_call(
        (
            normed, middle, up_shift_own, mask_own, second_norm_gain, up_adapter_reduce[0],
            output_adapter_expand[0], gathered_grad, up_full, down_full,
        )
    )
    block_own, input_own, shard_early, shard_late, whole_early, whole_late = back_call(
        (
            first_norm_gain, mask_own, down_offset_bias, side_u, side_o, side_d, grad_stage, output_full, qkv, context,
            tokens_own, cot_own, down_adapter_expand[0], joined_adapter_reduce[0], normed_first, side_q, grad, middle,
            normed, shard_feed, joined_full, out_parts, probs,
        )
    )
    return tuple(finish_call((shard_early, whole_early, shard_late, whole_late, block_own, input_own)))


def solution(mesh):
    spread = P(("dp", "tensor"), None)
    by_dp = P("dp", None)
    rows = P(None, "dp", "tensor")
    cols = P(None, "tensor", "dp")
    last = P(None, None, "tensor")
    middle = P(None, "tensor", None)
    vector = P(None, "tensor")
    return jax.shard_map(
        shards,
        mesh=mesh,
        in_specs=(
            spread, by_dp, by_dp, by_dp, P(), P(), P(), P(), rows, vector, cols, P(), rows, vector, cols, P(),
            P(), last, middle, P(), P(), last, middle, P(), spread,
        ),
        out_specs=(spread, spread, P(), last, middle, P(), P(), last, middle, P()),
        check_vma=False,
    )
```
